128 devices in a mesh: pipe: 2 (over core), expert: 32 (over y, x, z_hi), tensor: 2 (over z_lo).
Axes of the slice: x: 4, y: 4, z: 4 (z_hi: 2, z_lo: 2; z = z_hi * 2 + z_lo), core: 2. Of those that a mesh axis runs over, the one named last changes fastest.
Arguments:
- tokens: bfloat16 [2, 4096, 1536], P(None, 'expert'), may hold values from -6 to 6
- cotangent: float32 [2, 4096, 1536], P(None, 'expert'), may hold values from -6 to 6
- routes: int32 [2, 2, 4096, 4], P('pipe', None, 'expert'), may hold values from 0 to 31, all different within a row; in each aligned block of 128 rows (0 to 127, 128 to 255, ..., all dimensions but the last counted through in order) at most 32 rows name the same one
- attn_gain: bfloat16 [2, 1536], P('pipe'), may hold values from 0.5 to 1.5
- w_query: bfloat16 [2, 1536, 1536], P('pipe', None, 'tensor'), may hold values from -0.15625 to 0.15625
- key_weight: bfloat16 [2, 1536, 256], P('pipe', None, 'tensor'), may hold values from -0.15625 to 0.15625
- value_weight: bfloat16 [2, 1536, 256], P('pipe', None, 'tensor'), may hold values from -0.15625 to 0.15625
- w_out: bfloat16 [2, 1536, 1536], P('pipe', 'tensor'), may hold values from -0.875 to 0.875
- moe_gain: bfloat16 [2, 1536], P('pipe'), may hold values from 0.5 to 1.5
- w_router: bfloat16 [2, 1536, 32], P('pipe'), may hold values from -0.076660156 to 0.076660156
- w_gate: bfloat16 [2, 32, 1536, 768], P('pipe', 'expert', None, 'tensor'), may hold values from -0.15625 to 0.15625
- w_up: bfloat16 [2, 32, 1536, 768], P('pipe', 'expert', None, 'tensor'), may hold values from -0.15625 to 0.15625
- w_down: bfloat16 [2, 32, 768, 1536], P('pipe', 'expert', 'tensor'), may hold values from -0.625 to 0.625
Outputs:
- layer_out: float32 [2, 2, 4096, 1536], P('pipe', None, 'expert')
- input_grads: float32 [2, 2, 4096, 1536], P('pipe', None, 'expert')
- grad_attn_gain: float32 [2, 1536], P('pipe')
- grad_query: float32 [2, 1536, 1536], P('pipe', None, 'tensor')
- grad_key: float32 [2, 1536, 256], P('pipe', None, 'tensor')
- grad_value: float32 [2, 1536, 256], P('pipe', None, 'tensor')
- grad_out: float32 [2, 1536, 1536], P('pipe', 'tensor')
- grad_moe_gain: float32 [2, 1536], P('pipe')
- grad_router: float32 [2, 1536, 32], P('pipe')
- grad_gate: float32 [2, 32, 1536, 768], P('pipe', 'expert', None, 'tensor')
- grad_up: float32 [2, 32, 1536, 768], P('pipe', 'expert', None, 'tensor')
- grad_down: float32 [2, 32, 768, 1536], P('pipe', 'expert', 'tensor')
The draws below stay inside these ranges and needn't reach their ends.
Inputs may be any that keep to these rules, and one draw needn't show every extreme that they name: `routes`: each row names 4 different experts; among the 128 rows of one device in one layer and micro-batch (aligned blocks) no expert is named more than 32 times, and in some blocks one is named exactly 32 times.
All inputs are finite; a program needn't handle non-finite values.
Results may differ from the reference program's by a relative error of at most 0.025.
Values may be sent and summed in bfloat16 or wider, within the bound.
No kernel may reach another device: no remote copies, remote signals or barrier semaphores. Data moves between devices by JAX's collectives and lax.ppermute only.
A program may use at most 256 MiB of HBM per device.

```python
import math
import jax
import jax.numpy as jnp
import numpy as np
from jax import lax

MODEL_DIMENSION = 1536
QUERY_HEADS = 12
KEY_VALUE_HEADS = 2
HEAD_DIMENSION = 128
FF = 768
TOPK = 4
SEQ_LEN = 128
MB = 2
EXPERTS = 32
LAYER_COUNT = 2
TOKENS = 4096
CAP = 32


def level_of(key, shape, cuts, smallest, top_value):
    def one(position, blocks):
        steps = jax.random.uniform(jax.random.fold_in(jax.random.fold_in(key, 6), position), (blocks,), jnp.float32, smallest / len(cuts), top_value / len(cuts))
        return jnp.repeat(jnp.exp(steps), shape[position] // blocks).reshape((-1,) + (1,) * (len(shape) - position - 1))

    loudness = one(*cuts[0])
    for cut in cuts[1:]:
        loudness = loudness * one(*cut)
    return loudness


def shared_out(rng, own, number, rows, count, top, reach, skew):
    ranking = jax.random.permutation(rng, count)
    packed, usual = load_shares(count, rows * top, reach, skew, True), load_shares(count, rows * top, reach, skew, False)
    places = jnp.arange(count)

    def named(tallies, turn):
        used = int((tallies > 0).sum())
        fixed = max(1, used // 4)
        passed = fixed + (places - fixed + turn * (used - fixed)) % max(1, count - fixed)
        return jnp.zeros((count,), jnp.int32).at[ranking[jnp.where(places < fixed, places, passed)]].set(jnp.asarray(tallies, jnp.int32))

    tallies = jnp.where(number % 4 == 0, named(packed, number // 4), named(usual, number - number // 4 - 1))
    mixed = jax.random.permutation(jax.random.fold_in(own, 3), count)
    giver, receiver = mixed[0:count // 2 * 2:2], mixed[1:count // 2 * 2:2]
    room = jnp.minimum(tallies[giver] - 1, reach - tallies[receiver]) // 2
    room = jnp.where((giver == ranking[0]) | (receiver == ranking[0]) | (tallies[receiver] == 0), 0, jnp.maximum(room, 0))
    passed = jax.random.randint(jax.random.fold_in(own, 4), (count // 2,), 0, 1 << 20) % (room + 1)
    tallies = tallies.at[giver].add(-passed).at[receiver].add(passed)
    members = jnp.searchsorted(jnp.cumsum(tallies), jnp.arange(rows * top), side="right").astype(jnp.int32)
    listing = members.reshape(top, rows).T
    listing = listing[jax.random.permutation(jax.random.fold_in(own, 1), rows)]
    turn = jax.random.randint(jax.random.fold_in(own, 2), (rows, 1), 0, top)
    return jnp.take_along_axis(listing, (jnp.arange(top)[None, :] + turn) % top, axis=1)


def load_shares(amount, total, limit, slope, full):
    loads = [(1 << 20) // math.isqrt(grade ** slope) + 1 for grade in range(1, amount + 1)]
    largest = limit if full else min(limit, max(-(-total // amount), total * loads[0] // sum(loads)))
    least = 1 if total - largest >= amount - 1 else 0
    given, surplus = [largest] + [least] * (amount - 1), total - largest - least * (amount - 1)
    while surplus > 0:
        candidates = [i for i in range(1, amount) if given[i] < largest] or [i for i in range(1, amount) if given[i] < limit]
        whole, left = sum([loads[i] for i in candidates]), surplus
        for i in candidates:
            addition = min(limit - given[i], max(1, left * loads[i] // whole), surplus)
            given[i] = given[i] + addition
            surplus = surplus - addition
    return np.array(given)


def gaussian(rng, dims, scale, most, cuts=(), held_as=jnp.bfloat16):
    entries = jax.random.normal(rng, dims, jnp.float32) * scale
    if len(cuts) > 0:
        entries = level_of(rng, dims, cuts, -0.22, 0.18) * entries
    return jnp.clip(entries, min=-most, max=most).astype(held_as)


def setup_inputs(seed: int = 0) -> dict:
    streams_of = jax.random.split(jax.random.key(seed), 14)
    tokens = gaussian(streams_of[0], (MB, TOKENS, MODEL_DIMENSION), 1.0, 6.0, ((1, 32),))
    cotangent = gaussian(streams_of[1], (MB, TOKENS, MODEL_DIMENSION), 1.0, 6.0, ((1, 32),), jnp.float32)
    routes_keys = jax.random.split(jax.random.fold_in(streams_of[2], 1), LAYER_COUNT * MB * TOKENS // SEQ_LEN)
    routes_turns = jax.random.permutation(jax.random.fold_in(streams_of[2], 3), LAYER_COUNT * MB * TOKENS // SEQ_LEN)
    routes = jax.vmap(lambda own, number: shared_out(jax.random.fold_in(streams_of[2], 2), own, number, SEQ_LEN, EXPERTS, TOPK, CAP, 2))(routes_keys, routes_turns).reshape((LAYER_COUNT, MB, TOKENS, TOPK))
    attn_gain = jnp.clip(1.0 + 0.1 * jax.random.normal(streams_of[3], (LAYER_COUNT, MODEL_DIMENSION), jnp.float32), 0.5, 1.5).astype(jnp.bfloat16)
    w_query = gaussian(streams_of[4], (LAYER_COUNT, MODEL_DIMENSION, QUERY_HEADS * HEAD_DIMENSION), MODEL_DIMENSION ** -0.5, 0.15625, ((0, 2), (2, 2)))
    key_weight = gaussian(streams_of[5], (LAYER_COUNT, MODEL_DIMENSION, KEY_VALUE_HEADS * HEAD_DIMENSION), MODEL_DIMENSION ** -0.5, 0.15625, ((0, 2), (2, 2)))
    value_weight = gaussian(streams_of[6], (LAYER_COUNT, MODEL_DIMENSION, KEY_VALUE_HEADS * HEAD_DIMENSION), MODEL_DIMENSION ** -0.5, 0.15625, ((0, 2), (2, 2)))
    w_out = gaussian(streams_of[7], (LAYER_COUNT, QUERY_HEADS * HEAD_DIMENSION, MODEL_DIMENSION), (QUERY_HEADS * HEAD_DIMENSION // 32) ** -0.5, 0.875, ((0, 2), (1, 2)))
    moe_gain = jnp.clip(1.0 + 0.1 * jax.random.normal(streams_of[8], (LAYER_COUNT, MODEL_DIMENSION), jnp.float32), 0.5, 1.5).astype(jnp.bfloat16)
    w_router = gaussian(streams_of[9], (LAYER_COUNT, MODEL_DIMENSION, EXPERTS), 0.0128, 0.076660156, ((0, 2),))
    w_gate = gaussian(streams_of[10], (LAYER_COUNT, EXPERTS, MODEL_DIMENSION, FF), MODEL_DIMENSION ** -0.5, 0.15625, ((0, 2), (1, 32), (3, 2)))
    w_up = gaussian(streams_of[11], (LAYER_COUNT, EXPERTS, MODEL_DIMENSION, FF), MODEL_DIMENSION ** -0.5, 0.15625, ((0, 2), (1, 32), (3, 2)))
    w_down = gaussian(streams_of[12], (LAYER_COUNT, EXPERTS, FF, MODEL_DIMENSION), (FF // 8) ** -0.5, 0.625, ((0, 2), (1, 32), (2, 2)))
    return dict(tokens=tokens, cotangent=cotangent, routes=routes, attn_gain=attn_gain, w_query=w_query, key_weight=key_weight, value_weight=value_weight, w_out=w_out, moe_gain=moe_gain, w_router=w_router, w_gate=w_gate, w_up=w_up, w_down=w_down)


NORM_EPS = 1e-06
ROPE_BASE = 10000.0
EXACT = lax.Precision.HIGHEST

@jax.custom_vjp
def low(v):
    return lax.optimization_barrier(v.astype(jnp.bfloat16)).astype(jnp.float32)

@jax.custom_vjp
def low_back(v):
    return v

def low_keep(v):
    return (low(v), None)

def low_pass(kept, grad):
    return (grad,)

def back_keep(v):
    return (v, None)

def back_low(kept, grad):
    return (low(grad),)
low.defvjp(low_keep, low_pass)
low_back.defvjp(back_keep, back_low)

def rotary_tables(sequence_length):
    half_size = HEAD_DIMENSION // 2
    frequency = ROPE_BASE ** (-(jnp.arange(half_size, dtype=jnp.float32) * 2.0) / HEAD_DIMENSION)
    angles = jnp.arange(sequence_length, dtype=jnp.float32)[:, None] * frequency[None, :]
    cosine = jnp.concatenate([jnp.cos(angles), jnp.cos(angles)], axis=1)
    sine_table = jnp.concatenate([jnp.sin(angles), jnp.sin(angles)], axis=1)
    return (cosine, sine_table)

def rotate_half(vector):
    half_size = vector.shape[-1] // 2
    return jnp.concatenate([-vector[..., half_size:], vector[..., :half_size]], axis=-1)

def rotary_turn(vector, cosine, sine_table):
    return vector * cosine + rotate_half(vector) * sine_table

def norm_rows(vector, gain_vec):
    return vector * lax.rsqrt(lax.optimization_barrier(jnp.mean(vector * vector, axis=-1, keepdims=True)) + NORM_EPS) * gain_vec

def slot_places(route_ids):
    full_shape = route_ids.shape
    flat_route = route_ids.reshape(full_shape[:-2] + (full_shape[-2] * full_shape[-1],))
    onehot = (flat_route[..., None] == jnp.arange(EXPERTS, dtype=jnp.int32)).astype(jnp.int32)
    before = jnp.cumsum(onehot, axis=-2) - onehot
    return lax.optimization_barrier(jnp.sum(before * onehot, axis=-1)).reshape(full_shape).astype(jnp.int32)

def layer(section_input, route_ids, params):
    gain_a, wq, wk, wv, wo, gain_m, wr, wg, wu, wd = params
    micro_batch_count, sequence_total, sequence_length, model_width = section_input.shape
    query_group_size = QUERY_HEADS // KEY_VALUE_HEADS
    cosine, sine_table = rotary_tables(sequence_length)
    normed = low(norm_rows(section_input, gain_a))
    projected_queries = low_back(jnp.einsum('mnsd,de->mnse', normed, wq, precision=EXACT))
    projected_queries = projected_queries.reshape(micro_batch_count, sequence_total, sequence_length, KEY_VALUE_HEADS, query_group_size, HEAD_DIMENSION)
    projected_queries = low(rotary_turn(projected_queries, cosine[:, None, None, :], sine_table[:, None, None, :]) * HEAD_DIMENSION ** (-0.5))
    projected_keys = low_back(jnp.einsum('mnsd,de->mnse', normed, wk, precision=EXACT))
    projected_keys = projected_keys.reshape(micro_batch_count, sequence_total, sequence_length, KEY_VALUE_HEADS, HEAD_DIMENSION)
    projected_keys = low(rotary_turn(projected_keys, cosine[:, None, :], sine_table[:, None, :]))
    projected_values = low(low_back(jnp.einsum('mnsd,de->mnse', normed, wv, precision=EXACT)))
    projected_values = projected_values.reshape(micro_batch_count, sequence_total, sequence_length, KEY_VALUE_HEADS, HEAD_DIMENSION)
    scores = low_back(jnp.einsum('mnsghd,mntgd->mnghst', projected_queries, projected_keys, precision=EXACT))
    causal = jnp.arange(sequence_length)[:, None] >= jnp.arange(sequence_length)[None, :]
    scores = jnp.where(causal, scores, -1e+30)
    weights = low(jax.nn.softmax(scores, axis=-1))
    attended = jnp.einsum('mnghst,mntgd->mnsghd', weights, projected_values, precision=EXACT)
    attended = low(low_back(attended.reshape(micro_batch_count, sequence_total, sequence_length, QUERY_HEADS * HEAD_DIMENSION)))
    hidden = section_input + low_back(jnp.einsum('mnse,ed->mnsd', attended, wo, precision=EXACT))
    moe_in = low(norm_rows(hidden, gain_m))
    logits = jnp.einsum('mnsd,de->mnse', moe_in, wr, precision=EXACT)
    chosen = jnp.take_along_axis(logits, route_ids, axis=-1)
    gate_share = jax.nn.softmax(chosen, axis=-1)
    slot_place = slot_places(route_ids)
    block_id = (jnp.arange(micro_batch_count, dtype=jnp.int32)[:, None] * sequence_total + jnp.arange(sequence_total, dtype=jnp.int32)[None, :]).astype(jnp.int32)
    slot_row = (block_id[:, :, None, None] * CAP + slot_place).astype(jnp.int32)
    spread = jnp.broadcast_to(moe_in[:, :, :, None, :], route_ids.shape + (model_width,))
    buffer = jnp.zeros((EXPERTS, micro_batch_count * sequence_total * CAP, model_width), jnp.float32)
    buffer = low_back(buffer.at[route_ids, slot_row].set(spread))

    def expert(expert_item):
        expert_rows, w_g, w_u, w_d = expert_item
        gate_v = low_back(jnp.dot(expert_rows, w_g, precision=EXACT))
        up_v = low_back(jnp.dot(expert_rows, w_u, precision=EXACT))
        hidden_act = low(jax.nn.silu(gate_v) * up_v)
        return jnp.dot(hidden_act, w_d, precision=EXACT)
    outputs = lax.map(jax.checkpoint(expert), (buffer, wg, wu, wd))
    outputs = low(low_back(outputs))
    gathered = outputs[route_ids, slot_row]
    return hidden + lax.optimization_barrier(jnp.sum(gate_share[..., None] * gathered, axis=-2))

def reference(tokens, cotangent, routes, attn_gain, w_query, key_weight, value_weight, w_out, moe_gain, w_router, w_gate, w_up, w_down):
    sequence_total = TOKENS // SEQ_LEN
    full_shape = (MB, sequence_total, SEQ_LEN, MODEL_DIMENSION)
    section_input = tokens.astype(jnp.float32).reshape(full_shape)
    route_ids = routes.reshape(LAYER_COUNT, MB, sequence_total, SEQ_LEN, TOPK)
    params = tuple((w.astype(jnp.float32) for w in (attn_gain, w_query, key_weight, value_weight, w_out, moe_gain, w_router, w_gate, w_up, w_down)))

    def whole(first_in, shift_in, weight_set):
        first_out = layer(first_in, route_ids[0], tuple((w[0] for w in weight_set)))
        middle = low(low_back(first_out)) + shift_in
        last_out = layer(middle, route_ids[1], tuple((w[1] for w in weight_set)))
        return (last_out, first_out)
    last_out, pull_back, first_out = jax.vjp(whole, section_input, jnp.zeros(full_shape, jnp.float32), params, has_aux=True)
    grad_first, grad_middle, grad_params = pull_back(cotangent.astype(jnp.float32).reshape(full_shape))
    layer_out = jnp.stack([first_out, last_out]).reshape(LAYER_COUNT, MB, TOKENS, MODEL_DIMENSION)
    input_grads = jnp.stack([grad_first, grad_middle]).reshape(LAYER_COUNT, MB, TOKENS, MODEL_DIMENSION)
    return (layer_out, input_grads, grad_params[0], grad_params[1], grad_params[2], grad_params[3], grad_params[4], grad_params[5], grad_params[6], grad_params[7], grad_params[8], grad_params[9])
```

```python
import jax
import jax.numpy as jnp
from jax import lax
from jax.sharding import PartitionSpec as P

HEAD = 128
NORM_EPS = 1e-06
ROPE_BASE = 10000.0
BF16 = jnp.bfloat16
F32 = jnp.float32
SWAP = [(0, 1), (1, 0)]


def swap(value, axis):
    return lax.ppermute(value, axis, SWAP)


def expert_exchange(value):
    return lax.all_to_all(value, "expert", split_axis=0, concat_axis=0, tiled=True)


def mul(left, right, dims):
    return lax.dot_general(left, right, (dims, ((), ())), preferred_element_type=F32)


def mul_nn(left, right):
    return mul(left, right, ((1,), (0,)))


def mul_nt(left, right):
    return mul(left, right, ((1,), (1,)))


def mul_tn(left, right):
    return mul(left, right, ((0,), (0,)))


def rotary_tables(count):
    half = HEAD // 2
    frequency = ROPE_BASE ** (-(jnp.arange(half, dtype=F32) * 2.0) / HEAD)
    angles = jnp.arange(count, dtype=F32)[:, None] * frequency[None, :]
    cosine = jnp.concatenate([jnp.cos(angles), jnp.cos(angles)], axis=1)
    sine = jnp.concatenate([jnp.sin(angles), jnp.sin(angles)], axis=1)
    return cosine, sine


def turn(vector, cosine, sine):
    half = HEAD // 2
    moved = jnp.concatenate([-vector[..., half:], vector[..., :half]], axis=-1)
    return vector * cosine + moved * sine


def turn_back(grad, cosine, sine):
    half = HEAD // 2
    moved = grad * sine
    return grad * cosine + jnp.concatenate([moved[..., half:], -moved[..., :half]], axis=-1)


def row_scale_of(rows):
    return lax.rsqrt(jnp.mean(rows * rows, axis=-1, keepdims=True) + NORM_EPS)


def norm_back(rows, scale, gain, grad):
    scaled = grad * gain
    grad_gain = jnp.sum(grad * rows * scale, axis=0)
    grad_rows = scale * scaled - rows * scale**3 * jnp.mean(scaled * rows, axis=-1, keepdims=True)
    return grad_rows, grad_gain


def causal(count):
    return jnp.arange(count)[:, None] >= jnp.arange(count)[None, :]


def attend_forward(x, gain, wq, wk, wv, wo, cosine, sine):
    scale = row_scale_of(x)
    normed = (x * scale * gain).astype(BF16)
    count, heads = x.shape[0], wq.shape[1] // HEAD
    q = mul_nn(normed, wq).reshape(count, heads, HEAD)
    q = (turn(q, cosine[:, None], sine[:, None]) * HEAD**-0.5).astype(BF16)
    k = turn(mul_nn(normed, wk), cosine, sine).astype(BF16)
    v = mul_nn(normed, wv).astype(BF16)
    scores = jnp.einsum("shd,td->hst", q, k, preferred_element_type=F32)
    scores = jnp.where(causal(count), scores, -1e30)
    raised = jnp.exp(scores - jnp.max(scores, axis=-1, keepdims=True))
    weights = raised / jnp.sum(raised, axis=-1, keepdims=True)
    o = jnp.einsum("hst,td->shd", weights.astype(BF16), v, preferred_element_type=F32)
    o = o.reshape(count, heads * HEAD).astype(BF16)
    return mul_nn(o, wo).astype(BF16), (scale, normed, q, k, v, weights, o)


def attend_backward(dz, saved, wq, wk, wv, wo, cosine, sine):
    scale, normed, q, k, v, weights, o = saved
    count, heads = q.shape[0], q.shape[1]
    grad_out = mul_tn(o, dz)
    do = mul_nt(dz, wo).astype(BF16).reshape(count, heads, HEAD)
    dp = jnp.einsum("shd,td->hst", do, v, preferred_element_type=F32)
    ds = (weights * (dp - jnp.sum(weights * dp, axis=-1, keepdims=True))).astype(BF16)
    dv = jnp.einsum("hst,shd->td", weights.astype(BF16), do, preferred_element_type=F32).astype(BF16)
    dq = jnp.einsum("hst,td->shd", ds, k, preferred_element_type=F32)
    dq = (turn_back(dq, cosine[:, None], sine[:, None]) * HEAD**-0.5).astype(BF16)
    dq = dq.reshape(count, heads * HEAD)
    dk = jnp.einsum("hst,shd->td", ds, q, preferred_element_type=F32)
    dk = turn_back(dk, cosine, sine).astype(BF16)
    da = mul_nt(dq, wq) + mul_nt(dk, wk) + mul_nt(dv, wv)
    grads = (mul_tn(normed, dq), mul_tn(normed, dk), mul_tn(normed, dv), grad_out)
    return da.astype(BF16), grads


def slot_table(routes, experts, lanes, part):
    count = routes.shape[0]
    names = jnp.arange(experts, dtype=jnp.int32)
    hot = jnp.any(routes.T[:, None, :] == names[None, :, None], axis=0)
    before = (jnp.arange(count)[:, None] < jnp.arange(count)[None, :]).astype(BF16)
    rank = mul_nn(hot.astype(BF16), before).astype(jnp.int32)
    lane = jnp.arange(lanes, dtype=jnp.int32) + part * lanes
    chosen = hot[:, None, :] & (rank[:, None, :] == lane[None, :, None])
    return hot, chosen.reshape(experts * lanes, count).astype(BF16)


def gates_of(normed, w_router, hot):
    logits = mul(w_router, normed, ((0,), (1,)))
    logits = jnp.where(hot, logits, -1e30)
    raised = jnp.where(hot, jnp.exp(logits - jnp.max(logits, axis=0, keepdims=True)), 0.0)
    return raised / jnp.sum(raised, axis=0, keepdims=True)


def gated_table(table, gates):
    experts, count = gates.shape
    return (table.reshape(experts, -1, count) * gates[:, None, :].astype(BF16)).reshape(-1, count)


def spread(table, rows, experts):
    sent = mul_nn(table, rows).astype(BF16)
    return expert_exchange(sent.reshape(experts, -1, rows.shape[1])).reshape(-1, rows.shape[1])


def send_back(rows, experts):
    return expert_exchange(rows.reshape(experts, -1, rows.shape[1])).reshape(-1, rows.shape[1])


def experts_forward(rows, weights):
    total = 0.0
    for w_gate, w_up, w_down in weights:
        gate, up = mul_nn(rows, w_gate), mul_nn(rows, w_up)
        total = total + mul_nn((jax.nn.silu(gate) * up).astype(BF16), w_down)
    return total.astype(BF16)


def experts_backward(rows, grads, weights):
    total, out = 0.0, []
    for w_gate, w_up, w_down in weights:
        gate, up = mul_nn(rows, w_gate), mul_nn(rows, w_up)
        sig = jax.nn.sigmoid(gate)
        act = gate * sig
        hidden = (act * up).astype(BF16)
        grad_hidden = mul_nt(grads, w_down)
        grad_gate = (grad_hidden * up * sig * (1.0 + gate * (1.0 - sig))).astype(BF16)
        grad_up = (grad_hidden * act).astype(BF16)
        total = total + mul_nt(grad_gate, w_gate) + mul_nt(grad_up, w_up)
        out.append((mul_tn(rows, grad_gate), mul_tn(rows, grad_up), mul_tn(hidden, grads)))
    return total.astype(BF16), out


def place(index):
    return index // 8, (index // 2) % 4, index % 2


def index_of(y, x, z):
    return (y * 4 + x) * 2 + z


def partners(axis, flip):
    pairs = []
    for source in range(32):
        y, x, z = place(source)
        target = index_of(y ^ flip, x, z) if axis == "y" else index_of(y, x ^ flip, z)
        pairs.append((source, target))
    return pairs


def halving_orders():
    y, x, _ = place(lax.axis_index("expert"))
    xs = [(partners("x", 1), (x ^ (x >> 1)) & 1), (partners("x", 3), x >> 1)]
    ys = [(partners("y", 1), (y ^ (y >> 1)) & 1), (partners("y", 3), y >> 1)]
    return [xs + ys, xs[::-1] + ys[::-1], ys + xs, ys[::-1] + xs[::-1]]


def expert_sum(value):
    parts = list(value.reshape(4, value.shape[0] // 4, value.shape[1]))
    orders = halving_orders()
    for step in range(4):
        for i in range(4):
            pairs, bit = orders[i][step]
            halves = parts[i].reshape(2, parts[i].shape[0] // 2, parts[i].shape[1])
            give = lax.dynamic_index_in_dim(halves, 1 - bit, 0, keepdims=False)
            keep = lax.dynamic_index_in_dim(halves, bit, 0, keepdims=False)
            parts[i] = keep + lax.ppermute(give, "expert", pairs)
    across = [(source, source ^ 1) for source in range(32)]
    for i in range(4):
        parts[i] = parts[i] + lax.ppermute(parts[i], "expert", across)
    for step in (3, 2, 1, 0):
        for i in range(4):
            pairs, bit = orders[i][step]
            mine = parts[i]
            other = lax.ppermute(mine, "expert", pairs)
            parts[i] = jnp.where(
                bit == 0, jnp.concatenate([mine, other]), jnp.concatenate([other, mine])
            )
    return jnp.concatenate(parts)


def on_device(
    tokens,
    cotangent,
    routes,
    attn_gain,
    w_query,
    key_weight,
    value_weight,
    w_out,
    moe_gain,
    w_router,
    w_gate,
    w_up,
    w_down,
):
    core = lax.axis_index("pipe")
    part = lax.axis_index("tensor")
    first = core == 0
    experts = w_router.shape[2]
    count = tokens.shape[1]
    lanes = 2 * routes.shape[3] * count // experts // 2

    def layers(value):
        other = swap(value, "pipe")
        return jnp.where(first, value, other), jnp.where(first, other, value)

    def own_layer(zero, one):
        return jnp.where(first, zero, one)

    attn_gains = [v.astype(F32) for v in layers(attn_gain[0])]
    moe_gains = [v.astype(F32) for v in layers(moe_gain[0])]
    routers = layers(w_router[0])
    wqs, wks, wvs, wos = (layers(v[0]) for v in (w_query, key_weight, value_weight, w_out))
    own_half = (w_gate[0, 0], w_up[0, 0], w_down[0, 0])
    far_half = tuple(swap(v, "tensor") for v in own_half)
    near = [layers(v) for v in own_half]
    far = [layers(v) for v in far_half]
    ffs = [
        (tuple(v[layer] for v in near), tuple(v[layer] for v in far)) for layer in range(2)
    ]
    mine = lax.dynamic_index_in_dim(routes[0], core, 0, keepdims=False)
    give = lax.dynamic_index_in_dim(routes[0], 1 - core, 0, keepdims=False)
    got = swap(give, "pipe")
    picks = [jnp.where(first, mine, got), jnp.where(first, got, mine)]

    cosine, sine = rotary_tables(count)
    x = lax.dynamic_index_in_dim(tokens, core, 0, keepdims=False).astype(F32)
    top = lax.dynamic_index_in_dim(cotangent, core, 0, keepdims=False)

    kept, outs = [], []
    for layer in range(2):
        weights = (wqs[layer], wks[layer], wvs[layer], wos[layer])
        branch, saved = attend_forward(x, attn_gains[layer], *weights, cosine, sine)
        h = x + (branch.astype(F32) + swap(branch, "tensor").astype(F32))
        scale = row_scale_of(h)
        normed = (h * scale * moe_gains[layer]).astype(BF16)
        hot, table = slot_table(picks[layer], experts, lanes, part)
        gates = gates_of(normed, routers[layer], hot)
        gated = gated_table(table, gates)
        rows = spread(table, normed, experts)
        made = experts_forward(rows, ffs[layer])
        back = send_back(made, experts)
        share = mul_tn(gated, back).astype(BF16)
        y = h + (share.astype(F32) + swap(share, "tensor").astype(F32))
        outs.append(y)
        kept.append((x, saved, h, scale, normed, table, gates, gated, rows, back, weights))
        x = y.astype(BF16).astype(F32)

    grad = top
    attn_grads, ff_grads, in_grads = [None, None], [None, None], [None, None]
    for layer in (1, 0):
        x, saved, h, scale, normed, table, gates, gated, rows, back, weights = kept[layer]
        grad_b = grad.astype(BF16)
        seen = (mul_nt(back, grad_b) * table.astype(F32)).reshape(experts, lanes, count)
        grad_gates = jnp.sum(seen, axis=1)
        grad_gates = grad_gates + swap(grad_gates, "tensor")
        dlogits = gates * (grad_gates - jnp.sum(gates * grad_gates, axis=0, keepdims=True))
        dlogits = dlogits.astype(BF16)
        grad_rows = spread(gated, grad_b, experts)
        dx, ff_grads[layer] = experts_backward(rows, grad_rows, ffs[layer])
        dback = send_back(dx, experts)
        share = mul_tn(table, dback).astype(BF16)
        grad_normed = share.astype(F32) + swap(share, "tensor").astype(F32)
        grad_normed = grad_normed + mul(dlogits, routers[layer], ((0,), (1,)))
        grad_router = mul(normed, dlogits, ((0,), (1,)))
        grad_h, grad_moe_gain = norm_back(h, scale, moe_gains[layer], grad_normed)
        grad_h = grad + grad_h
        da, attn = attend_backward(grad_h.astype(BF16), saved, *weights, cosine, sine)
        da = da.astype(F32) + swap(da, "tensor").astype(F32)
        grad_x, grad_attn_gain = norm_back(x, saved[0], attn_gains[layer], da)
        grad = grad_h + grad_x
        in_grads[layer] = grad
        dq, dk, dv, dout = (v.astype(BF16) for v in attn)
        side = jnp.concatenate(
            [grad_router, grad_attn_gain[:, None], grad_moe_gain[:, None]], axis=1
        )
        side = jnp.pad(side, ((0, 0), (0, 128 - side.shape[1]))).astype(BF16)
        width = dout.shape[1] // 2
        dout = jnp.concatenate([dout[:, :width], dout[:, width:]], axis=0)
        attn_grads[layer] = jnp.concatenate([dq, dk, dv, dout, side], axis=1)
        grad = grad.astype(BF16).astype(F32)

    def both_parts(zero, one):
        sent = own_layer(one, zero).astype(BF16)
        return own_layer(zero, one).astype(F32) + swap(sent, "pipe").astype(F32)

    packed = both_parts(attn_grads[0], attn_grads[1]).astype(BF16)
    packed = expert_sum(packed).astype(F32)
    ff_out = []
    for i in range(3):
        near_sum = both_parts(ff_grads[0][0][i], ff_grads[1][0][i])
        far_sum = both_parts(ff_grads[0][1][i], ff_grads[1][1][i])
        ff_out.append(near_sum + swap(far_sum.astype(BF16), "tensor").astype(F32))

    def by_layer(zero, one):
        own, other = own_layer(zero, one), own_layer(one, zero)
        got = swap(other, "pipe")
        return jnp.where(first, jnp.stack([own, got]), jnp.stack([got, own]))

    q_width, kv_width = w_query.shape[2], key_weight.shape[2]
    a, b = q_width + kv_width, q_width + 2 * kv_width
    c = b + w_out.shape[2] // 2
    half = w_out.shape[1]
    grad_out = jnp.concatenate([packed[:half, b:c], packed[half:, b:c]], axis=1)
    side = packed[:, c:]
    return (
        by_layer(*outs)[None],
        by_layer(*in_grads)[None],
        side[:, experts][None],
        packed[:, :q_width][None],
        packed[:, q_width:a][None],
        packed[:, a:b][None],
        grad_out[None],
        side[:, experts + 1][None],
        side[:, :experts][None],
        ff_out[0][None, None],
        ff_out[1][None, None],
        ff_out[2][None, None],
    )


def solution(mesh):
    layered = P("pipe", None, "expert", None)
    by_expert = P("pipe", "expert", None, "tensor")
    columns = P("pipe", None, "tensor")
    rows = P("pipe", "tensor", None)
    down = P("pipe", "expert", "tensor", None)
    whole = P("pipe", None)
    router = P("pipe", None, None)
    tokens = P(None, "expert", None)
    return jax.shard_map(
        on_device,
        mesh=mesh,
        in_specs=(
            tokens,
            tokens,
            layered,
            whole,
            columns,
            columns,
            columns,
            rows,
            whole,
            router,
            by_expert,
            by_expert,
            down,
        ),
        out_specs=(
            layered,
            layered,
            whole,
            columns,
            columns,
            columns,
            rows,
            whole,
            router,
            by_expert,
            by_expert,
            down,
        ),
        check_vma=False,
    )
```

```python
import jax
import jax.numpy as jnp
from jax import lax
from jax.experimental import pallas as pl
from jax.experimental.pallas import tpu as pltpu
from jax.sharding import PartitionSpec as P

HEAD = 128
NORM_EPS = 1e-06
ROPE_BASE = 10000.0
BF16 = jnp.bfloat16
F32 = jnp.float32
SWAP = [(0, 1), (1, 0)]
VMEM_LIMIT = 52 * 1024 * 1024


def swap(value, axis):
    return lax.ppermute(value, axis, SWAP)


def slot_groups(experts):
    return [[e * 2 + ((e % 2) ^ s) for e in range(experts)] for s in range(2)]


def expert_exchange(value):
    return lax.all_to_all(
        value,
        ("expert", "tensor"),
        split_axis=0,
        concat_axis=0,
        axis_index_groups=slot_groups(value.shape[0]),
        tiled=True,
    )


def plane_groups(level):
    groups = []
    for z in range(2):
        for i in range(4):
            along_y = [(y * 4 + i) * 2 + z for y in range(4)]
            along_x = [(i * 4 + x) * 2 + z for x in range(4)]
            zero, one = (along_y, along_x) if level == 0 else (along_x, along_y)
            groups += [zero, [32 + e for e in one]]
    return groups


def mul(left, right, dims):
    return lax.dot_general(left, right, (dims, ((), ())), preferred_element_type=F32)


def mul_nn(left, right):
    return mul(left, right, ((1,), (0,)))


def mul_nt(left, right):
    return mul(left, right, ((1,), (1,)))


def mul_tn(left, right):
    return mul(left, right, ((0,), (0,)))


VMEM = pl.BlockSpec(memory_space=pltpu.VMEM)
SMEM = pl.BlockSpec(memory_space=pltpu.SMEM)
ANY = pl.BlockSpec(memory_space=pl.ANY)


def call(body, outs, in_specs, scratch, operands, name, spaces=None):
    return pl.pallas_call(
        body,
        out_shape=[jax.ShapeDtypeStruct(shape, kind) for shape, kind in outs],
        in_specs=in_specs,
        out_specs=spaces or [VMEM] * len(outs),
        scratch_shapes=scratch,
        compiler_params=pltpu.CompilerParams(vmem_limit_bytes=VMEM_LIMIT),
        cost_estimate=pl.CostEstimate(flops=1024, bytes_accessed=1024, transcendentals=0),
        name=name,
    )(*operands)


def fetch(own, mine, theirs, target, sem):
    @pl.when(own == 1)
    def _():
        pltpu.make_async_copy(mine, target, sem).start()

    @pl.when(own != 1)
    def _():
        pltpu.make_async_copy(theirs, target, sem).start()


def arrive(mine, target, sem):
    pltpu.make_async_copy(mine, target, sem).wait()


def rotary_tables(count):
    half = HEAD // 2
    frequency = ROPE_BASE ** (-(jnp.arange(half, dtype=F32) * 2.0) / HEAD)
    angles = jnp.arange(count, dtype=F32)[:, None] * frequency[None, :]
    cosine = jnp.concatenate([jnp.cos(angles), jnp.cos(angles)], axis=1)
    sine = jnp.concatenate([-jnp.sin(angles), jnp.sin(angles)], axis=1)
    return cosine, sine


def turn(vector, cosine, sine):
    return vector * cosine + pltpu.roll(vector, HEAD // 2, 1) * sine


def turn_back(grad, cosine, sine):
    return grad * cosine - pltpu.roll(grad, HEAD // 2, 1) * sine


def row_scale_of(rows):
    return lax.rsqrt(jnp.mean(rows * rows, axis=-1, keepdims=True) + NORM_EPS)


def norm_back(rows, scale, gain, grad):
    scaled = grad * gain
    return scale * scaled - rows * (scale * scale * scale) * jnp.mean(
        scaled * rows, axis=-1, keepdims=True
    )


def attention_weights(q, k):
    count = q.shape[0]
    scores = mul_nt(q, k)
    row = lax.broadcasted_iota(jnp.int32, (count, count), 0)
    column = lax.broadcasted_iota(jnp.int32, (count, count), 1)
    scores = jnp.where(row >= column, scores, -1e30)
    raised = jnp.exp(scores - jnp.max(scores, axis=-1, keepdims=True))
    return raised / jnp.sum(raised, axis=-1, keepdims=True)


def head_of(index):
    return slice(index * HEAD, (index + 1) * HEAD)


def attend_body(own, x_ref, h_ref, a_ref, b_ref, gain, cos, sin, refs, outs, scratch):
    (wq, wq_r, wk, wk_r, wv, wv_r, wo, wo_r) = refs
    (qkv_s, wo_s, sems) = scratch
    (branch, q_o, kv_o, o_o, x_o, y_o) = outs
    mine = own[0]
    width = wo.shape[0]
    heads = width // HEAD
    kv_at = width + HEAD
    moves = [
        (wq, wq_r, qkv_s.at[:, :width]),
        (wk, wk_r, qkv_s.at[:, width:kv_at]),
        (wv, wv_r, qkv_s.at[:, kv_at:]),
        (wo, wo_r, wo_s),
    ]
    for i, (a, b, target) in enumerate(moves):
        fetch(mine, a, b, target, sems.at[i])
    if h_ref is None:
        x = x_ref[...].astype(F32)
    else:
        y = h_ref[...] + (a_ref[...].astype(F32) + b_ref[...].astype(F32))
        y_o[...] = y
        x_o[...] = y.astype(BF16)
        x = y.astype(BF16).astype(F32)
    normed = (x * row_scale_of(x) * gain[...]).astype(BF16)
    cosine, sine = cos[...], sin[...]
    for i in range(3):
        arrive(moves[i][0], moves[i][2], sems.at[i])
    made = mul_nn(normed, qkv_s[...])
    k = turn(made[:, width : width + HEAD], cosine, sine).astype(BF16)
    v = made[:, width + HEAD :].astype(BF16)
    kv_o[:, :HEAD] = k
    kv_o[:, HEAD:] = v
    for i in range(heads):
        q = (turn(made[:, head_of(i)], cosine, sine) * HEAD**-0.5).astype(BF16)
        q_o[:, head_of(i)] = q
        weights = attention_weights(q, k)
        o_o[:, head_of(i)] = mul_nn(weights.astype(BF16), v).astype(BF16)
    arrive(wo, wo_s, sems.at[3])
    branch[...] = mul_nn(o_o[...], wo_s[...]).astype(BF16)


def attend_forward(own, source, gain, cosine, sine, weights):
    later = isinstance(source, tuple)
    count = cosine.shape[0]
    width, model = weights[6].shape

    def body(own_ref, *refs):
        if later:
            h_ref, a_ref, b_ref, gain_ref, cos, sin = refs[:6]
            x_ref, rest = None, refs[6:]
        else:
            x_ref, gain_ref, cos, sin = refs[:4]
            h_ref, a_ref, b_ref, rest = None, None, None, refs[4:]
        ws, rest = rest[:8], rest[8:]
        outs, scratch = (rest[:6], rest[6:]) if later else (rest[:4] + (None, None), rest[4:])
        attend_body(
            own_ref, x_ref, h_ref, a_ref, b_ref, gain_ref, cos, sin, ws, outs, scratch
        )

    outs = [
        ((count, model), BF16),
        ((count, width), BF16),
        ((count, 2 * HEAD), BF16),
        ((count, width), BF16),
    ]
    if later:
        outs += [((count, model), BF16), ((count, model), F32)]
    values = source if later else (source,)
    return call(
        body,
        outs,
        [SMEM] + [VMEM] * (len(values) + 3) + [ANY] * 8,
        [
            pltpu.VMEM((model, width + 2 * HEAD), BF16),
            pltpu.VMEM((width, model), BF16),
            pltpu.SemaphoreType.DMA((4,)),
        ],
        (own, *values, gain, cosine, sine, *weights),
        "attend_forward",
    )


def hot_of(routes_ref, experts):
    count = routes_ref.shape[1]
    names = lax.broadcasted_iota(jnp.int32, (experts, count), 0)
    hot = routes_ref[0:1, :] == names
    for pick in range(1, routes_ref.shape[0]):
        hot = hot | (routes_ref[pick : pick + 1, :] == names)
    return hot


def slot_tables(lane, routes, top, experts, lanes):
    count, model = top.shape
    slots = experts * lanes

    def body(lane_ref, first_ref, second_ref, top_ref, first_o, second_o, rows_o):
        row = lax.broadcasted_iota(jnp.int32, (count, count), 0)
        column = lax.broadcasted_iota(jnp.int32, (count, count), 1)
        before = jnp.where(row < column, 1.0, 0.0).astype(BF16)
        place = lax.broadcasted_iota(jnp.int32, (lanes, count), 0).astype(F32)
        start = (lane_ref[0] * lanes).astype(F32)
        for routes_ref, out in ((first_ref, first_o), (second_ref, second_o)):
            hot = hot_of(routes_ref, experts)
            rank = mul_nn(jnp.where(hot, 1.0, 0.0).astype(BF16), before)
            rank = jnp.where(hot, rank, -1.0) - start
            for e in range(experts):
                chosen = jnp.where(rank[e : e + 1, :] == place, 1.0, 0.0)
                out[e * lanes : (e + 1) * lanes, :] = chosen.astype(BF16)
        rows_o[...] = mul_nn(second_o[...], top_ref[...].astype(BF16)).astype(BF16)

    return call(
        body,
        [((slots, count), BF16), ((slots, count), BF16), ((slots, model), BF16)],
        [SMEM] + [VMEM] * 3,
        [],
        (lane, *routes, top),
        "slot_tables",
    )


def pair_columns(value, count):
    high = value.astype(BF16).astype(F32)
    lanes = lax.broadcasted_iota(jnp.int32, (count, HEAD), 1)
    both = jnp.where(lanes == 0, high, jnp.where(lanes == 1, value - high, 0.0))
    return both.astype(BF16)


def dispatch(table, routes, x, own, received, gain, router, lanes, with_gates):
    count, model = x.shape
    experts = router.shape[0]
    slots = experts * lanes
    wide = model + HEAD if with_gates else model

    def body(table_ref, routes_ref, x_ref, a_ref, b_ref, gain_ref, router_ref, *outs):
        h_o, rows_o, gated_o, gates_o = outs
        h = x_ref[...].astype(F32) + (a_ref[...].astype(F32) + b_ref[...].astype(F32))
        h_o[...] = h
        normed = (h * row_scale_of(h) * gain_ref[...]).astype(BF16)
        rows_o[:, :model] = mul_nn(table_ref[...], normed).astype(BF16)
        hot = hot_of(routes_ref, experts)
        logits = jnp.where(hot, mul_nt(router_ref[...], normed), -1e30)
        raised = jnp.where(hot, jnp.exp(logits - jnp.max(logits, axis=0, keepdims=True)), 0.0)
        gates = raised / jnp.sum(raised, axis=0, keepdims=True)
        gates_o[...] = gates
        for e in range(experts):
            spot = slice(e * lanes, (e + 1) * lanes)
            gated = table_ref[spot, :].astype(F32) * gates[e : e + 1, :]
            gated_o[spot, :] = gated.astype(BF16)
            if with_gates:
                total = jnp.sum(gated, axis=1, keepdims=True)
                rows_o[spot, model:] = pair_columns(total, lanes)

    return call(
        body,
        [
            ((count, model), F32),
            ((slots, wide), BF16),
            ((slots, count), BF16),
            ((experts, count), F32),
        ],
        [VMEM] * 7,
        [],
        (table, routes, x, own, received, gain, router),
        "dispatch",
    )


def collect(table, back, experts):
    slots, count = table.shape
    lanes = slots // experts
    model = back.shape[1] - HEAD

    def body(table_ref, back_ref, share_o, seen_s):
        share_o[:, :model] = mul_tn(table_ref[...], back_ref[:, :model]).astype(BF16)
        value = back_ref[:, model:].astype(F32)
        value = value[:, 0:1] + value[:, 1:2]
        seen_s[...] = jnp.zeros_like(seen_s)
        for e in range(experts):
            spot = slice(e * lanes, (e + 1) * lanes)
            part = table_ref[spot, :].astype(F32) * value[spot, :]
            seen_s[e : e + 1, :] = jnp.sum(part, axis=0, keepdims=True)
        seen = seen_s[:experts, :]
        high = seen.astype(BF16).astype(F32)
        seen_s[experts : 2 * experts, :] = seen - high
        seen_s[:experts, :] = high
        share_o[:, model:] = seen_s[...].T.astype(BF16)

    return call(
        body,
        [((count, model + HEAD), BF16)],
        [VMEM] * 2,
        [pltpu.VMEM((HEAD, count), F32)],
        (table, back),
        "collect",
    )[0]


def turn_over(grad, x, own, received, gain, table, gated, back, experts):
    slots, count = table.shape
    lanes = slots // experts
    model = x.shape[1]

    def body(g_ref, x_ref, a_ref, b_ref, gain_ref, table_ref, gated_ref, back_ref, *outs):
        grad_o, low_o, rows_o, seen_o = outs
        x_v = x_ref[...].astype(F32)
        da = a_ref[...].astype(F32) + b_ref[...].astype(F32)
        total = g_ref[...] + norm_back(x_v, row_scale_of(x_v), gain_ref[...], da)
        grad_o[...] = total
        low = total.astype(BF16)
        low_o[...] = low
        rows_o[...] = mul_nn(gated_ref[...], low).astype(BF16)
        seen = mul_nt(back_ref[...], low) * table_ref[...].astype(F32)
        for e in range(experts):
            spot = slice(e * lanes, (e + 1) * lanes)
            seen_o[e : e + 1, :] = jnp.sum(seen[spot, :], axis=0, keepdims=True)

    return call(
        body,
        [
            ((count, model), F32),
            ((count, model), BF16),
            ((slots, model), BF16),
            ((experts, count), F32),
        ],
        [VMEM] * 8,
        [],
        (grad, x, own, received, gain, table, gated, back),
        "turn_over",
    )


def expert_moves(sources, wgu, wd, half):
    hidden = 2 * half
    targets = (wgu.at[:, :half], wgu.at[:, hidden : hidden + half], wd.at[:half, :])
    targets += (wgu.at[:, half:hidden], wgu.at[:, hidden + half :], wd.at[half:, :])
    return [(sources[i], sources[i + 3], t) for i, t in zip((0, 1, 2, 6, 7, 8), targets)]


def experts_forward(own, rows, weights):
    slots, model = rows.shape
    half = weights[0].shape[1]
    hidden = 2 * half
    tile = 256

    def body(own_ref, x_ref, *refs):
        sources, (y_o, wgu, wd, h_s, sems) = refs[:12], refs[12:]
        moves = expert_moves(sources, wgu, wd, half)
        for i in (0, 1, 3, 4, 2, 5):
            fetch(own_ref[0], moves[i][0], moves[i][1], moves[i][2], sems.at[i])
        for i in (0, 1, 3, 4):
            arrive(moves[i][0], moves[i][2], sems.at[i])

        def step(c, carry):
            at = pl.multiple_of(c * tile, tile)
            gate = mul_nn(x_ref[...], wgu[:, pl.ds(at, tile)])
            up = mul_nn(x_ref[...], wgu[:, pl.ds(at + hidden, tile)])
            act = gate / (1.0 + jnp.exp(-gate))
            h_s[:, pl.ds(at, tile)] = (act * up).astype(BF16)
            return carry

        lax.fori_loop(0, hidden // tile, step, 0)
        for i in (2, 5):
            arrive(moves[i][0], moves[i][2], sems.at[i])

        def finish(c, carry):
            spot = pl.ds(pl.multiple_of(c * tile, tile), tile)
            y_o[:, spot] = mul_nn(h_s[...], wd[:, spot]).astype(BF16)
            return carry

        lax.fori_loop(0, model // tile, finish, 0)

    return call(
        body,
        [((slots, model), BF16)],
        [SMEM, VMEM] + [ANY] * 12,
        [
            pltpu.VMEM((model, 2 * hidden), BF16),
            pltpu.VMEM((hidden, model), BF16),
            pltpu.VMEM((slots, hidden), BF16),
            pltpu.SemaphoreType.DMA((6,)),
        ],
        (own, rows, *weights),
        "experts_forward",
    )[0]


def experts_backward(own, rows, grads, weights):
    slots, wide = rows.shape
    model, half = weights[0].shape
    hidden = 2 * half
    gated = wide > model
    tile = 256

    def body(own_ref, x_ref, g_ref, *refs):
        sources, refs = refs[:12], refs[12:]
        dx_o, h_o, dgu_o, wgu, wd, sems = refs[:6]
        moves = expert_moves(sources, wgu, wd, half)
        for i in (0, 1, 3, 4, 2, 5):
            fetch(own_ref[0], moves[i][0], moves[i][1], moves[i][2], sems.at[i])
        if gated:
            scale = x_ref[:, model:].astype(F32)
            scale = scale[:, 0:1] + scale[:, 1:2]
            seen_s = refs[6]
            seen_s[...] = jnp.zeros_like(seen_s)
        for i in range(6):
            arrive(moves[i][0], moves[i][2], sems.at[i])

        def step(c, carry):
            at = pl.multiple_of(c * tile, tile)
            spot, later = pl.ds(at, tile), pl.ds(at + hidden, tile)
            gate = mul_nn(x_ref[:, :model], wgu[:, spot])
            up = mul_nn(x_ref[:, :model], wgu[:, later])
            sig = 1.0 / (1.0 + jnp.exp(-gate))
            act = gate * sig
            made = act * up
            h_o[:, spot] = made.astype(BF16)
            grad_hidden = mul_nt(g_ref[...], wd[spot, :])
            if gated:
                seen = made * grad_hidden
                seen_s[...] += seen[:, :HEAD] + seen[:, HEAD:]
                grad_hidden = grad_hidden * scale
            dgu_o[:, spot] = (grad_hidden * up * sig * (1.0 + gate * (1.0 - sig))).astype(BF16)
            dgu_o[:, later] = (grad_hidden * act).astype(BF16)
            return carry

        lax.fori_loop(0, hidden // tile, step, 0)

        def finish(c, carry):
            spot = pl.ds(pl.multiple_of(c * tile, tile), tile)
            dx_o[:, spot] = mul_nt(dgu_o[...], wgu[spot, :]).astype(BF16)
            return carry

        lax.fori_loop(0, model // tile, finish, 0)
        if gated:
            total = jnp.sum(seen_s[...], axis=1, keepdims=True)
            dx_o[:, model:] = pair_columns(total, slots)

    return call(
        body,
        [((slots, wide), BF16), ((slots, hidden), BF16), ((slots, 2 * hidden), BF16)],
        [SMEM, VMEM, VMEM] + [ANY] * 12,
        [
            pltpu.VMEM((model, 2 * hidden), BF16),
            pltpu.VMEM((hidden, model), BF16),
            pltpu.SemaphoreType.DMA((6,)),
        ]
        + ([pltpu.VMEM((slots, HEAD), F32)] if gated else []),
        (own, rows, grads, *weights),
        "experts_backward",
    )


def experts_grads(own, rows, grads, hidden_rows, dgu, weights):
    slots, wide = rows.shape
    model, half = weights[0].shape
    hidden = 2 * half
    blocks = model // half
    gated = wide > model
    tile = 256

    def body(own_ref, x_ref, g_ref, h_ref, dgu_ref, *refs):
        sources, refs = refs[:4], refs[4:]
        near_o, far_o, refs = refs[0], refs[1], refs[2:]
        if gated:
            y_o, xt_s, dy_s, wd, sems = refs
            moves = [
                (sources[0], sources[1], wd.at[:half, :]),
                (sources[2], sources[3], wd.at[half:, :]),
            ]
            for i, (a, b, target) in enumerate(moves):
                fetch(own_ref[0], a, b, target, sems.at[i])
            scale = x_ref[:, model:].astype(F32)
            scale = scale[:, 0:1] + scale[:, 1:2]
            dy_s[...] = (g_ref[...].astype(F32) * scale).astype(BF16)
        else:
            (xt_s,), dy_s = refs, g_ref
        for i in range(model // tile):
            xt_s[i * tile : (i + 1) * tile, :] = x_ref[:, i * tile : (i + 1) * tile].T
        if gated:
            for i, (a, b, target) in enumerate(moves):
                arrive(a, target, sems.at[i])

        def step(c, carry):
            spot = pl.ds(pl.multiple_of(c * tile, tile), tile)
            made = mul_nn(xt_s[spot, :], dgu_ref[...]).astype(BF16)
            near_o[spot, :half] = made[:, :half]
            far_o[spot, :half] = made[:, half:hidden]
            near_o[spot, half:hidden] = made[:, hidden : hidden + half]
            far_o[spot, half:hidden] = made[:, hidden + half :]
            if gated:
                y_o[:, spot] = mul_nn(h_ref[...], wd[:, spot]).astype(BF16)
            return carry

        lax.fori_loop(0, model // tile, step, 0)
        down = tile // 2
        for i in range(hidden // down):
            made = mul_tn(h_ref[:, i * down : (i + 1) * down], dy_s[...]).astype(BF16)
            low = i * down
            out, low = (near_o, low) if low < half else (far_o, low - half)
            for j in range(blocks):
                at = j * half + low
                out[at : at + down, hidden:] = made[:, j * half : (j + 1) * half]

    outs = [((model, 3 * half), BF16)] * 2
    scratch = [pltpu.VMEM((model, slots), BF16)]
    if gated:
        outs = outs + [((slots, model), BF16)]
        scratch += [
            pltpu.VMEM((slots, model), BF16),
            pltpu.VMEM((hidden, model), BF16),
            pltpu.SemaphoreType.DMA((2,)),
        ]
    return call(
        body,
        outs,
        [SMEM] + [VMEM] * 4 + [ANY] * 4,
        scratch,
        (own, rows, grads, hidden_rows, dgu, *[weights[i] for i in (2, 5, 8, 11)]),
        "experts_grads",
    )


def attend_backward(
    own, grad, h, x, shares, gates, seen, router, moe_gain, attn_gain, kept, cosine, sine, weights
):
    count, model = h.shape
    width = weights[6].shape[0]
    heads = width // HEAD
    experts = router.shape[0]
    kv_at, out_at = width + HEAD, width + 2 * HEAD
    riding = len(seen) == 0

    def body(own_ref, *refs):
        (g_ref, h_ref, x_ref, a_ref, b_ref, gates_ref) = refs[:6]
        refs = refs[6:]
        if riding:
            tail = a_ref[:, model:].astype(F32) + b_ref[:, model:].astype(F32)
            tail = tail.T
            grad_gates = tail[:experts, :] + tail[experts : 2 * experts, :]
        else:
            grad_gates = refs[0][...] + refs[1][...]
            refs = refs[2:]
        (router_ref, mgain_ref, again_ref, q_ref, kv_ref, cos, sin) = refs[:7]
        (wq, wq_r, wk, wk_r, wv, wv_r, wo, wo_r) = refs[7:15]
        (dqkv_o, da_o, gh_o, dlogits_o, gains_o) = refs[15:20]
        (qkv_s, wo_s, sems) = refs[20:]
        mine = own_ref[0]
        moves = [
            (wo, wo_r, wo_s),
            (wq, wq_r, qkv_s.at[:, :width]),
            (wk, wk_r, qkv_s.at[:, width:kv_at]),
            (wv, wv_r, qkv_s.at[:, kv_at:]),
        ]
        for i, (a, b, target) in enumerate(moves):
            fetch(mine, a, b, target, sems.at[i])
        gates_v = gates_ref[...]
        dlogits = gates_v * (grad_gates - jnp.sum(gates_v * grad_gates, axis=0, keepdims=True))
        dlogits = dlogits.astype(BF16)
        dlogits_o[...] = dlogits
        dn = a_ref[:, :model].astype(F32) + b_ref[:, :model].astype(F32)
        dn = dn + mul_tn(dlogits, router_ref[...])
        hv = h_ref[...]
        scale = row_scale_of(hv)
        gh = g_ref[...].astype(F32) + norm_back(hv, scale, mgain_ref[...], dn)
        gh_o[...] = gh
        moe_part = jnp.sum(dn * hv * scale, axis=0, keepdims=True)
        dz = gh.astype(BF16)
        arrive(wo, wo_s, sems.at[0])
        do = mul_nt(dz, wo_s[...]).astype(BF16)
        cosine_v, sine_v = cos[...], sin[...]
        k, v = kv_ref[:, :HEAD], kv_ref[:, HEAD:]
        dk, dv = 0.0, 0.0
        for i in range(heads):
            q = q_ref[:, head_of(i)]
            p = attention_weights(q, k)
            do_i = do[:, head_of(i)]
            dp = mul_nt(do_i, v)
            ds = (p * (dp - jnp.sum(p * dp, axis=-1, keepdims=True))).astype(BF16)
            dv = dv + mul_tn(p.astype(BF16), do_i)
            dk = dk + mul_tn(ds, q)
            dq = turn_back(mul_nn(ds, k), cosine_v, sine_v) * HEAD**-0.5
            dqkv_o[:, head_of(i)] = dq.astype(BF16)
        dqkv_o[:, width:kv_at] = turn_back(dk, cosine_v, sine_v).astype(BF16)
        dqkv_o[:, kv_at:] = dv.astype(BF16)
        for i in range(1, 4):
            arrive(moves[i][0], moves[i][2], sems.at[i])
        da = mul_nt(dqkv_o[...], qkv_s[...])
        da_o[...] = da.astype(BF16)
        xv = x_ref[...].astype(F32)
        attn_part = jnp.sum(da * xv * row_scale_of(xv), axis=0, keepdims=True)
        lane = lax.broadcasted_iota(jnp.int32, (16, model), 0)
        total = jnp.zeros((16, model), F32)
        for i, value in enumerate((attn_part, moe_part)):
            high = value.astype(BF16).astype(F32)
            total = jnp.where(lane == 2 * i, high, total)
            total = jnp.where(lane == 2 * i + 1, value - high, total)
        gains_o[...] = total.astype(BF16)

    q, kv, _ = kept
    operands = (own, grad, h, x, *shares, gates, *seen, router, moe_gain, attn_gain)
    operands += (q, kv, cosine, sine)
    return call(
        body,
        [
            ((count, out_at), BF16),
            ((count, model), BF16),
            ((count, model), F32),
            ((experts, count), BF16),
            ((16, model), BF16),
        ],
        [SMEM] + [VMEM] * (len(operands) - 1) + [ANY] * 8,
        [
            pltpu.VMEM((model, out_at), BF16),
            pltpu.VMEM((width, model), BF16),
            pltpu.SemaphoreType.DMA((4,)),
        ],
        (*operands, *weights),
        "attend_backward",
    )


def attend_grads(own, x, h, grad_h, o, dqkv, dlogits, gains, attn_gain, moe_gain):
    count, model = h.shape
    width, out_at = o.shape[1], dqkv.shape[1]
    experts = dlogits.shape[0]
    side_at = out_at + model // 2
    tile = 256
    parts = model // tile // 2

    def body(own_ref, x_ref, h_ref, gh_ref, o_ref, dqkv_ref, dl_ref, gains_ref, again, mgain, *rest):
        keep_o, give_o, left_s, pack_s, sems = rest
        xv = x_ref[...].astype(F32)
        normed = (xv * row_scale_of(xv) * again[...]).astype(BF16)
        for i in range(model // tile):
            left_s[i * tile : (i + 1) * tile, :] = normed[:, i * tile : (i + 1) * tile].T
        hv = h_ref[...]
        normed_m = (hv * row_scale_of(hv) * mgain[...]).astype(BF16)
        dz = gh_ref[...].astype(BF16)
        row = lax.broadcasted_iota(jnp.int32, (experts, HEAD), 0)
        column = lax.broadcasted_iota(jnp.int32, (experts, HEAD), 1)
        spread_logits = mul_tn(dl_ref[...], jnp.where(row == column, 1.0, 0.0).astype(BF16))
        spread_logits = spread_logits.astype(BF16)
        row = lax.broadcasted_iota(jnp.int32, (16, HEAD), 0)
        column = lax.broadcasted_iota(jnp.int32, (16, HEAD), 1)
        hit = (column == experts + row // 2) & (row < 4)
        marks = jnp.where(hit, 1.0, 0.0).astype(BF16)

        def step(c, carry):
            spot = pl.ds(pl.multiple_of(c * tile, tile), tile)
            target = pl.ds(pl.multiple_of(lax.rem(c, parts) * tile, tile), tile)
            made = mul_nn(left_s[spot, :], dqkv_ref[...]).astype(BF16)
            pack_s[lax.div(c, parts), target, :out_at] = made
            return carry

        lax.fori_loop(0, model // tile, step, 0)
        for i in range(width // HEAD):
            made = mul_tn(o_ref[:, head_of(i)], dz).astype(BF16)
            spot = slice(i * HEAD, (i + 1) * HEAD)
            pack_s[0, spot, out_at:side_at] = made[:, : model // 2]
            pack_s[1, spot, out_at:side_at] = made[:, model // 2 :]
        for i in range(model // tile):
            spot = slice(i * tile, (i + 1) * tile)
            total = mul_tn(normed_m[:, spot], spread_logits) + mul_tn(gains_ref[:, spot], marks)
            at = (i % parts) * tile
            pack_s[i // parts, at : at + tile, side_at:] = total.astype(BF16)
        kept = 1 - own_ref[0]
        copies = [
            pltpu.make_async_copy(pack_s.at[kept], keep_o, sems.at[0]),
            pltpu.make_async_copy(pack_s.at[1 - kept], give_o, sems.at[1]),
        ]
        for copy in copies:
            copy.start()
        for copy in copies:
            copy.wait()

    return call(
        body,
        [((model // 2, side_at + HEAD), BF16)] * 2,
        [SMEM] + [VMEM] * 9,
        [
            pltpu.VMEM((model, count), BF16),
            pltpu.VMEM((2, model // 2, side_at + HEAD), BF16),
            pltpu.SemaphoreType.DMA((2,)),
        ],
        (own, x, h, grad_h, o, dqkv, dlogits, gains, attn_gain, moe_gain),
        "attend_grads",
        [ANY, ANY],
    )


def ff_total(core, zero, one):
    model, wide = zero[0].shape
    half = wide // 3
    blocks = model // half
    pieces = len(zero) - 2
    rows = model // pieces
    count = len(zero)

    def body(core_ref, *refs):
        ins, outs, (held, sems) = refs[: 2 * count], refs[2 * count : 2 * count + 3], refs[-2:]
        targets = [held.at[0], held.at[1]]
        targets += [held.at[2, i * rows : (i + 1) * rows] for i in range(pieces)]
        for i, target in enumerate(targets):
            fetch(core_ref[0], ins[count + i], ins[i], target, sems.at[i])
        for i, target in enumerate(targets):
            arrive(ins[i], target, sems.at[i])

        def total(rows, columns):
            return (
                held[0, rows, columns].astype(F32)
                + held[1, rows, columns].astype(F32)
                + held[2, rows, columns].astype(F32)
            )

        for i in range(blocks):
            spot = slice(i * half, (i + 1) * half)
            outs[0][spot, :] = total(spot, slice(0, half))
            outs[1][spot, :] = total(spot, slice(half, 2 * half))
            outs[2][:, spot] = total(spot, slice(2 * half, wide))

    return call(
        body,
        [((model, half), F32), ((model, half), F32), ((half, model), F32)],
        [SMEM] + [ANY] * (2 * count),
        [pltpu.VMEM((3, model, wide), BF16), pltpu.SemaphoreType.DMA((count,))],
        (core, *zero, *one),
        "ff_total",
    )


def attn_total(core, zero, one, width, model):
    rows, wide = zero[0].shape
    out_at = width + 2 * HEAD
    side_at = out_at + model // 2

    def body(core_ref, *refs):
        ins, outs, (held, sems) = refs[:4], refs[4:9], refs[9:]
        for i in range(2):
            fetch(core_ref[0], ins[2 + i], ins[i], held.at[i], sems.at[i])
        query, key, value, out, side = outs
        for i in range(2):
            arrive(ins[i], held.at[i], sems.at[i])
            spot = slice(i * rows, (i + 1) * rows)
            query[spot, :] = held[i, :, :width].astype(F32)
            key[spot, :] = held[i, :, width : width + HEAD].astype(F32)
            value[spot, :] = held[i, :, width + HEAD : out_at].astype(F32)
            out[:, i * (model // 2) : (i + 1) * (model // 2)] = held[i, :, out_at:side_at].astype(F32)
            side[spot, :] = held[i, :, side_at:].astype(F32)

    return call(
        body,
        [
            ((model, width), F32),
            ((model, HEAD), F32),
            ((model, HEAD), F32),
            ((width, model), F32),
            ((model, wide - side_at), F32),
        ],
        [SMEM] + [ANY] * 4,
        [pltpu.VMEM((2, rows, wide), BF16), pltpu.SemaphoreType.DMA((2,))],
        (core, *zero, *one),
        "attn_total",
    )


def exchange_rows(rows, experts):
    return expert_exchange(rows.reshape(experts, -1, rows.shape[1])).reshape(-1, rows.shape[1])


def plane_exchange(value, level):
    return lax.all_to_all(
        value,
        ("pipe", "expert"),
        split_axis=0,
        concat_axis=0,
        axis_index_groups=plane_groups(level),
        tiled=True,
    )


def plane_sum(value, level):
    rows, wide = value.shape
    arrived = plane_exchange(value.reshape(4, rows // 4, wide), level)
    return jnp.sum(arrived.astype(F32), axis=0).astype(BF16)


def plane_copy(piece, level):
    rows, wide = piece.shape
    spread = jnp.broadcast_to(piece[None], (4, rows, wide))
    return plane_exchange(spread, level).reshape(4 * rows, wide)


def plane_gather(piece, level):
    return lax.all_gather(
        piece, ("pipe", "expert"), axis=0, axis_index_groups=plane_groups(level), tiled=True
    )


def across_planes(piece):
    return piece + lax.ppermute(piece, "expert", [(e, e ^ 1) for e in range(32)])


def after(value, *others):
    return lax.optimization_barrier((value, *others))[0]


def on_device(
    tokens,
    cotangent,
    routes,
    attn_gain,
    w_query,
    key_weight,
    value_weight,
    w_out,
    moe_gain,
    w_router,
    w_gate,
    w_up,
    w_down,
):
    core = lax.axis_index("pipe")
    part = lax.axis_index("tensor")
    first = core == 0
    experts = w_router.shape[2]
    count, model = tokens.shape[1], tokens.shape[2]
    lanes = 2 * routes.shape[3] * count // experts // 2
    lane = (part ^ (lax.axis_index("expert") % 2)).astype(jnp.int32).reshape(1)
    owns = [(core == layer).astype(jnp.int32).reshape(1) for layer in range(2)]

    mine = lax.dynamic_index_in_dim(routes[0], core, 0, keepdims=False)
    give = lax.dynamic_index_in_dim(routes[0], 1 - core, 0, keepdims=False)
    got = swap(give, "pipe")
    picks = [jnp.where(first, mine, got).T, jnp.where(first, got, mine).T]
    half = w_gate.shape[3]
    width = w_out.shape[1]
    mine_w = (w_query[0], key_weight[0], value_weight[0], w_out[0])
    attn_weights = [v for w in mine_w for v in (w, swap(w, "pipe"))]
    small = jnp.concatenate([w_router[0].T, attn_gain, moe_gain], axis=0)
    small_r = swap(small, "pipe")
    smalls = jnp.where(first, small, small_r), jnp.where(first, small_r, small)
    routers = [v[:experts] for v in smalls]
    attn_gains = [v[experts : experts + 1].astype(F32) for v in smalls]
    moe_gains = [v[experts + 1 :].astype(F32) for v in smalls]

    def over(value, layer):
        return lax.ppermute(value, "pipe", [(1 - layer, layer)])

    def across(value, layer):
        pairs = [(2 * layer, 2 * layer + 1), (2 * layer + 1, 2 * layer)]
        return lax.ppermute(value, ("pipe", "tensor"), pairs)

    cosine, sine = rotary_tables(count)
    x_0 = lax.dynamic_index_in_dim(tokens, core, 0, keepdims=False)
    top = lax.dynamic_index_in_dim(cotangent, core, 0, keepdims=False)
    near = (w_gate[0, 0], w_up[0, 0], w_down[0, 0])
    far_0 = [across(near[0], 0)]

    table_0, table_1, top_rows = slot_tables(lane, picks, top, experts, lanes)
    x_0 = after(x_0, table_0)
    branch, *kept_0 = attend_forward(owns[0], x_0, attn_gains[0], cosine, sine, attn_weights)
    branch_r = swap(after(branch, far_0[0]), "tensor")
    far_0 += [across(after(w, branch_r), 0) for w in near[1:]]
    h_0, rows, gated_0, gates_0 = dispatch(
        table_0, picks[0], x_0, branch, branch_r, moe_gains[0], routers[0], lanes, False
    )
    rows_0 = exchange_rows(rows, experts)
    near_r = [swap(after(w, branch_r), "pipe") for w in near]
    far_0r = [over(w, 1) for w in far_0]
    rows_0 = after(rows_0, *near_r, *far_0r)
    far_1 = [across(after(w, rows_0), 1) for w in near[:2]]
    ff_0 = (*near, *near_r, *far_0, *far_0r)
    back_0 = exchange_rows(experts_forward(owns[0], rows_0, ff_0), experts)
    share = after(mul_tn(gated_0, back_0).astype(BF16), *far_1)
    share_r = swap(share, "tensor")
    top_rows = exchange_rows(after(top_rows, share), experts)
    far_1r = [over(after(w, share_r), 0) for w in far_1]

    branch, *kept_1, x_1, y_0 = attend_forward(
        owns[1], (h_0, share, share_r), attn_gains[1], cosine, sine, attn_weights
    )
    branch_r = swap(branch, "tensor")
    far_1 += [across(after(near[2], branch_r), 1)]
    far_1r += [over(far_1[2], 0)]
    h_1, rows, gated_1, gates_1 = dispatch(
        table_1, picks[1], x_1, branch, branch_r, moe_gains[1], routers[1], lanes, True
    )
    rows_1 = exchange_rows(after(rows, top_rows), experts)
    ff_1 = (*near, *near_r, *far_1, *far_1r)
    dx, made, dgu = experts_backward(owns[1], rows_1, top_rows, ff_1)
    dx = exchange_rows(dx, experts)
    near_1, far_g1, out_rows = experts_grads(owns[1], rows_1, top_rows, made, dgu, ff_1)
    dx = after(dx, near_1)
    pieces = model // 3

    def far_pieces(mine, theirs):
        return [
            mine[i : i + pieces] + theirs[i : i + pieces] for i in range(0, model, pieces)
        ]

    share = collect(table_1, dx, experts)
    share_r = swap(share, "tensor")
    back_1 = exchange_rows(after(out_rows, share), experts)
    near_1r, far_r = over(after(near_1, share), 1), over(after(far_g1, share), 1)
    dqkv, da, grad_h, dlogits, gains = attend_backward(
        owns[1], top, h_1, x_1, (share, share_r), gates_1, (),
        routers[1], moe_gains[1], attn_gains[1], kept_1, cosine, sine, attn_weights,
    )
    da_r = swap(after(da, near_1r, far_r), "tensor")
    far_sum = far_pieces(far_g1, far_r)
    keep, give = attend_grads(
        owns[1], x_1, h_1, grad_h, kept_1[2], dqkv, dlogits, gains, attn_gains[1], moe_gains[1]
    )
    grad_1, grad, rows, seen = turn_over(
        grad_h, x_1, da, after(da_r, back_1, keep), attn_gains[1], table_0, gated_0, back_0,
        experts,
    )

    seen_r = swap(seen, "tensor")
    grad_rows = exchange_rows(rows, experts)
    far_z = [across(after(far_sum[0], rows), 1)]
    half_1 = keep + swap(after(give, rows), "pipe")
    share = mul_tn(gated_1, back_1).astype(BF16)
    share_r = swap(after(share, rows), "tensor")
    grad_rows = after(grad_rows, half_1, share_r, seen_r, far_z[0])
    y_1 = h_1 + (share.astype(F32) + share_r.astype(F32))
    far_z += [across(after(far_sum[1], grad_rows), 1)]
    dx, made, dgu = experts_backward(owns[0], rows_0, grad_rows, ff_0)
    far_z += [across(after(far_sum[2], dx), 1)]
    ff_grads_1 = (near_1, near_1r, *far_z)
    dx = exchange_rows(after(dx, far_z[1]), experts)
    near_0, far_g0 = experts_grads(owns[0], rows_0, grad_rows, made, dgu, ff_0)
    dx = after(dx, near_0, far_z[2])
    share = mul_tn(table_0, dx).astype(BF16)
    share_r = swap(share, "tensor")
    level_1 = plane_sum(after(half_1, share), 0)
    near_0r, far_r = over(after(near_0, share), 0), over(after(far_g0, share), 0)
    dqkv, da, grad_h, dlogits, gains = attend_backward(
        owns[0], grad, h_0, x_0, (share, share_r), gates_0, (seen, seen_r),
        routers[0], moe_gains[0], attn_gains[0], kept_0, cosine, sine, attn_weights,
    )
    da_r = swap(after(da, near_0r, far_r), "tensor")
    keep, give = attend_grads(
        owns[0], x_0, h_0, grad_h, kept_0[2], after(dqkv, level_1), dlogits, gains,
        attn_gains[0], moe_gains[0],
    )
    far_sum = far_pieces(far_g0, far_r)

    half_0 = after(keep, *far_sum) + swap(give, "pipe")
    far_z = [across(after(far_sum[0], half_0), 0)]
    level_0 = plane_sum(half_0, 0)
    level = after(jnp.concatenate([level_0, level_1], axis=1), far_z[0], da_r)
    wide = level_0.shape[1]
    piece = across_planes(plane_sum(level, 1))
    far_z += [across(after(v, piece), 0) for v in far_sum[1:]]
    part = plane_copy(piece, 1)
    da = da.astype(F32) + da_r.astype(F32)
    x_f = x_0.astype(F32)
    grad_0 = grad_h + norm_back(x_f, row_scale_of(x_f), attn_gains[0], da)
    ff_grads_0 = (near_0, near_0r, *far_z)

    def by_layer(zero, one):
        own, other = jnp.where(first, zero, one), jnp.where(first, one, zero)
        got = swap(other, "pipe")
        return got, jnp.where(first, jnp.stack([own, got]), jnp.stack([got, own]))

    got_y, layer_out = by_layer(y_0, y_1)
    got_g, input_grads = by_layer(grad_0, grad_1)
    part = after(part, got_y, got_g)
    sum_0 = plane_copy(part[:, :wide], 0)
    sum_1 = plane_gather(part[:, wide:], 0)
    core_v = core.astype(jnp.int32).reshape(1)
    gate_g, up_g, down_g = ff_total(core_v, ff_grads_0, ff_grads_1)
    over_0, over_1 = over(after(sum_0, gate_g), 0), over(sum_1, 1)
    query_g, key_g, value_g, out_g, side = attn_total(
        core_v, (sum_0, over_0), (sum_1, over_1), width, model
    )
    at = wide - HEAD + experts
    attn_part = jnp.concatenate(
        [
            jnp.where(first, zero[:, at], one[:, at]).astype(F32)
            for zero, one in ((sum_0, sum_1), (over_0, over_1))
        ]
    )
    attn_part = attn_part + swap(attn_part, "tensor")
    return (
        layer_out[None],
        input_grads[None],
        attn_part[None],
        query_g[None],
        key_g[None],
        value_g[None],
        out_g[None],
        side[:, experts + 1][None],
        side[:, :experts][None],
        gate_g[None, None],
        up_g[None, None],
        down_g[None, None],
    )


def solution(mesh):
    layered = P("pipe", None, "expert", None)
    by_expert = P("pipe", "expert", None, "tensor")
    columns = P("pipe", None, "tensor")
    rows = P("pipe", "tensor", None)
    down = P("pipe", "expert", "tensor", None)
    whole = P("pipe", None)
    router = P("pipe", None, None)
    tokens = P(None, "expert", None)
    return jax.shard_map(
        on_device,
        mesh=mesh,
        in_specs=(
            tokens,
            tokens,
            layered,
            whole,
            columns,
            columns,
            columns,
            rows,
            whole,
            router,
            by_expert,
            by_expert,
            down,
        ),
        out_specs=(
            layered,
            layered,
            whole,
            columns,
            columns,
            columns,
            rows,
            whole,
            router,
            by_expert,
            by_expert,
            down,
        ),
        check_vma=False,
    )
```

```python
import jax
import jax.numpy as jnp
from jax import lax
from jax.experimental import pallas as pl
from jax.experimental.pallas import tpu as pltpu
from jax.sharding import PartitionSpec as P

HEAD = 128
NORM_EPS = 1e-06
ROPE_BASE = 10000.0
BF16 = jnp.bfloat16
F32 = jnp.float32
SWAP = [(0, 1), (1, 0)]
VMEM_LIMIT = 52 * 1024 * 1024


def swap(value, axis):
    return lax.ppermute(value, axis, SWAP)


def slot_groups(experts):
    return [[e * 2 + ((e % 2) ^ s) for e in range(experts)] for s in range(2)]


def expert_exchange(value):
    return lax.all_to_all(
        value,
        ("expert", "tensor"),
        split_axis=0,
        concat_axis=0,
        axis_index_groups=slot_groups(value.shape[0]),
        tiled=True,
    )


def plane_groups(level):
    groups = []
    if level < 2:
        for z in range(2):
            for i in range(4):
                along_y = [(y * 4 + i) * 2 + z for y in range(4)]
                along_x = [(i * 4 + x) * 2 + z for x in range(4)]
                zero, one = (along_y, along_x) if level == 0 else (along_x, along_y)
                groups += [zero, [32 + e for e in one]]
    else:
        for i in range(4):
            along_x = [(i * 4 + x) * 2 + z for x in range(4) for z in range(2)]
            along_y = [(y * 4 + i) * 2 + z for y in range(4) for z in range(2)]
            groups += [along_x, [32 + e for e in along_y]]
    return groups


def mul(left, right, dims):
    return lax.dot_general(left, right, (dims, ((), ())), preferred_element_type=F32)


def mul_nn(left, right):
    return mul(left, right, ((1,), (0,)))


def mul_nt(left, right):
    return mul(left, right, ((1,), (1,)))


def mul_tn(left, right):
    return mul(left, right, ((0,), (0,)))


VMEM = pl.BlockSpec(memory_space=pltpu.VMEM)
SMEM = pl.BlockSpec(memory_space=pltpu.SMEM)
ANY = pl.BlockSpec(memory_space=pl.ANY)


def call(body, outs, in_specs, scratch, operands, name, spaces=None):
    return pl.pallas_call(
        body,
        out_shape=[jax.ShapeDtypeStruct(shape, kind) for shape, kind in outs],
        in_specs=in_specs,
        out_specs=spaces or [VMEM] * len(outs),
        scratch_shapes=scratch,
        compiler_params=pltpu.CompilerParams(vmem_limit_bytes=VMEM_LIMIT),
        cost_estimate=pl.CostEstimate(flops=1024, bytes_accessed=1024, transcendentals=0),
        name=name,
    )(*operands)


def fetch(own, mine, theirs, target, sem):
    @pl.when(own == 1)
    def _():
        pltpu.make_async_copy(mine, target, sem).start()

    @pl.when(own != 1)
    def _():
        pltpu.make_async_copy(theirs, target, sem).start()


def arrive(mine, target, sem):
    pltpu.make_async_copy(mine, target, sem).wait()


def rotary_tables(count):
    half = HEAD // 2
    frequency = ROPE_BASE ** (-(jnp.arange(half, dtype=F32) * 2.0) / HEAD)
    angles = jnp.arange(count, dtype=F32)[:, None] * frequency[None, :]
    cosine = jnp.concatenate([jnp.cos(angles), jnp.cos(angles)], axis=1)
    sine = jnp.concatenate([-jnp.sin(angles), jnp.sin(angles)], axis=1)
    return cosine, sine


def turn(vector, cosine, sine):
    return vector * cosine + pltpu.roll(vector, HEAD // 2, 1) * sine


def turn_back(grad, cosine, sine):
    return grad * cosine - pltpu.roll(grad, HEAD // 2, 1) * sine


def row_scale_of(rows):
    return lax.rsqrt(jnp.mean(rows * rows, axis=-1, keepdims=True) + NORM_EPS)


def norm_back(rows, scale, gain, grad):
    scaled = grad * gain
    return scale * scaled - rows * (scale * scale * scale) * jnp.mean(
        scaled * rows, axis=-1, keepdims=True
    )


def attention_weights(q, k):
    count = q.shape[0]
    scores = mul_nt(q, k)
    row = lax.broadcasted_iota(jnp.int32, (count, count), 0)
    column = lax.broadcasted_iota(jnp.int32, (count, count), 1)
    scores = jnp.where(row >= column, scores, -1e30)
    raised = jnp.exp(scores - jnp.max(scores, axis=-1, keepdims=True))
    return raised / jnp.sum(raised, axis=-1, keepdims=True)


def head_of(index):
    return slice(index * HEAD, (index + 1) * HEAD)


def attend_body(own, x_ref, h_ref, a_ref, b_ref, gain, cos, sin, refs, outs, scratch):
    (wq, wq_r, wk, wk_r, wv, wv_r, wo, wo_r) = refs
    (qkv_s, wo_s, sems) = scratch
    (branch, q_o, kv_o, o_o, x_o, y_o) = outs
    mine = own[0]
    width = wo.shape[0]
    heads = width // HEAD
    kv_at = width + HEAD
    moves = [
        (wq, wq_r, qkv_s.at[:, :width]),
        (wk, wk_r, qkv_s.at[:, width:kv_at]),
        (wv, wv_r, qkv_s.at[:, kv_at:]),
        (wo, wo_r, wo_s),
    ]
    for i, (a, b, target) in enumerate(moves):
        fetch(mine, a, b, target, sems.at[i])
    if h_ref is None:
        x = x_ref[...].astype(F32)
    else:
        y = h_ref[...] + (a_ref[...].astype(F32) + b_ref[...].astype(F32))
        y_o[...] = y
        x_o[...] = y.astype(BF16)
        x = y.astype(BF16).astype(F32)
    normed = (x * row_scale_of(x) * gain[...]).astype(BF16)
    cosine, sine = cos[...], sin[...]
    for i in range(3):
        arrive(moves[i][0], moves[i][2], sems.at[i])
    made = mul_nn(normed, qkv_s[...])
    k = turn(made[:, width : width + HEAD], cosine, sine).astype(BF16)
    v = made[:, width + HEAD :].astype(BF16)
    kv_o[:, :HEAD] = k
    kv_o[:, HEAD:] = v
    for i in range(heads):
        q = (turn(made[:, head_of(i)], cosine, sine) * HEAD**-0.5).astype(BF16)
        q_o[:, head_of(i)] = q
        weights = attention_weights(q, k)
        o_o[:, head_of(i)] = mul_nn(weights.astype(BF16), v).astype(BF16)
    arrive(wo, wo_s, sems.at[3])
    branch[...] = mul_nn(o_o[...], wo_s[...]).astype(BF16)


def attend_forward(own, source, gain, cosine, sine, weights):
    later = isinstance(source, tuple)
    count = cosine.shape[0]
    width, model = weights[6].shape

    def body(own_ref, *refs):
        if later:
            h_ref, a_ref, b_ref, gain_ref, cos, sin = refs[:6]
            x_ref, rest = None, refs[6:]
        else:
            x_ref, gain_ref, cos, sin = refs[:4]
            h_ref, a_ref, b_ref, rest = None, None, None, refs[4:]
        ws, rest = rest[:8], rest[8:]
        outs, scratch = (rest[:6], rest[6:]) if later else (rest[:4] + (None, None), rest[4:])
        attend_body(
            own_ref, x_ref, h_ref, a_ref, b_ref, gain_ref, cos, sin, ws, outs, scratch
        )

    outs = [
        ((count, model), BF16),
        ((count, width), BF16),
        ((count, 2 * HEAD), BF16),
        ((count, width), BF16),
    ]
    if later:
        outs += [((count, model), BF16), ((count, model), F32)]
    values = source if later else (source,)
    return call(
        body,
        outs,
        [SMEM] + [VMEM] * (len(values) + 3) + [ANY] * 8,
        [
            pltpu.VMEM((model, width + 2 * HEAD), BF16),
            pltpu.VMEM((width, model), BF16),
            pltpu.SemaphoreType.DMA((4,)),
        ],
        (own, *values, gain, cosine, sine, *weights),
        "attend_forward",
    )


def hot_of(routes_ref, experts):
    count = routes_ref.shape[1]
    names = lax.broadcasted_iota(jnp.int32, (experts, count), 0)
    hot = routes_ref[0:1, :] == names
    for pick in range(1, routes_ref.shape[0]):
        hot = hot | (routes_ref[pick : pick + 1, :] == names)
    return hot


def slot_tables(lane, routes, top, experts, lanes):
    count, model = top.shape
    slots = experts * lanes

    def body(lane_ref, first_ref, second_ref, top_ref, first_o, second_o, rows_o):
        row = lax.broadcasted_iota(jnp.int32, (count, count), 0)
        column = lax.broadcasted_iota(jnp.int32, (count, count), 1)
        before = jnp.where(row < column, 1.0, 0.0).astype(BF16)
        place = lax.broadcasted_iota(jnp.int32, (lanes, count), 0).astype(F32)
        start = (lane_ref[0] * lanes).astype(F32)
        for routes_ref, out in ((first_ref, first_o), (second_ref, second_o)):
            hot = hot_of(routes_ref, experts)
            rank = mul_nn(jnp.where(hot, 1.0, 0.0).astype(BF16), before)
            rank = jnp.where(hot, rank, -1.0) - start
            for e in range(experts):
                chosen = jnp.where(rank[e : e + 1, :] == place, 1.0, 0.0)
                out[e * lanes : (e + 1) * lanes, :] = chosen.astype(BF16)
        rows_o[...] = mul_nn(second_o[...], top_ref[...].astype(BF16)).astype(BF16)

    return call(
        body,
        [((slots, count), BF16), ((slots, count), BF16), ((slots, model), BF16)],
        [SMEM] + [VMEM] * 3,
        [],
        (lane, *routes, top),
        "slot_tables",
    )


def pair_columns(value, count):
    high = value.astype(BF16).astype(F32)
    lanes = lax.broadcasted_iota(jnp.int32, (count, HEAD), 1)
    both = jnp.where(lanes == 0, high, jnp.where(lanes == 1, value - high, 0.0))
    return both.astype(BF16)


def dispatch(table, routes, x, own, received, gain, router, lanes, with_gates):
    count, model = x.shape
    experts = router.shape[0]
    slots = experts * lanes
    wide = model + HEAD if with_gates else model

    def body(table_ref, routes_ref, x_ref, a_ref, b_ref, gain_ref, router_ref, *outs):
        h_o, rows_o, gated_o, gates_o = outs
        h = x_ref[...].astype(F32) + (a_ref[...].astype(F32) + b_ref[...].astype(F32))
        h_o[...] = h
        normed = (h * row_scale_of(h) * gain_ref[...]).astype(BF16)
        rows_o[:, :model] = mul_nn(table_ref[...], normed).astype(BF16)
        hot = hot_of(routes_ref, experts)
        logits = jnp.where(hot, mul_nt(router_ref[...], normed), -1e30)
        raised = jnp.where(hot, jnp.exp(logits - jnp.max(logits, axis=0, keepdims=True)), 0.0)
        gates = raised / jnp.sum(raised, axis=0, keepdims=True)
        gates_o[...] = gates
        for e in range(experts):
            spot = slice(e * lanes, (e + 1) * lanes)
            gated = table_ref[spot, :].astype(F32) * gates[e : e + 1, :]
            gated_o[spot, :] = gated.astype(BF16)
            if with_gates:
                total = jnp.sum(gated, axis=1, keepdims=True)
                rows_o[spot, model:] = pair_columns(total, lanes)

    return call(
        body,
        [
            ((count, model), F32),
            ((slots, wide), BF16),
            ((slots, count), BF16),
            ((experts, count), F32),
        ],
        [VMEM] * 7,
        [],
        (table, routes, x, own, received, gain, router),
        "dispatch",
    )


def collect(table, back, experts):
    slots, count = table.shape
    lanes = slots // experts
    model = back.shape[1] - HEAD

    def body(table_ref, back_ref, share_o, seen_s):
        share_o[:, :model] = mul_tn(table_ref[...], back_ref[:, :model]).astype(BF16)
        value = back_ref[:, model:].astype(F32)
        value = value[:, 0:1] + value[:, 1:2]
        seen_s[...] = jnp.zeros_like(seen_s)
        for e in range(experts):
            spot = slice(e * lanes, (e + 1) * lanes)
            part = table_ref[spot, :].astype(F32) * value[spot, :]
            seen_s[e : e + 1, :] = jnp.sum(part, axis=0, keepdims=True)
        seen = seen_s[:experts, :]
        high = seen.astype(BF16).astype(F32)
        seen_s[experts : 2 * experts, :] = seen - high
        seen_s[:experts, :] = high
        share_o[:, model:] = seen_s[...].T.astype(BF16)

    return call(
        body,
        [((count, model + HEAD), BF16)],
        [VMEM] * 2,
        [pltpu.VMEM((HEAD, count), F32)],
        (table, back),
        "collect",
    )[0]


def turn_over(grad, x, own, received, gain, table, gated, back, experts):
    slots, count = table.shape
    lanes = slots // experts
    model = x.shape[1]

    def body(g_ref, x_ref, a_ref, b_ref, gain_ref, table_ref, gated_ref, back_ref, *outs):
        grad_o, low_o, rows_o, seen_o = outs
        x_v = x_ref[...].astype(F32)
        da = a_ref[...].astype(F32) + b_ref[...].astype(F32)
        total = g_ref[...] + norm_back(x_v, row_scale_of(x_v), gain_ref[...], da)
        grad_o[...] = total
        low = total.astype(BF16)
        low_o[...] = low
        rows_o[...] = mul_nn(gated_ref[...], low).astype(BF16)
        seen = mul_nt(back_ref[...], low) * table_ref[...].astype(F32)
        for e in range(experts):
            spot = slice(e * lanes, (e + 1) * lanes)
            seen_o[e : e + 1, :] = jnp.sum(seen[spot, :], axis=0, keepdims=True)

    return call(
        body,
        [
            ((count, model), F32),
            ((count, model), BF16),
            ((slots, model), BF16),
            ((experts, count), F32),
        ],
        [VMEM] * 8,
        [],
        (grad, x, own, received, gain, table, gated, back),
        "turn_over",
    )


def expert_moves(sources, wgu, wd, half):
    hidden = 2 * half
    targets = (wgu.at[:, :half], wgu.at[:, hidden : hidden + half], wd.at[:half, :])
    targets += (wgu.at[:, half:hidden], wgu.at[:, hidden + half :], wd.at[half:, :])
    return [(sources[i], sources[i + 3], t) for i, t in zip((0, 1, 2, 6, 7, 8), targets)]


def experts_forward(own, rows, weights):
    slots, model = rows.shape
    half = weights[0].shape[1]
    hidden = 2 * half
    tile = 256

    def body(own_ref, x_ref, *refs):
        sources, (y_o, x_s, wgu, wd, h_s, sems) = refs[:12], refs[12:]
        moves = expert_moves(sources, wgu, wd, half)
        arrival = pltpu.make_async_copy(x_ref, x_s, sems.at[6])
        arrival.start()
        for i in (0, 1, 3, 4, 2, 5):
            fetch(own_ref[0], moves[i][0], moves[i][1], moves[i][2], sems.at[i])
        arrival.wait()
        for i in (0, 1):
            arrive(moves[i][0], moves[i][2], sems.at[i])

        def step(c, carry):
            @pl.when(c == 1)
            def _():
                for i in (3, 4):
                    arrive(moves[i][0], moves[i][2], sems.at[i])

            at = pl.multiple_of(c * tile, tile)
            gate = mul_nn(x_s[...], wgu[:, pl.ds(at, tile)])
            up = mul_nn(x_s[...], wgu[:, pl.ds(at + hidden, tile)])
            act = gate / (1.0 + jnp.exp(-gate))
            h_s[:, pl.ds(at, tile)] = (act * up).astype(BF16)
            return carry

        lax.fori_loop(0, hidden // tile, step, 0)
        for i in (2, 5):
            arrive(moves[i][0], moves[i][2], sems.at[i])

        def finish(c, carry):
            spot = pl.ds(pl.multiple_of(c * tile, tile), tile)
            y_o[:, spot] = mul_nn(h_s[...], wd[:, spot]).astype(BF16)
            return carry

        lax.fori_loop(0, model // tile, finish, 0)

    return call(
        body,
        [((slots, model), BF16)],
        [SMEM] + [ANY] * 13,
        [
            pltpu.VMEM((slots, model), BF16),
            pltpu.VMEM((model, 2 * hidden), BF16),
            pltpu.VMEM((hidden, model), BF16),
            pltpu.VMEM((slots, hidden), BF16),
            pltpu.SemaphoreType.DMA((7,)),
        ],
        (own, rows, *weights),
        "experts_forward",
    )[0]


def experts_backward(own, rows, grads, weights):
    slots, wide = rows.shape
    model, half = weights[0].shape
    hidden = 2 * half
    gated = wide > model
    tile = 256

    def body(own_ref, x_ref, g_ref, *refs):
        sources, refs = refs[:12], refs[12:]
        dx_o, h_o, dgu_o, x_s, g_s, h_s, dgu_s, wgu, wd, sems = refs[:10]
        moves = expert_moves(sources, wgu, wd, half)
        arrivals = [
            pltpu.make_async_copy(x_ref, x_s, sems.at[6]),
            pltpu.make_async_copy(g_ref, g_s, sems.at[7]),
        ]
        leaving = [
            pltpu.make_async_copy(h_s, h_o, sems.at[8]),
            pltpu.make_async_copy(dgu_s, dgu_o, sems.at[9]),
        ]
        arrivals[0].start()
        for i in (0, 1, 2, 3, 4, 5):
            fetch(own_ref[0], moves[i][0], moves[i][1], moves[i][2], sems.at[i])
            if i == 1:
                arrivals[1].start()
        arrivals[0].wait()
        if gated:
            scale = x_s[:, model:].astype(F32)
            scale = scale[:, 0:1] + scale[:, 1:2]
            seen_s = refs[10]
            seen_s[...] = jnp.zeros_like(seen_s)
        for i in (0, 1):
            arrive(moves[i][0], moves[i][2], sems.at[i])
        arrivals[1].wait()
        arrive(moves[2][0], moves[2][2], sems.at[2])

        def step(c, carry):
            @pl.when(c == 1)
            def _():
                for i in (3, 4, 5):
                    arrive(moves[i][0], moves[i][2], sems.at[i])

            at = pl.multiple_of(c * tile, tile)
            spot, later = pl.ds(at, tile), pl.ds(at + hidden, tile)
            gate = mul_nn(x_s[:, :model], wgu[:, spot])
            up = mul_nn(x_s[:, :model], wgu[:, later])
            sig = 1.0 / (1.0 + jnp.exp(-gate))
            act = gate * sig
            made = act * up
            h_s[:, spot] = made.astype(BF16)
            grad_hidden = mul_nt(g_s[...], wd[spot, :])
            if gated:
                seen = made * grad_hidden
                seen_s[...] += seen[:, :HEAD] + seen[:, HEAD:]
                grad_hidden = grad_hidden * scale
            dgu_s[:, spot] = (grad_hidden * up * sig * (1.0 + gate * (1.0 - sig))).astype(BF16)
            dgu_s[:, later] = (grad_hidden * act).astype(BF16)
            return carry

        lax.fori_loop(0, hidden // tile, step, 0)
        for copy in leaving:
            copy.start()

        def finish(c, carry):
            spot = pl.ds(pl.multiple_of(c * tile, tile), tile)
            dx_o[:, spot] = mul_nt(dgu_s[...], wgu[spot, :]).astype(BF16)
            return carry

        lax.fori_loop(0, model // tile, finish, 0)
        if gated:
            total = jnp.sum(seen_s[...], axis=1, keepdims=True)
            dx_o[:, model:] = pair_columns(total, slots)
        for copy in leaving:
            copy.wait()

    return call(
        body,
        [((slots, wide), BF16), ((slots, hidden), BF16), ((slots, 2 * hidden), BF16)],
        [SMEM] + [ANY] * 14,
        [
            pltpu.VMEM((slots, wide), BF16),
            pltpu.VMEM((slots, model), BF16),
            pltpu.VMEM((slots, hidden), BF16),
            pltpu.VMEM((slots, 2 * hidden), BF16),
            pltpu.VMEM((model, 2 * hidden), BF16),
            pltpu.VMEM((hidden, model), BF16),
            pltpu.SemaphoreType.DMA((10,)),
        ]
        + ([pltpu.VMEM((slots, HEAD), F32)] if gated else []),
        (own, rows, grads, *weights),
        "experts_backward",
        [VMEM, ANY, ANY],
    )


def experts_grads(own, rows, grads, hidden_rows, dgu, weights):
    slots, wide = rows.shape
    model, half = weights[0].shape
    hidden = 2 * half
    blocks = model // half
    gated = wide > model
    tile = 256

    def body(own_ref, x_ref, g_ref, h_ref, dgu_ref, *refs):
        sources, refs = refs[:4], refs[4:]
        both_o, refs = refs[0], refs[1:]
        if gated:
            y_o, xt_s, dy_s, wd, sems = refs
            moves = [
                (sources[0], sources[1], wd.at[:half, :]),
                (sources[2], sources[3], wd.at[half:, :]),
            ]
            for i, (a, b, target) in enumerate(moves):
                fetch(own_ref[0], a, b, target, sems.at[i])
            scale = x_ref[:, model:].astype(F32)
            scale = scale[:, 0:1] + scale[:, 1:2]
            dy_s[...] = (g_ref[...].astype(F32) * scale).astype(BF16)
        else:
            (xt_s,), dy_s = refs, g_ref
        for i in range(model // tile):
            xt_s[i * tile : (i + 1) * tile, :] = x_ref[:, i * tile : (i + 1) * tile].T
        if gated:
            for i, (a, b, target) in enumerate(moves):
                arrive(a, target, sems.at[i])

        def step(c, carry):
            spot = pl.ds(pl.multiple_of(c * tile, tile), tile)
            made = mul_nn(xt_s[spot, :], dgu_ref[...]).astype(BF16)
            both_o[0, spot, :half] = made[:, :half]
            both_o[1, spot, :half] = made[:, half:hidden]
            both_o[0, spot, half:hidden] = made[:, hidden : hidden + half]
            both_o[1, spot, half:hidden] = made[:, hidden + half :]
            if gated:
                y_o[:, spot] = mul_nn(h_ref[...], wd[:, spot]).astype(BF16)
            return carry

        lax.fori_loop(0, model // tile, step, 0)
        down = tile // 2
        for i in range(hidden // down):
            made = mul_tn(h_ref[:, i * down : (i + 1) * down], dy_s[...]).astype(BF16)
            low = i * down
            side, low = (0, low) if low < half else (1, low - half)
            for j in range(blocks):
                at = j * half + low
                both_o[side, at : at + down, hidden:] = made[:, j * half : (j + 1) * half]

    outs = [((2, model, 3 * half), BF16)]
    scratch = [pltpu.VMEM((model, slots), BF16)]
    if gated:
        outs = outs + [((slots, model), BF16)]
        scratch += [
            pltpu.VMEM((slots, model), BF16),
            pltpu.VMEM((hidden, model), BF16),
            pltpu.SemaphoreType.DMA((2,)),
        ]
    return call(
        body,
        outs,
        [SMEM] + [VMEM] * 4 + [ANY] * 4,
        scratch,
        (own, rows, grads, hidden_rows, dgu, *[weights[i] for i in (2, 5, 8, 11)]),
        "experts_grads",
    )


def attend_backward(
    own, grad, h, x, shares, gates, seen, router, moe_gain, attn_gain, kept, cosine, sine, weights
):
    count, model = h.shape
    width = weights[6].shape[0]
    heads = width // HEAD
    experts = router.shape[0]
    kv_at, out_at = width + HEAD, width + 2 * HEAD
    riding = len(seen) == 0

    def body(own_ref, *refs):
        (g_ref, h_ref, x_ref, a_ref, b_ref, gates_ref) = refs[:6]
        refs = refs[6:]
        if riding:
            tail = a_ref[:, model:].astype(F32) + b_ref[:, model:].astype(F32)
            tail = tail.T
            grad_gates = tail[:experts, :] + tail[experts : 2 * experts, :]
        else:
            grad_gates = refs[0][...] + refs[1][...]
            refs = refs[2:]
        (router_ref, mgain_ref, again_ref, q_ref, kv_ref, cos, sin) = refs[:7]
        (wq, wq_r, wk, wk_r, wv, wv_r, wo, wo_r) = refs[7:15]
        (dqkv_o, da_o, gh_o, dlogits_o, gains_o) = refs[15:20]
        (qkv_s, wo_s, sems) = refs[20:]
        mine = own_ref[0]
        moves = [
            (wo, wo_r, wo_s),
            (wq, wq_r, qkv_s.at[:, :width]),
            (wk, wk_r, qkv_s.at[:, width:kv_at]),
            (wv, wv_r, qkv_s.at[:, kv_at:]),
        ]
        for i, (a, b, target) in enumerate(moves):
            fetch(mine, a, b, target, sems.at[i])
        gates_v = gates_ref[...]
        dlogits = gates_v * (grad_gates - jnp.sum(gates_v * grad_gates, axis=0, keepdims=True))
        dlogits = dlogits.astype(BF16)
        dlogits_o[...] = dlogits
        dn = a_ref[:, :model].astype(F32) + b_ref[:, :model].astype(F32)
        dn = dn + mul_tn(dlogits, router_ref[...])
        hv = h_ref[...]
        scale = row_scale_of(hv)
        gh = g_ref[...].astype(F32) + norm_back(hv, scale, mgain_ref[...], dn)
        gh_o[...] = gh
        moe_part = jnp.sum(dn * hv * scale, axis=0, keepdims=True)
        dz = gh.astype(BF16)
        arrive(wo, wo_s, sems.at[0])
        do = mul_nt(dz, wo_s[...]).astype(BF16)
        cosine_v, sine_v = cos[...], sin[...]
        k, v = kv_ref[:, :HEAD], kv_ref[:, HEAD:]
        dk, dv = 0.0, 0.0
        for i in range(heads):
            q = q_ref[:, head_of(i)]
            p = attention_weights(q, k)
            do_i = do[:, head_of(i)]
            dp = mul_nt(do_i, v)
            ds = (p * (dp - jnp.sum(p * dp, axis=-1, keepdims=True))).astype(BF16)
            dv = dv + mul_tn(p.astype(BF16), do_i)
            dk = dk + mul_tn(ds, q)
            dq = turn_back(mul_nn(ds, k), cosine_v, sine_v) * HEAD**-0.5
            dqkv_o[:, head_of(i)] = dq.astype(BF16)
        dqkv_o[:, width:kv_at] = turn_back(dk, cosine_v, sine_v).astype(BF16)
        dqkv_o[:, kv_at:] = dv.astype(BF16)
        for i in range(1, 4):
            arrive(moves[i][0], moves[i][2], sems.at[i])
        da = mul_nt(dqkv_o[...], qkv_s[...])
        da_o[...] = da.astype(BF16)
        xv = x_ref[...].astype(F32)
        attn_part = jnp.sum(da * xv * row_scale_of(xv), axis=0, keepdims=True)
        lane = lax.broadcasted_iota(jnp.int32, (16, model), 0)
        total = jnp.zeros((16, model), F32)
        for i, value in enumerate((attn_part, moe_part)):
            high = value.astype(BF16).astype(F32)
            total = jnp.where(lane == 2 * i, high, total)
            total = jnp.where(lane == 2 * i + 1, value - high, total)
        gains_o[...] = total.astype(BF16)

    q, kv, _ = kept
    operands = (own, grad, h, x, *shares, gates, *seen, router, moe_gain, attn_gain)
    operands += (q, kv, cosine, sine)
    return call(
        body,
        [
            ((count, out_at), BF16),
            ((count, model), BF16),
            ((count, model), F32),
            ((experts, count), BF16),
            ((16, model), BF16),
        ],
        [SMEM] + [VMEM] * (len(operands) - 1) + [ANY] * 8,
        [
            pltpu.VMEM((model, out_at), BF16),
            pltpu.VMEM((width, model), BF16),
            pltpu.SemaphoreType.DMA((4,)),
        ],
        (*operands, *weights),
        "attend_backward",
    )


def attend_grads(own, x, h, grad_h, o, dqkv, dlogits, gains, gains_r, attn_gain, moe_gain):
    count, model = h.shape
    width, out_at = o.shape[1], dqkv.shape[1]
    experts = dlogits.shape[0]
    side_at = out_at + model // 2
    tile = 256
    parts = model // tile // 2

    def body(own_ref, x_ref, h_ref, gh_ref, o_ref, dqkv_ref, dl_ref, *rest):
        gains_ref, far_ref, again, mgain, *rest = rest
        keep_o, give_o, left_s, pack_s, sems = rest
        xv = x_ref[...].astype(F32)
        normed = (xv * row_scale_of(xv) * again[...]).astype(BF16)
        for i in range(model // tile):
            left_s[i * tile : (i + 1) * tile, :] = normed[:, i * tile : (i + 1) * tile].T
        hv = h_ref[...]
        normed_m = (hv * row_scale_of(hv) * mgain[...]).astype(BF16)
        dz = gh_ref[...].astype(BF16)
        row = lax.broadcasted_iota(jnp.int32, (experts, HEAD), 0)
        column = lax.broadcasted_iota(jnp.int32, (experts, HEAD), 1)
        spread_logits = mul_tn(dl_ref[...], jnp.where(row == column, 1.0, 0.0).astype(BF16))
        spread_logits = spread_logits.astype(BF16)
        row = lax.broadcasted_iota(jnp.int32, (16, HEAD), 0)
        column = lax.broadcasted_iota(jnp.int32, (16, HEAD), 1)
        hit = (column == experts + row // 2) & (row < 4)
        marks = jnp.where(hit, 1.0, 0.0).astype(BF16)
        far_marks = jnp.where(hit & (row < 2), 1.0, 0.0).astype(BF16)

        def step(c, carry):
            spot = pl.ds(pl.multiple_of(c * tile, tile), tile)
            target = pl.ds(pl.multiple_of(lax.rem(c, parts) * tile, tile), tile)
            made = mul_nn(left_s[spot, :], dqkv_ref[...]).astype(BF16)
            pack_s[lax.div(c, parts), target, :out_at] = made
            return carry

        lax.fori_loop(0, model // tile, step, 0)
        for i in range(width // HEAD):
            made = mul_tn(o_ref[:, head_of(i)], dz).astype(BF16)
            spot = slice(i * HEAD, (i + 1) * HEAD)
            pack_s[0, spot, out_at:side_at] = made[:, : model // 2]
            pack_s[1, spot, out_at:side_at] = made[:, model // 2 :]
        for i in range(model // tile):
            spot = slice(i * tile, (i + 1) * tile)
            total = mul_tn(normed_m[:, spot], spread_logits)
            total = total + mul_tn(gains_ref[:, spot], marks)
            total = total + mul_tn(far_ref[:, spot], far_marks)
            at = (i % parts) * tile
            pack_s[i // parts, at : at + tile, side_at:] = total.astype(BF16)
        kept = 1 - own_ref[0]
        copies = [
            pltpu.make_async_copy(pack_s.at[kept], keep_o, sems.at[0]),
            pltpu.make_async_copy(pack_s.at[1 - kept], give_o, sems.at[1]),
        ]
        for copy in copies:
            copy.start()
        for copy in copies:
            copy.wait()

    return call(
        body,
        [((model // 2, side_at + HEAD), BF16)] * 2,
        [SMEM] + [VMEM] * 10,
        [
            pltpu.VMEM((model, count), BF16),
            pltpu.VMEM((2, model // 2, side_at + HEAD), BF16),
            pltpu.SemaphoreType.DMA((2,)),
        ],
        (own, x, h, grad_h, o, dqkv, dlogits, gains, gains_r, attn_gain, moe_gain),
        "attend_grads",
        [ANY, ANY],
    )


def ff_total(core, zero, one):
    _, model, wide = zero[0].shape
    half = wide // 3
    blocks = model // half

    def parts(refs):
        return [refs[0].at[0], refs[1].at[0], *refs[2:]]

    def body(core_ref, *refs):
        first, second = parts(refs[: len(zero)]), parts(refs[len(zero) : len(zero) + len(one)])
        outs, (held, sems) = refs[-5:-2], refs[-2:]

        def moves(sources):
            targets, low = [held.at[0], held.at[1]], 0
            for ref in sources[2:]:
                targets.append(held.at[2, low : low + ref.shape[0]])
                low += ref.shape[0]
            pairs = enumerate(zip(sources, targets))
            return [pltpu.make_async_copy(a, b, sems.at[i]) for i, (a, b) in pairs]

        for number, sources in ((0, first), (1, second)):

            @pl.when(core_ref[0] == number)
            def _(sources=sources):
                for copy in moves(sources):
                    copy.start()
                for copy in moves(sources):
                    copy.wait()

        def total(rows, columns):
            return (
                held[0, rows, columns].astype(F32)
                + held[1, rows, columns].astype(F32)
                + held[2, rows, columns].astype(F32)
            )

        for i in range(blocks):
            spot = slice(i * half, (i + 1) * half)
            outs[0][spot, :] = total(spot, slice(0, half))
            outs[1][spot, :] = total(spot, slice(half, 2 * half))
            outs[2][:, spot] = total(spot, slice(2 * half, wide))

    return call(
        body,
        [((model, half), F32), ((model, half), F32), ((half, model), F32)],
        [SMEM] + [ANY] * (len(zero) + len(one)),
        [pltpu.VMEM((3, model, wide), BF16), pltpu.SemaphoreType.DMA((4,))],
        (core, *zero, *one),
        "ff_total",
    )


def attn_total(core, zero, one, width, model, experts):
    rows, wide = zero[0].shape
    out_at = width + 2 * HEAD
    side_at = out_at + model // 2

    def body(core_ref, *refs):
        ins, outs, (held, sems) = refs[:4], refs[4:11], refs[11:]
        fetch(core_ref[0], ins[3], ins[1], held.at[1], sems.at[1])
        piece = rows // 16

        @pl.when(core_ref[0] == 1)
        def _():
            for y in range(4):
                for x in range(4):
                    source = ins[2].at[(y * 4 + x) * piece : (y * 4 + x + 1) * piece]
                    target = held.at[0, (x * 4 + y) * piece : (x * 4 + y + 1) * piece]
                    pltpu.make_async_copy(source, target, sems.at[0]).start()

        @pl.when(core_ref[0] != 1)
        def _():
            pltpu.make_async_copy(ins[0], held.at[0], sems.at[0]).start()

        query, key, value, out, router, attn, moe = outs
        for i in range(2):
            arrive(ins[i], held.at[i], sems.at[i])
            spot = slice(i * rows, (i + 1) * rows)
            query[spot, :] = held[i, :, :width].astype(F32)
            key[spot, :] = held[i, :, width : width + HEAD].astype(F32)
            value[spot, :] = held[i, :, width + HEAD : out_at].astype(F32)
            out[:, i * (model // 2) : (i + 1) * (model // 2)] = held[i, :, out_at:side_at].astype(F32)
            for j in range(0, rows, HEAD):
                side = held[i, j : j + HEAD, side_at:].astype(F32).T
                at = slice(i * rows + j, i * rows + j + HEAD)
                router[:, at] = side[:experts, :]
                attn[:, at] = side[experts : experts + 1, :]
                moe[:, at] = side[experts + 1 : experts + 2, :]

    return call(
        body,
        [
            ((model, width), F32),
            ((model, HEAD), F32),
            ((model, HEAD), F32),
            ((width, model), F32),
            ((experts, model), F32),
            ((1, model), F32),
            ((1, model), F32),
        ],
        [SMEM] + [ANY] * 4,
        [pltpu.VMEM((2, rows, wide), BF16), pltpu.SemaphoreType.DMA((2,))],
        (core, *zero, *one),
        "attn_total",
    )


def exchange_rows(rows, experts):
    return expert_exchange(rows.reshape(experts, -1, rows.shape[1])).reshape(-1, rows.shape[1])


def plane_exchange(value, level):
    return lax.all_to_all(
        value,
        ("pipe", "expert"),
        split_axis=0,
        concat_axis=0,
        axis_index_groups=plane_groups(level),
        tiled=True,
    )


def plane_sum(value, level, *others):
    rows, wide = value.shape
    count = len(plane_groups(level)[0])
    arrived = plane_exchange(value.reshape(count, rows // count, wide), level)
    return jnp.sum(after(arrived, *others).astype(F32), axis=0).astype(BF16)


def plane_copy(piece, level):
    rows, wide = piece.shape
    count = len(plane_groups(level)[0])
    spread = jnp.broadcast_to(piece[None], (count, rows, wide))
    return plane_exchange(spread, level).reshape(count * rows, wide)


def gather_plane(piece):
    plane = [[(y * 4 + x) * 2 + z for y in range(4) for x in range(4)] for z in range(2)]
    groups = plane + [[32 + e for e in group] for group in plane]
    return lax.all_gather(
        piece, ("pipe", "expert"), axis=0, axis_index_groups=groups, tiled=True
    )


def background_sum(value, level):
    return lax.psum_scatter(
        value,
        ("pipe", "expert"),
        scatter_dimension=0,
        axis_index_groups=plane_groups(level),
        tiled=True,
    )


def across_planes(piece):
    return piece + lax.ppermute(piece, "expert", [(e, e ^ 1) for e in range(32)])


def after(value, *others):
    return lax.optimization_barrier((value, *others))[0]


def on_device(
    tokens,
    cotangent,
    routes,
    attn_gain,
    w_query,
    key_weight,
    value_weight,
    w_out,
    moe_gain,
    w_router,
    w_gate,
    w_up,
    w_down,
):
    core = lax.axis_index("pipe")
    part = lax.axis_index("tensor")
    first = core == 0
    experts = w_router.shape[2]
    count, model = tokens.shape[1], tokens.shape[2]
    lanes = 2 * routes.shape[3] * count // experts // 2
    lane = (part ^ (lax.axis_index("expert") % 2)).astype(jnp.int32).reshape(1)
    owns = [(core == layer).astype(jnp.int32).reshape(1) for layer in range(2)]

    mine = lax.dynamic_index_in_dim(routes[0], core, 0, keepdims=False)
    give = lax.dynamic_index_in_dim(routes[0], 1 - core, 0, keepdims=False)
    got = swap(give, "pipe")
    picks = [jnp.where(first, mine, got).T, jnp.where(first, got, mine).T]
    half = w_gate.shape[3]
    width = w_out.shape[1]
    mine_w = (w_query[0], key_weight[0], value_weight[0], w_out[0])
    attn_weights = [v for w in mine_w for v in (w, swap(w, "pipe"))]
    small = jnp.concatenate([w_router[0].T, attn_gain, moe_gain], axis=0)
    small_r = swap(small, "pipe")
    smalls = jnp.where(first, small, small_r), jnp.where(first, small_r, small)
    routers = [v[:experts] for v in smalls]
    attn_gains = [v[experts : experts + 1].astype(F32) for v in smalls]
    moe_gains = [v[experts + 1 :].astype(F32) for v in smalls]

    def over(value, layer):
        return lax.ppermute(value, "pipe", [(1 - layer, layer)])

    def across(value, layer):
        pairs = [(2 * layer, 2 * layer + 1), (2 * layer + 1, 2 * layer)]
        return lax.ppermute(value, ("pipe", "tensor"), pairs)

    def by_layer(zero, one):
        own, other = jnp.where(first, zero, one), jnp.where(first, one, zero)
        got = swap(other, "pipe")
        return got, jnp.where(first, jnp.stack([own, got]), jnp.stack([got, own]))

    cosine, sine = rotary_tables(count)
    x_0 = lax.dynamic_index_in_dim(tokens, core, 0, keepdims=False)
    top = lax.dynamic_index_in_dim(cotangent, core, 0, keepdims=False)
    near = (w_gate[0, 0], w_up[0, 0], w_down[0, 0])
    far_0 = [across(near[0], 0)]

    table_0, table_1, top_rows = slot_tables(lane, picks, top, experts, lanes)
    x_0 = after(x_0, table_0)
    branch, *kept_0 = attend_forward(owns[0], x_0, attn_gains[0], cosine, sine, attn_weights)
    branch_r = swap(after(branch, far_0[0]), "tensor")
    far_0 += [across(after(w, branch_r), 0) for w in near[1:]]
    h_0, rows, gated_0, gates_0 = dispatch(
        table_0, picks[0], x_0, branch, branch_r, moe_gains[0], routers[0], lanes, False
    )
    rows_0 = exchange_rows(rows, experts)
    near_r = [swap(after(w, branch_r), "pipe") for w in near]
    far_0r = [over(w, 1) for w in far_0]
    rows_0 = after(rows_0, *near_r, *far_0r)
    far_1 = [across(after(w, rows_0), 1) for w in near[:2]]
    ff_0 = (*near, *near_r, *far_0, *far_0r)
    back_0 = exchange_rows(experts_forward(owns[0], rows_0, ff_0), experts)
    share = after(mul_tn(gated_0, back_0).astype(BF16), *far_1)
    share_r = swap(share, "tensor")
    top_rows = exchange_rows(after(top_rows, share), experts)
    far_1r = [over(after(w, share_r), 0) for w in far_1]

    branch, *kept_1, x_1, y_0 = attend_forward(
        owns[1], (h_0, share, share_r), attn_gains[1], cosine, sine, attn_weights
    )
    branch_r = swap(branch, "tensor")
    far_1 += [across(after(near[2], branch_r), 1)]
    far_1r += [over(far_1[2], 0)]
    h_1, rows, gated_1, gates_1 = dispatch(
        table_1, picks[1], x_1, branch, branch_r, moe_gains[1], routers[1], lanes, True
    )
    rows_1 = exchange_rows(after(rows, top_rows), experts)
    ff_1 = (*near, *near_r, *far_1, *far_1r)
    dx, made, dgu = experts_backward(owns[1], rows_1, top_rows, ff_1)
    dx = exchange_rows(dx, experts)
    both_1, out_rows = experts_grads(owns[1], rows_1, top_rows, made, dgu, ff_1)
    dx = after(dx, both_1)
    share = collect(table_1, dx, experts)
    share_r = swap(share, "tensor")
    back_1 = exchange_rows(after(out_rows, share), experts)
    both_1r = over(after(both_1, share), 1)
    dqkv, da, grad_h, dlogits, gains = attend_backward(
        owns[1], top, h_1, x_1, (share, share_r), gates_1, (),
        routers[1], moe_gains[1], attn_gains[1], kept_1, cosine, sine, attn_weights,
    )
    da_r = swap(after(da, both_1r), "tensor")
    far_sum = both_1[1] + both_1r[1]
    gains_r = swap(gains, "tensor")
    grad_1, grad, rows, seen = turn_over(
        grad_h, x_1, da, after(da_r, back_1, far_sum, gains_r), attn_gains[1], table_0, gated_0, back_0,
        experts,
    )

    grad_rows = exchange_rows(rows, experts)
    far_z = across(after(far_sum, da_r), 1)
    ff_grads_1 = (both_1, both_1r, far_z)
    keep, give = attend_grads(
        owns[1], x_1, h_1, grad_h, kept_1[2], dqkv, dlogits, gains, gains_r,
        attn_gains[1], moe_gains[1],
    )
    seen_r = swap(seen, "tensor")
    grad_rows = after(grad_rows, keep)
    dx, made, dgu = experts_backward(owns[0], rows_0, grad_rows, ff_0)
    half_1 = keep + swap(after(give, dx), "pipe")
    level_1 = background_sum(half_1, 0)
    late = mul_tn(gated_1, after(back_1, dx)).astype(BF16)
    dx = exchange_rows(dx, experts)
    (both_0,) = experts_grads(owns[0], rows_0, grad_rows, made, dgu, ff_0)
    late_r = swap(late, "tensor")
    y_1 = h_1 + (late.astype(F32) + late_r.astype(F32))
    dx = after(dx, both_0, late_r, far_z, half_1, seen_r)
    share = mul_tn(table_0, dx).astype(BF16)
    share_r = swap(share, "tensor")
    level_1 = background_sum(after(level_1, dx), 1)
    both_0r = over(after(both_0, share), 0)
    dqkv, da, grad_h, dlogits, gains = attend_backward(
        owns[0], grad, h_0, x_0, (share, share_r), gates_0, (seen, seen_r),
        routers[0], moe_gains[0], attn_gains[0], kept_0, cosine, sine, attn_weights,
    )
    gains_r = swap(gains, "tensor")
    keep, give = attend_grads(
        owns[0], x_0, h_0, grad_h, kept_0[2], dqkv, dlogits, gains, gains_r,
        attn_gains[0], moe_gains[0],
    )

    cuts = ((0, model * 2 // 3), (model * 2 // 3, model))
    far_sum = [both_0[1, a:b] + both_0r[1, a:b] for a, b in cuts]
    half_0 = after(keep, *far_sum) + swap(give, "pipe")
    da_r = swap(after(da, half_0), "tensor")
    got_y, layer_out = by_layer(y_0, after(y_1, keep))
    level_0 = plane_sum(half_0, 0, da_r, got_y)
    piece_1 = across_planes(after(level_1, level_0))
    sum_1 = gather_plane(piece_1)
    part = plane_copy(plane_sum(level_0, 2), 2)
    far_z = [across(after(v, part), 0) for v in far_sum]
    da = da.astype(F32) + after(da_r, part).astype(F32)
    x_f = x_0.astype(F32)
    grad_0 = grad_h + norm_back(x_f, row_scale_of(x_f), attn_gains[0], da)
    got_g, input_grads = by_layer(grad_0, grad_1)
    ff_grads_0 = (both_0, both_0r, *far_z)
    sum_0 = after(plane_copy(part, 0), far_z[0])
    core_v = core.astype(jnp.int32).reshape(1)
    over_0, over_1 = over(after(sum_0, got_g), 0), over(sum_1, 1)
    query_g, key_g, value_g, out_g, router_g, attn_g, moe_g = attn_total(
        core_v, (sum_0, over_0), (sum_1, over_1), width, model, experts
    )
    gate_g, up_g, down_g = ff_total(after(core_v, moe_g), ff_grads_0, ff_grads_1)
    return (
        layer_out[None],
        input_grads[None],
        attn_g,
        query_g[None],
        key_g[None],
        value_g[None],
        out_g[None],
        moe_g,
        router_g.T[None],
        gate_g[None, None],
        up_g[None, None],
        down_g[None, None],
    )


def solution(mesh):
    layered = P("pipe", None, "expert", None)
    by_expert = P("pipe", "expert", None, "tensor")
    columns = P("pipe", None, "tensor")
    rows = P("pipe", "tensor", None)
    down = P("pipe", "expert", "tensor", None)
    whole = P("pipe", None)
    router = P("pipe", None, None)
    tokens = P(None, "expert", None)
    return jax.shard_map(
        on_device,
        mesh=mesh,
        in_specs=(
            tokens,
            tokens,
            layered,
            whole,
            columns,
            columns,
            columns,
            rows,
            whole,
            router,
            by_expert,
            by_expert,
            down,
        ),
        out_specs=(
            layered,
            layered,
            whole,
            columns,
            columns,
            columns,
            rows,
            whole,
            router,
            by_expert,
            by_expert,
            down,
        ),
        check_vma=False,
    )
```

```python
import jax
import jax.numpy as jnp
from jax import lax
from jax.experimental import pallas as pl
from jax.experimental.pallas import tpu as pltpu
from jax.sharding import PartitionSpec as P

HEAD = 128
NORM_EPS = 1e-06
ROPE_BASE = 10000.0
BF16 = jnp.bfloat16
F32 = jnp.float32
SWAP = [(0, 1), (1, 0)]
VMEM_LIMIT = 52 * 1024 * 1024


def swap(value, axis):
    return lax.ppermute(value, axis, SWAP)


def slot_groups(experts):
    return [[e * 2 + ((e % 2) ^ s) for e in range(experts)] for s in range(2)]


def expert_exchange(value):
    return lax.all_to_all(
        value,
        ("expert", "tensor"),
        split_axis=0,
        concat_axis=0,
        axis_index_groups=slot_groups(value.shape[0]),
        tiled=True,
    )


def plane_groups(level):
    groups = []
    if level < 2:
        for z in range(2):
            for i in range(4):
                along_y = [(y * 4 + i) * 2 + z for y in range(4)]
                along_x = [(i * 4 + x) * 2 + z for x in range(4)]
                zero, one = (along_y, along_x) if level == 0 else (along_x, along_y)
                groups += [zero, [32 + e for e in one]]
    else:
        for i in range(4):
            along_x = [(i * 4 + x) * 2 + z for x in range(4) for z in range(2)]
            along_y = [(y * 4 + i) * 2 + z for y in range(4) for z in range(2)]
            groups += [along_x, [32 + e for e in along_y]]
    return groups


def mul(left, right, dims):
    return lax.dot_general(left, right, (dims, ((), ())), preferred_element_type=F32)


def mul_nn(left, right):
    return mul(left, right, ((1,), (0,)))


def mul_nt(left, right):
    return mul(left, right, ((1,), (1,)))


def mul_tn(left, right):
    return mul(left, right, ((0,), (0,)))


VMEM = pl.BlockSpec(memory_space=pltpu.VMEM)
SMEM = pl.BlockSpec(memory_space=pltpu.SMEM)
ANY = pl.BlockSpec(memory_space=pl.ANY)
HBM = pl.BlockSpec(memory_space=pltpu.HBM)


def call(body, outs, in_specs, scratch, operands, name, spaces=None, aliases=None):
    return pl.pallas_call(
        body,
        out_shape=[jax.ShapeDtypeStruct(shape, kind) for shape, kind in outs],
        in_specs=in_specs,
        out_specs=spaces or [VMEM] * len(outs),
        scratch_shapes=scratch,
        input_output_aliases=aliases or {},
        compiler_params=pltpu.CompilerParams(vmem_limit_bytes=VMEM_LIMIT),
        cost_estimate=pl.CostEstimate(flops=1024, bytes_accessed=1024, transcendentals=0),
        name=name,
    )(*operands)


def fetch(own, mine, theirs, target, sem):
    @pl.when(own == 1)
    def _():
        pltpu.make_async_copy(mine, target, sem).start()

    @pl.when(own != 1)
    def _():
        pltpu.make_async_copy(theirs, target, sem).start()


def arrive(mine, target, sem):
    pltpu.make_async_copy(mine, target, sem).wait()


def rotary_tables(count):
    half = HEAD // 2
    frequency = ROPE_BASE ** (-(jnp.arange(half, dtype=F32) * 2.0) / HEAD)
    angles = jnp.arange(count, dtype=F32)[:, None] * frequency[None, :]
    cosine = jnp.concatenate([jnp.cos(angles), jnp.cos(angles)], axis=1)
    sine = jnp.concatenate([-jnp.sin(angles), jnp.sin(angles)], axis=1)
    return cosine, sine


def turn(vector, cosine, sine):
    return vector * cosine + pltpu.roll(vector, HEAD // 2, 1) * sine


def turn_back(grad, cosine, sine):
    return grad * cosine - pltpu.roll(grad, HEAD // 2, 1) * sine


def row_scale_of(rows):
    return lax.rsqrt(jnp.mean(rows * rows, axis=-1, keepdims=True) + NORM_EPS)


def norm_back(rows, scale, gain, grad):
    scaled = grad * gain
    return scale * scaled - rows * (scale * scale * scale) * jnp.mean(
        scaled * rows, axis=-1, keepdims=True
    )


def attention_weights(q, k):
    count = q.shape[0]
    scores = mul_nt(q, k)
    row = lax.broadcasted_iota(jnp.int32, (count, count), 0)
    column = lax.broadcasted_iota(jnp.int32, (count, count), 1)
    scores = jnp.where(row >= column, scores, -1e30)
    raised = jnp.exp(scores - jnp.max(scores, axis=-1, keepdims=True))
    return raised / jnp.sum(raised, axis=-1, keepdims=True)


def head_of(index):
    return slice(index * HEAD, (index + 1) * HEAD)


def attend_body(own, x_ref, h_ref, a_ref, b_ref, gain, cos, sin, refs, outs, scratch):
    (wq, wq_r, wk, wk_r, wv, wv_r, wo, wo_r) = refs
    (qkv_s, wo_s, sems) = scratch
    (branch, q_o, kv_o, o_o, x_o, y_o) = outs
    mine = own[0]
    width = wo.shape[0]
    heads = width // HEAD
    kv_at = width + HEAD
    moves = [
        (wq, wq_r, qkv_s.at[:, :width]),
        (wk, wk_r, qkv_s.at[:, width:kv_at]),
        (wv, wv_r, qkv_s.at[:, kv_at:]),
        (wo, wo_r, wo_s),
    ]
    for i, (a, b, target) in enumerate(moves):
        fetch(mine, a, b, target, sems.at[i])
    if h_ref is None:
        x = x_ref[...].astype(F32)
    else:
        y = h_ref[...] + (a_ref[...].astype(F32) + b_ref[...].astype(F32))
        y_o[...] = y
        x_o[...] = y.astype(BF16)
        x = y.astype(BF16).astype(F32)
    normed = (x * row_scale_of(x) * gain[...]).astype(BF16)
    cosine, sine = cos[...], sin[...]
    for i in range(3):
        arrive(moves[i][0], moves[i][2], sems.at[i])
    made = mul_nn(normed, qkv_s[...])
    k = turn(made[:, width : width + HEAD], cosine, sine).astype(BF16)
    v = made[:, width + HEAD :].astype(BF16)
    kv_o[:, :HEAD] = k
    kv_o[:, HEAD:] = v
    for i in range(heads):
        q = (turn(made[:, head_of(i)], cosine, sine) * HEAD**-0.5).astype(BF16)
        q_o[:, head_of(i)] = q
        weights = attention_weights(q, k)
        o_o[:, head_of(i)] = mul_nn(weights.astype(BF16), v).astype(BF16)
    arrive(wo, wo_s, sems.at[3])
    branch[...] = mul_nn(o_o[...], wo_s[...]).astype(BF16)


def attend_forward(own, source, gain, cosine, sine, weights):
    later = isinstance(source, tuple)
    count = cosine.shape[0]
    width, model = weights[6].shape

    def body(own_ref, *refs):
        if later:
            h_ref, a_ref, b_ref, gain_ref, cos, sin = refs[:6]
            x_ref, rest = None, refs[6:]
        else:
            x_ref, gain_ref, cos, sin = refs[:4]
            h_ref, a_ref, b_ref, rest = None, None, None, refs[4:]
        ws, rest = rest[:8], rest[8:]
        outs, scratch = (rest[:6], rest[6:]) if later else (rest[:4] + (None, None), rest[4:])
        attend_body(
            own_ref, x_ref, h_ref, a_ref, b_ref, gain_ref, cos, sin, ws, outs, scratch
        )

    outs = [
        ((count, model), BF16),
        ((count, width), BF16),
        ((count, 2 * HEAD), BF16),
        ((count, width), BF16),
    ]
    if later:
        outs += [((count, model), BF16), ((count, model), F32)]
    values = source if later else (source,)
    return call(
        body,
        outs,
        [SMEM] + [VMEM] * (len(values) + 3) + [ANY] * 8,
        [
            pltpu.VMEM((model, width + 2 * HEAD), BF16),
            pltpu.VMEM((width, model), BF16),
            pltpu.SemaphoreType.DMA((4,)),
        ],
        (own, *values, gain, cosine, sine, *weights),
        "attend_forward",
    )


def hot_of(routes_ref, experts):
    count = routes_ref.shape[1]
    names = lax.broadcasted_iota(jnp.int32, (experts, count), 0)
    hot = routes_ref[0:1, :] == names
    for pick in range(1, routes_ref.shape[0]):
        hot = hot | (routes_ref[pick : pick + 1, :] == names)
    return hot


def slot_tables(lane, routes, top, experts, lanes):
    count, model = top.shape
    slots = experts * lanes

    def body(lane_ref, first_ref, second_ref, top_ref, first_o, second_o, rows_o):
        row = lax.broadcasted_iota(jnp.int32, (count, count), 0)
        column = lax.broadcasted_iota(jnp.int32, (count, count), 1)
        before = jnp.where(row < column, 1.0, 0.0).astype(BF16)
        place = lax.broadcasted_iota(jnp.int32, (lanes, count), 0).astype(F32)
        start = (lane_ref[0] * lanes).astype(F32)
        for routes_ref, out in ((first_ref, first_o), (second_ref, second_o)):
            hot = hot_of(routes_ref, experts)
            rank = mul_nn(jnp.where(hot, 1.0, 0.0).astype(BF16), before)
            rank = jnp.where(hot, rank, -1.0) - start
            for e in range(experts):
                chosen = jnp.where(rank[e : e + 1, :] == place, 1.0, 0.0)
                out[e * lanes : (e + 1) * lanes, :] = chosen.astype(BF16)
        rows_o[...] = mul_nn(second_o[...], top_ref[...].astype(BF16)).astype(BF16)

    return call(
        body,
        [((slots, count), BF16), ((slots, count), BF16), ((slots, model), BF16)],
        [SMEM] + [VMEM] * 3,
        [],
        (lane, *routes, top),
        "slot_tables",
    )


def pair_columns(value, count):
    high = value.astype(BF16).astype(F32)
    lanes = lax.broadcasted_iota(jnp.int32, (count, HEAD), 1)
    both = jnp.where(lanes == 0, high, jnp.where(lanes == 1, value - high, 0.0))
    return both.astype(BF16)


def dispatch(table, routes, x, own, received, gain, router, lanes, with_gates):
    count, model = x.shape
    experts = router.shape[0]
    slots = experts * lanes
    wide = model + HEAD if with_gates else model

    def body(table_ref, routes_ref, x_ref, a_ref, b_ref, gain_ref, router_ref, *outs):
        h_o, rows_o, gated_o, gates_o = outs
        h = x_ref[...].astype(F32) + (a_ref[...].astype(F32) + b_ref[...].astype(F32))
        h_o[...] = h
        normed = (h * row_scale_of(h) * gain_ref[...]).astype(BF16)
        rows_o[:, :model] = mul_nn(table_ref[...], normed).astype(BF16)
        hot = hot_of(routes_ref, experts)
        logits = jnp.where(hot, mul_nt(router_ref[...], normed), -1e30)
        raised = jnp.where(hot, jnp.exp(logits - jnp.max(logits, axis=0, keepdims=True)), 0.0)
        gates = raised / jnp.sum(raised, axis=0, keepdims=True)
        gates_o[...] = gates
        for e in range(experts):
            spot = slice(e * lanes, (e + 1) * lanes)
            gated = table_ref[spot, :].astype(F32) * gates[e : e + 1, :]
            gated_o[spot, :] = gated.astype(BF16)
            if with_gates:
                total = jnp.sum(gated, axis=1, keepdims=True)
                rows_o[spot, model:] = pair_columns(total, lanes)

    return call(
        body,
        [
            ((count, model), F32),
            ((slots, wide), BF16),
            ((slots, count), BF16),
            ((experts, count), F32),
        ],
        [VMEM] * 7,
        [],
        (table, routes, x, own, received, gain, router),
        "dispatch",
    )


def collect(table, back, experts):
    slots, count = table.shape
    lanes = slots // experts
    model = back.shape[1] - HEAD

    def body(table_ref, back_ref, share_o, seen_s):
        share_o[:, :model] = mul_tn(table_ref[...], back_ref[:, :model]).astype(BF16)
        value = back_ref[:, model:].astype(F32)
        value = value[:, 0:1] + value[:, 1:2]
        seen_s[...] = jnp.zeros_like(seen_s)
        for e in range(experts):
            spot = slice(e * lanes, (e + 1) * lanes)
            part = table_ref[spot, :].astype(F32) * value[spot, :]
            seen_s[e : e + 1, :] = jnp.sum(part, axis=0, keepdims=True)
        seen = seen_s[:experts, :]
        high = seen.astype(BF16).astype(F32)
        seen_s[experts : 2 * experts, :] = seen - high
        seen_s[:experts, :] = high
        share_o[:, model:] = seen_s[...].T.astype(BF16)

    return call(
        body,
        [((count, model + HEAD), BF16)],
        [VMEM] * 2,
        [pltpu.VMEM((HEAD, count), F32)],
        (table, back),
        "collect",
    )[0]


def turn_over(grad, x, own, received, gain, gated):
    slots, count = gated.shape
    model = x.shape[1]

    def body(g_ref, x_ref, a_ref, b_ref, gain_ref, gated_ref, grad_o, low_o, rows_o):
        x_v = x_ref[...].astype(F32)
        da = a_ref[...].astype(F32) + b_ref[...].astype(F32)
        total = g_ref[...] + norm_back(x_v, row_scale_of(x_v), gain_ref[...], da)
        grad_o[...] = total
        low = total.astype(BF16)
        low_o[...] = low
        rows_o[...] = mul_nn(gated_ref[...], low).astype(BF16)

    return call(
        body,
        [((count, model), F32), ((count, model), BF16), ((slots, model), BF16)],
        [VMEM] * 6,
        [],
        (grad, x, own, received, gain, gated),
        "turn_over",
    )


def gates_seen(back, low, table, experts):
    slots, count = table.shape
    lanes = slots // experts

    def body(back_ref, low_ref, table_ref, seen_o):
        seen = mul_nt(back_ref[...], low_ref[...]) * table_ref[...].astype(F32)
        for e in range(experts):
            spot = slice(e * lanes, (e + 1) * lanes)
            seen_o[e : e + 1, :] = jnp.sum(seen[spot, :], axis=0, keepdims=True)

    return call(
        body, [((experts, count), F32)], [VMEM] * 3, [], (back, low, table), "gates_seen"
    )[0]


def expert_sources(refs, half):
    if len(refs) == 12:
        return refs
    far, far_r = refs[6], refs[8]
    columns = (slice(0, half), slice(half, 2 * half))
    return (
        *refs[:6],
        *[far.at[:, spot] for spot in columns],
        refs[7],
        *[far_r.at[:, spot] for spot in columns],
        refs[9],
    )


def expert_moves(sources, wgu, wd, half):
    hidden = 2 * half
    targets = (wgu.at[:, :half], wgu.at[:, hidden : hidden + half], wd.at[:half, :])
    targets += (wgu.at[:, half:hidden], wgu.at[:, hidden + half :], wd.at[half:, :])
    return [(sources[i], sources[i + 3], t) for i, t in zip((0, 1, 2, 6, 7, 8), targets)]


def experts_forward(own, rows, weights):
    slots, model = rows.shape
    half = weights[0].shape[1]
    hidden = 2 * half
    tile = 256

    def body(own_ref, x_ref, *refs):
        sources, (y_o, x_s, wgu, wd, h_s, sems) = refs[:12], refs[12:]
        moves = expert_moves(sources, wgu, wd, half)
        arrival = pltpu.make_async_copy(x_ref, x_s, sems.at[6])
        arrival.start()
        for i in (0, 1, 3, 4, 2, 5):
            fetch(own_ref[0], moves[i][0], moves[i][1], moves[i][2], sems.at[i])
        arrival.wait()
        for i in (0, 1):
            arrive(moves[i][0], moves[i][2], sems.at[i])

        def step(c, carry):
            @pl.when(c == 1)
            def _():
                for i in (3, 4):
                    arrive(moves[i][0], moves[i][2], sems.at[i])

            at = pl.multiple_of(c * tile, tile)
            gate = mul_nn(x_s[...], wgu[:, pl.ds(at, tile)])
            up = mul_nn(x_s[...], wgu[:, pl.ds(at + hidden, tile)])
            act = gate / (1.0 + jnp.exp(-gate))
            h_s[:, pl.ds(at, tile)] = (act * up).astype(BF16)
            return carry

        lax.fori_loop(0, hidden // tile, step, 0)
        for i in (2, 5):
            arrive(moves[i][0], moves[i][2], sems.at[i])

        def finish(c, carry):
            spot = pl.ds(pl.multiple_of(c * tile, tile), tile)
            y_o[:, spot] = mul_nn(h_s[...], wd[:, spot]).astype(BF16)
            return carry

        lax.fori_loop(0, model // tile, finish, 0)

    return call(
        body,
        [((slots, model), BF16)],
        [SMEM] + [ANY] * 13,
        [
            pltpu.VMEM((slots, model), BF16),
            pltpu.VMEM((model, 2 * hidden), BF16),
            pltpu.VMEM((hidden, model), BF16),
            pltpu.VMEM((slots, hidden), BF16),
            pltpu.SemaphoreType.DMA((7,)),
        ],
        (own, rows, *weights),
        "experts_forward",
    )[0]


def experts_backward(own, rows, grads, weights):
    slots, wide = rows.shape
    model, half = weights[0].shape
    hidden = 2 * half
    gated = wide > model
    tile = 256

    def body(own_ref, x_ref, g_ref, *refs):
        sources, refs = expert_sources(refs[: len(weights)], half), refs[len(weights) :]
        dx_o, h_o, dgu_o, x_s, g_s, h_s, dgu_s, wgu, wd, sems = refs[:10]
        moves = expert_moves(sources, wgu, wd, half)
        arrivals = [
            pltpu.make_async_copy(x_ref, x_s, sems.at[6]),
            pltpu.make_async_copy(g_ref, g_s, sems.at[7]),
        ]
        leaving = [
            pltpu.make_async_copy(h_s, h_o, sems.at[8]),
            pltpu.make_async_copy(dgu_s, dgu_o, sems.at[9]),
        ]
        arrivals[0].start()
        for i in (0, 1, 2, 3, 4, 5):
            fetch(own_ref[0], moves[i][0], moves[i][1], moves[i][2], sems.at[i])
            if i == 1:
                arrivals[1].start()
        arrivals[0].wait()
        if gated:
            scale = x_s[:, model:].astype(F32)
            scale = scale[:, 0:1] + scale[:, 1:2]
            seen_s = refs[10]
            seen_s[...] = jnp.zeros_like(seen_s)
        for i in (0, 1):
            arrive(moves[i][0], moves[i][2], sems.at[i])
        arrivals[1].wait()
        arrive(moves[2][0], moves[2][2], sems.at[2])

        def step(c, carry):
            @pl.when(c == 1)
            def _():
                for i in (3, 4, 5):
                    arrive(moves[i][0], moves[i][2], sems.at[i])

            at = pl.multiple_of(c * tile, tile)
            spot, later = pl.ds(at, tile), pl.ds(at + hidden, tile)
            gate = mul_nn(x_s[:, :model], wgu[:, spot])
            up = mul_nn(x_s[:, :model], wgu[:, later])
            sig = 1.0 / (1.0 + jnp.exp(-gate))
            act = gate * sig
            made = act * up
            h_s[:, spot] = made.astype(BF16)
            grad_hidden = mul_nt(g_s[...], wd[spot, :])
            if gated:
                seen = made * grad_hidden
                seen_s[...] += seen[:, :HEAD] + seen[:, HEAD:]
                grad_hidden = grad_hidden * scale
            dgu_s[:, spot] = (grad_hidden * up * sig * (1.0 + gate * (1.0 - sig))).astype(BF16)
            dgu_s[:, later] = (grad_hidden * act).astype(BF16)
            return carry

        lax.fori_loop(0, hidden // tile, step, 0)
        for copy in leaving:
            copy.start()

        def finish(c, carry):
            spot = pl.ds(pl.multiple_of(c * tile, tile), tile)
            dx_o[:, spot] = mul_nt(dgu_s[...], wgu[spot, :]).astype(BF16)
            return carry

        lax.fori_loop(0, model // tile, finish, 0)
        if gated:
            total = jnp.sum(seen_s[...], axis=1, keepdims=True)
            dx_o[:, model:] = pair_columns(total, slots)
        for copy in leaving:
            copy.wait()

    return call(
        body,
        [((slots, wide), BF16), ((slots, hidden), BF16), ((slots, 2 * hidden), BF16)],
        [SMEM] + [ANY] * (2 + len(weights)),
        [
            pltpu.VMEM((slots, wide), BF16),
            pltpu.VMEM((slots, model), BF16),
            pltpu.VMEM((slots, hidden), BF16),
            pltpu.VMEM((slots, 2 * hidden), BF16),
            pltpu.VMEM((model, 2 * hidden), BF16),
            pltpu.VMEM((hidden, model), BF16),
            pltpu.SemaphoreType.DMA((10,)),
        ]
        + ([pltpu.VMEM((slots, HEAD), F32)] if gated else []),
        (own, rows, grads, *weights),
        "experts_backward",
        [VMEM, ANY, ANY],
    )


def experts_grads(own, rows, grads, hidden_rows, dgu, weights):
    slots, wide = rows.shape
    model, half = weights[0].shape
    hidden = 2 * half
    blocks = model // half
    gated = wide > model
    tile = 256

    def body(own_ref, x_in, g_in, h_in, dgu_in, *refs):
        sources, refs = refs[:4], refs[4:]
        both_o, refs = refs[0], refs[1:]
        x_ref, g_ref, h_ref, dgu_ref, load = refs[-5:]
        refs = refs[:-5]
        loads = [
            pltpu.make_async_copy(a, b, load.at[i])
            for i, (a, b) in enumerate(
                ((x_in, x_ref), (dgu_in, dgu_ref), (g_in, g_ref), (h_in, h_ref))
            )
        ]
        for copy in loads:
            copy.start()
        if gated:
            y_o, xt_s, dy_s, wd, sems = refs
            moves = [
                (sources[0], sources[1], wd.at[:half, :]),
                (sources[2], sources[3], wd.at[half:, :]),
            ]
            for i, (a, b, target) in enumerate(moves):
                fetch(own_ref[0], a, b, target, sems.at[i])
            loads[0].wait()
            scale = x_ref[:, model:].astype(F32)
            scale = scale[:, 0:1] + scale[:, 1:2]
        else:
            (xt_s,), dy_s = refs, g_ref
            loads[0].wait()
        for i in range(model // tile):
            xt_s[i * tile : (i + 1) * tile, :] = x_ref[:, i * tile : (i + 1) * tile].T
        for copy in loads[1:]:
            copy.wait()
        if gated:
            dy_s[...] = (g_ref[...].astype(F32) * scale).astype(BF16)
            for i, (a, b, target) in enumerate(moves):
                arrive(a, target, sems.at[i])

        def step(c, carry):
            spot = pl.ds(pl.multiple_of(c * tile, tile), tile)
            made = mul_nn(xt_s[spot, :], dgu_ref[...]).astype(BF16)
            both_o[0, spot, :half] = made[:, :half]
            both_o[1, spot, :half] = made[:, half:hidden]
            both_o[0, spot, half:hidden] = made[:, hidden : hidden + half]
            both_o[1, spot, half:hidden] = made[:, hidden + half :]
            if gated:
                y_o[:, spot] = mul_nn(h_ref[...], wd[:, spot]).astype(BF16)
            return carry

        lax.fori_loop(0, model // tile, step, 0)
        down = tile // 2
        for i in range(hidden // down):
            made = mul_tn(h_ref[:, i * down : (i + 1) * down], dy_s[...]).astype(BF16)
            low = i * down
            side, low = (0, low) if low < half else (1, low - half)
            for j in range(blocks):
                at = j * half + low
                both_o[side, at : at + down, hidden:] = made[:, j * half : (j + 1) * half]

    outs = [((2, model, 3 * half), BF16)]
    scratch = [pltpu.VMEM((model, slots), BF16)]
    if gated:
        outs = outs + [((slots, model), BF16)]
        scratch += [
            pltpu.VMEM((slots, model), BF16),
            pltpu.VMEM((hidden, model), BF16),
            pltpu.SemaphoreType.DMA((2,)),
        ]
    scratch += [
        pltpu.VMEM((slots, wide), BF16),
        pltpu.VMEM((slots, model), BF16),
        pltpu.VMEM((slots, hidden), BF16),
        pltpu.VMEM((slots, 2 * hidden), BF16),
        pltpu.SemaphoreType.DMA((4,)),
    ]
    return call(
        body,
        outs,
        [SMEM] + [ANY] * 8,
        scratch,
        (own, rows, grads, hidden_rows, dgu, *[weights[i] for i in (2, 5, -(len(weights) // 6) - 2, -1)]),
        "experts_grads",
    )


def attend_backward(
    own, grad, h, x, shares, gates, seen, router, moe_gain, attn_gain, kept, cosine, sine, weights
):
    count, model = h.shape
    width = weights[6].shape[0]
    heads = width // HEAD
    experts = router.shape[0]
    kv_at, out_at = width + HEAD, width + 2 * HEAD
    riding = len(seen) == 0

    def body(own_ref, *refs):
        (g_ref, h_ref, x_ref, a_ref, b_ref, gates_ref) = refs[:6]
        refs = refs[6:]
        if riding:
            tail = a_ref[:, model:].astype(F32) + b_ref[:, model:].astype(F32)
            tail = tail.T
            grad_gates = tail[:experts, :] + tail[experts : 2 * experts, :]
        else:
            grad_gates = refs[0][...] + refs[1][...]
            refs = refs[2:]
        (router_ref, mgain_ref, again_ref, q_ref, kv_ref, cos, sin) = refs[:7]
        (wq, wq_r, wk, wk_r, wv, wv_r, wo, wo_r) = refs[7:15]
        (dqkv_o, da_o, gh_o, dlogits_o, gains_o) = refs[15:20]
        (qkv_s, wo_s, sems) = refs[20:]
        mine = own_ref[0]
        moves = [
            (wo, wo_r, wo_s),
            (wq, wq_r, qkv_s.at[:, :width]),
            (wk, wk_r, qkv_s.at[:, width:kv_at]),
            (wv, wv_r, qkv_s.at[:, kv_at:]),
        ]
        for i, (a, b, target) in enumerate(moves):
            fetch(mine, a, b, target, sems.at[i])
        gates_v = gates_ref[...]
        dlogits = gates_v * (grad_gates - jnp.sum(gates_v * grad_gates, axis=0, keepdims=True))
        dlogits = dlogits.astype(BF16)
        dlogits_o[...] = dlogits
        dn = a_ref[:, :model].astype(F32) + b_ref[:, :model].astype(F32)
        dn = dn + mul_tn(dlogits, router_ref[...])
        hv = h_ref[...]
        scale = row_scale_of(hv)
        gh = g_ref[...].astype(F32) + norm_back(hv, scale, mgain_ref[...], dn)
        gh_o[...] = gh
        moe_part = jnp.sum(dn * hv * scale, axis=0, keepdims=True)
        dz = gh.astype(BF16)
        arrive(wo, wo_s, sems.at[0])
        do = mul_nt(dz, wo_s[...]).astype(BF16)
        cosine_v, sine_v = cos[...], sin[...]
        k, v = kv_ref[:, :HEAD], kv_ref[:, HEAD:]
        dk, dv = 0.0, 0.0
        for i in range(heads):
            q = q_ref[:, head_of(i)]
            p = attention_weights(q, k)
            do_i = do[:, head_of(i)]
            dp = mul_nt(do_i, v)
            ds = (p * (dp - jnp.sum(p * dp, axis=-1, keepdims=True))).astype(BF16)
            dv = dv + mul_tn(p.astype(BF16), do_i)
            dk = dk + mul_tn(ds, q)
            dq = turn_back(mul_nn(ds, k), cosine_v, sine_v) * HEAD**-0.5
            dqkv_o[:, head_of(i)] = dq.astype(BF16)
        dqkv_o[:, width:kv_at] = turn_back(dk, cosine_v, sine_v).astype(BF16)
        dqkv_o[:, kv_at:] = dv.astype(BF16)
        for i in range(1, 4):
            arrive(moves[i][0], moves[i][2], sems.at[i])
        da = mul_nt(dqkv_o[...], qkv_s[...])
        da_o[...] = da.astype(BF16)
        xv = x_ref[...].astype(F32)
        attn_part = jnp.sum(da * xv * row_scale_of(xv), axis=0, keepdims=True)
        lane = lax.broadcasted_iota(jnp.int32, (16, model), 0)
        total = jnp.zeros((16, model), F32)
        for i, value in enumerate((attn_part, moe_part)):
            high = value.astype(BF16).astype(F32)
            total = jnp.where(lane == 2 * i, high, total)
            total = jnp.where(lane == 2 * i + 1, value - high, total)
        gains_o[...] = total.astype(BF16)

    q, kv, _ = kept
    operands = (own, grad, h, x, *shares, gates, *seen, router, moe_gain, attn_gain)
    operands += (q, kv, cosine, sine)
    return call(
        body,
        [
            ((count, out_at), BF16),
            ((count, model), BF16),
            ((count, model), F32),
            ((experts, count), BF16),
            ((16, model), BF16),
        ],
        [SMEM] + [VMEM] * (len(operands) - 1) + [ANY] * 8,
        [
            pltpu.VMEM((model, out_at), BF16),
            pltpu.VMEM((width, model), BF16),
            pltpu.SemaphoreType.DMA((4,)),
        ],
        (*operands, *weights),
        "attend_backward",
    )


def attend_grads(own, x, h, grad_h, o, dqkv, dlogits, gains, gains_r, attn_gain, moe_gain):
    count, model = h.shape
    width, out_at = o.shape[1], dqkv.shape[1]
    experts = dlogits.shape[0]
    side_at = out_at + model // 2
    tile = 256
    parts = model // tile // 2

    def body(own_ref, x_ref, h_ref, gh_ref, o_ref, dqkv_ref, dl_ref, *rest):
        gains_ref, far_ref, again, mgain, *rest = rest
        keep_o, give_o, left_s, pack_s, sems = rest
        xv = x_ref[...].astype(F32)
        normed = (xv * row_scale_of(xv) * again[...]).astype(BF16)
        for i in range(model // tile):
            left_s[i * tile : (i + 1) * tile, :] = normed[:, i * tile : (i + 1) * tile].T
        hv = h_ref[...]
        normed_m = (hv * row_scale_of(hv) * mgain[...]).astype(BF16)
        dz = gh_ref[...].astype(BF16)
        row = lax.broadcasted_iota(jnp.int32, (experts, HEAD), 0)
        column = lax.broadcasted_iota(jnp.int32, (experts, HEAD), 1)
        spread_logits = mul_tn(dl_ref[...], jnp.where(row == column, 1.0, 0.0).astype(BF16))
        spread_logits = spread_logits.astype(BF16)
        row = lax.broadcasted_iota(jnp.int32, (16, HEAD), 0)
        column = lax.broadcasted_iota(jnp.int32, (16, HEAD), 1)
        hit = (column == experts + row // 2) & (row < 4)
        marks = jnp.where(hit, 1.0, 0.0).astype(BF16)
        far_marks = jnp.where(hit & (row < 2), 1.0, 0.0).astype(BF16)

        def step(c, carry):
            spot = pl.ds(pl.multiple_of(c * tile, tile), tile)
            target = pl.ds(pl.multiple_of(lax.rem(c, parts) * tile, tile), tile)
            made = mul_nn(left_s[spot, :], dqkv_ref[...]).astype(BF16)
            pack_s[lax.div(c, parts), target, :out_at] = made
            return carry

        lax.fori_loop(0, model // tile, step, 0)
        for i in range(width // HEAD):
            made = mul_tn(o_ref[:, head_of(i)], dz).astype(BF16)
            spot = slice(i * HEAD, (i + 1) * HEAD)
            pack_s[0, spot, out_at:side_at] = made[:, : model // 2]
            pack_s[1, spot, out_at:side_at] = made[:, model // 2 :]
        for i in range(model // tile):
            spot = slice(i * tile, (i + 1) * tile)
            total = mul_tn(normed_m[:, spot], spread_logits)
            total = total + mul_tn(gains_ref[:, spot], marks)
            total = total + mul_tn(far_ref[:, spot], far_marks)
            at = (i % parts) * tile
            pack_s[i // parts, at : at + tile, side_at:] = total.astype(BF16)
        kept = 1 - own_ref[0]
        copies = [
            pltpu.make_async_copy(pack_s.at[kept], keep_o, sems.at[0]),
            pltpu.make_async_copy(pack_s.at[1 - kept], give_o, sems.at[1]),
        ]
        for copy in copies:
            copy.start()
        for copy in copies:
            copy.wait()

    return call(
        body,
        [((model // 2, side_at + HEAD), BF16)] * 2,
        [SMEM] + [VMEM] * 10,
        [
            pltpu.VMEM((model, count), BF16),
            pltpu.VMEM((2, model // 2, side_at + HEAD), BF16),
            pltpu.SemaphoreType.DMA((2,)),
        ],
        (own, x, h, grad_h, o, dqkv, dlogits, gains, gains_r, attn_gain, moe_gain),
        "attend_grads",
        [ANY, ANY],
    )


def move_all(pairs, sems, first):
    copies = [pltpu.make_async_copy(a, b, sems.at[first + i]) for i, (a, b) in enumerate(pairs)]
    for copy in copies:
        copy.start()
    return copies


def ff_total(core, which, zero, one, done):
    _, model, wide = zero[0].shape
    half = wide // 3
    rows = model // 2
    low = which * rows
    pieces = rows // half

    given = len(zero) + len(one)

    def body(core_ref, *refs):
        ins = (refs[: len(zero)], refs[len(zero) : given])
        outs = refs[given + len(done) : given + len(done) + 3]
        held, gate_s, up_s, down_s, sems = refs[given + len(done) + 3 :]
        spot = slice(low, low + rows)
        for number in range(2):
            near, near_r = ins[number][:2]
            pairs = [(near.at[0, spot], held.at[0]), (near_r.at[0, spot], held.at[1])]
            start = 0
            for z in ins[number][2:]:
                stop = start + z.shape[0]
                a, b = max(start, low), min(stop, low + rows)
                if a < b:
                    pairs.append((z.at[a - start : b - start], held.at[2, a - low : b - low]))
                start = stop

            @pl.when(core_ref[0] == number)
            def _(pairs=pairs):
                for copy in move_all(pairs, sems, 0):
                    copy.wait()

        def total(at, columns):
            return (
                held[0, at, columns].astype(F32)
                + held[1, at, columns].astype(F32)
                + held[2, at, columns].astype(F32)
            )

        gate_s[...] = total(slice(0, rows), slice(0, half))
        up_s[...] = total(slice(0, rows), slice(half, 2 * half))
        for i in range(pieces):
            at = slice(i * half, (i + 1) * half)
            down_s[:, at] = total(at, slice(2 * half, wide))
        pairs = (
            (gate_s, outs[0].at[spot]),
            (up_s, outs[1].at[spot]),
            (down_s, outs[2].at[:, spot]),
        )
        for copy in move_all(pairs, sems, 4):
            copy.wait()

    return call(
        body,
        [((model, half), F32), ((model, half), F32), ((half, model), F32)],
        [SMEM] + [HBM] * (given + len(done)),
        [
            pltpu.VMEM((3, rows, wide), BF16),
            pltpu.VMEM((rows, half), F32),
            pltpu.VMEM((rows, half), F32),
            pltpu.VMEM((half, rows), F32),
            pltpu.SemaphoreType.DMA((7,)),
        ],
        (core, *zero, *one, *done),
        "ff_total",
        [HBM] * 3,
        {1 + given + i: i for i in range(len(done))},
    )


def attn_total(core, which, zero, one, done, width, model, experts):
    rows, wide = zero.shape
    out_at = width + 2 * HEAD
    side_at = out_at + model // 2
    mixed = which == 0

    def body(core_ref, zero_ref, one_ref, *refs):
        outs = refs[len(done) : len(done) + 7]
        held, query, key, value, out, router, gains, sems = refs[len(done) + 7 :]
        piece = rows // 16

        @pl.when(core_ref[0] == 1)
        def _():
            if mixed:
                for y in range(4):
                    for x in range(4):
                        source = one_ref.at[(y * 4 + x) * piece : (y * 4 + x + 1) * piece]
                        target = held.at[(x * 4 + y) * piece : (x * 4 + y + 1) * piece]
                        pltpu.make_async_copy(source, target, sems.at[0]).start()
            else:
                pltpu.make_async_copy(one_ref, held, sems.at[0]).start()

        @pl.when(core_ref[0] != 1)
        def _():
            pltpu.make_async_copy(zero_ref, held, sems.at[0]).start()

        pltpu.make_async_copy(zero_ref, held, sems.at[0]).wait()
        spot = slice(which * rows, (which + 1) * rows)
        query[...] = held[:, :width].astype(F32)
        copies = move_all([(query, outs[0].at[spot])], sems, 1)
        out[...] = held[:, out_at:side_at].astype(F32)
        copies += move_all([(out, outs[3].at[:, spot])], sems, 2)
        key[...] = held[:, width : width + HEAD].astype(F32)
        value[...] = held[:, width + HEAD : out_at].astype(F32)
        for j in range(0, rows, HEAD):
            side = held[j : j + HEAD, side_at:].astype(F32).T
            at = slice(j, j + HEAD)
            router[:, at] = side[:experts, :]
            gains[:, at] = side[experts : experts + 8, :]
        pairs = (
            (key, outs[1].at[spot]),
            (value, outs[2].at[spot]),
            (router, outs[4].at[:, spot]),
            (gains.at[0:1], outs[5].at[:, spot]),
            (gains.at[1:2], outs[6].at[:, spot]),
        )
        copies += move_all(pairs, sems, 3)
        for copy in copies:
            copy.wait()

    return call(
        body,
        [
            ((model, width), F32),
            ((model, HEAD), F32),
            ((model, HEAD), F32),
            ((width, model), F32),
            ((experts, model), F32),
            ((1, model), F32),
            ((1, model), F32),
        ],
        [SMEM] + [HBM] * (2 + len(done)),
        [
            pltpu.VMEM((rows, wide), BF16),
            pltpu.VMEM((rows, width), F32),
            pltpu.VMEM((rows, HEAD), F32),
            pltpu.VMEM((rows, HEAD), F32),
            pltpu.VMEM((width, model // 2), F32),
            pltpu.VMEM((experts, rows), F32),
            pltpu.VMEM((8, rows), F32),
            pltpu.SemaphoreType.DMA((8,)),
        ],
        (core, zero, one, *done),
        "attn_total",
        [HBM] * 7,
        {3 + i: i for i in range(len(done))},
    )


def exchange_rows(rows, experts):
    return expert_exchange(rows.reshape(experts, -1, rows.shape[1])).reshape(-1, rows.shape[1])


def plane_exchange(value, level):
    return lax.all_to_all(
        value,
        ("pipe", "expert"),
        split_axis=0,
        concat_axis=0,
        axis_index_groups=plane_groups(level),
        tiled=True,
    )


def plane_sum(value, level, *others):
    rows, wide = value.shape
    count = len(plane_groups(level)[0])
    arrived = plane_exchange(value.reshape(count, rows // count, wide), level)
    return jnp.sum(after(arrived, *others).astype(F32), axis=0).astype(BF16)


def plane_copy(piece, level):
    rows, wide = piece.shape
    count = len(plane_groups(level)[0])
    spread = jnp.broadcast_to(piece[None], (count, rows, wide))
    return plane_exchange(spread, level).reshape(count * rows, wide)


def gather_plane(piece):
    plane = [[(y * 4 + x) * 2 + z for y in range(4) for x in range(4)] for z in range(2)]
    groups = plane + [[32 + e for e in group] for group in plane]
    return lax.all_gather(
        piece, ("pipe", "expert"), axis=0, axis_index_groups=groups, tiled=True
    )


def background_sum(value, level):
    return lax.psum_scatter(
        value,
        ("pipe", "expert"),
        scatter_dimension=0,
        axis_index_groups=plane_groups(level),
        tiled=True,
    )


def across_planes(piece):
    return piece + lax.ppermute(piece, "expert", [(e, e ^ 1) for e in range(32)])


def after(value, *others):
    return lax.optimization_barrier((value, *others))[0]


def on_device(
    tokens,
    cotangent,
    routes,
    attn_gain,
    w_query,
    key_weight,
    value_weight,
    w_out,
    moe_gain,
    w_router,
    w_gate,
    w_up,
    w_down,
):
    core = lax.axis_index("pipe")
    part = lax.axis_index("tensor")
    first = core == 0
    experts = w_router.shape[2]
    count, model = tokens.shape[1], tokens.shape[2]
    lanes = 2 * routes.shape[3] * count // experts // 2
    lane = (part ^ (lax.axis_index("expert") % 2)).astype(jnp.int32).reshape(1)
    owns = [(core == layer).astype(jnp.int32).reshape(1) for layer in range(2)]

    mine = lax.dynamic_index_in_dim(routes[0], core, 0, keepdims=False)
    give = lax.dynamic_index_in_dim(routes[0], 1 - core, 0, keepdims=False)
    got = swap(give, "pipe")
    picks = [jnp.where(first, mine, got).T, jnp.where(first, got, mine).T]
    half = w_gate.shape[3]
    width = w_out.shape[1]
    mine_w = (w_query[0], key_weight[0], value_weight[0], w_out[0])
    attn_weights = [v for w in mine_w for v in (w, swap(w, "pipe"))]
    small = jnp.concatenate([w_router[0].T, attn_gain, moe_gain], axis=0)
    small_r = swap(small, "pipe")
    smalls = jnp.where(first, small, small_r), jnp.where(first, small_r, small)
    routers = [v[:experts] for v in smalls]
    attn_gains = [v[experts : experts + 1].astype(F32) for v in smalls]
    moe_gains = [v[experts + 1 :].astype(F32) for v in smalls]

    def over(value, layer):
        return lax.ppermute(value, "pipe", [(1 - layer, layer)])

    def across(value, layer):
        pairs = [(2 * layer, 2 * layer + 1), (2 * layer + 1, 2 * layer)]
        return lax.ppermute(value, ("pipe", "tensor"), pairs)

    def by_layer(zero, one):
        own, other = jnp.where(first, zero, one), jnp.where(first, one, zero)
        got = swap(other, "pipe")
        return got, jnp.where(first, jnp.stack([own, got]), jnp.stack([got, own]))

    cosine, sine = rotary_tables(count)
    x_0 = lax.dynamic_index_in_dim(tokens, core, 0, keepdims=False)
    top = lax.dynamic_index_in_dim(cotangent, core, 0, keepdims=False)
    near = (w_gate[0, 0], w_up[0, 0], w_down[0, 0])
    far_0 = [across(near[0], 0)]

    table_0, table_1, top_rows = slot_tables(lane, picks, top, experts, lanes)
    x_0 = after(x_0, table_0)
    branch, *kept_0 = attend_forward(owns[0], x_0, attn_gains[0], cosine, sine, attn_weights)
    branch_r = swap(after(branch, far_0[0]), "tensor")
    far_0 += [across(after(w, branch_r), 0) for w in near[1:]]
    h_0, rows, gated_0, gates_0 = dispatch(
        table_0, picks[0], x_0, branch, branch_r, moe_gains[0], routers[0], lanes, False
    )
    rows_0 = exchange_rows(rows, experts)
    near_r = [swap(after(w, branch_r), "pipe") for w in near]
    far_0r = [over(w, 1) for w in far_0]
    rows_0 = after(rows_0, *near_r, *far_0r)
    pair = jnp.concatenate(near[:2], axis=1)
    far_1 = [across(after(pair, rows_0), 1)]
    ff_0 = (*near, *near_r, *far_0, *far_0r)
    back_0 = exchange_rows(experts_forward(owns[0], rows_0, ff_0), experts)
    share = after(mul_tn(gated_0, back_0).astype(BF16), *far_1)
    share_r = swap(share, "tensor")
    top_rows = exchange_rows(after(top_rows, share), experts)
    far_1r = [over(after(w, share_r), 0) for w in far_1]

    branch, *kept_1, x_1, y_0 = attend_forward(
        owns[1], (h_0, share, share_r), attn_gains[1], cosine, sine, attn_weights
    )
    branch_r = swap(branch, "tensor")
    far_1 += [across(after(near[2], branch_r), 1)]
    far_1r += [over(far_1[1], 0)]
    h_1, rows, gated_1, gates_1 = dispatch(
        table_1, picks[1], x_1, branch, branch_r, moe_gains[1], routers[1], lanes, True
    )
    rows_1 = exchange_rows(after(rows, top_rows), experts)
    ff_1 = (*near, *near_r, *far_1, *far_1r)
    dx, made, dgu = experts_backward(owns[1], rows_1, top_rows, ff_1)
    dx = exchange_rows(dx, experts)
    both_1, out_rows = experts_grads(owns[1], rows_1, top_rows, made, dgu, ff_1)
    dx = after(dx, both_1)
    share = collect(table_1, dx, experts)
    share_r = swap(share, "tensor")
    back_1 = exchange_rows(after(out_rows, share), experts)
    both_1r = over(after(both_1, share), 1)
    dqkv, da, grad_h, dlogits, gains = attend_backward(
        owns[1], top, h_1, x_1, (share, share_r), gates_1, (),
        routers[1], moe_gains[1], attn_gains[1], kept_1, cosine, sine, attn_weights,
    )
    da_r = swap(after(da, both_1r), "tensor")
    far_sum = both_1[1] + both_1r[1]
    gains_r = swap(gains, "tensor")
    grad_1, grad, rows = turn_over(
        grad_h, x_1, da, after(da_r, back_1, far_sum, gains_r), attn_gains[1], gated_0
    )

    grad_rows = exchange_rows(rows, experts)
    far_z = across(after(far_sum, da_r), 1)
    ff_grads_1 = (both_1, both_1r, far_z)
    keep, give = attend_grads(
        owns[1], x_1, h_1, grad_h, kept_1[2], dqkv, dlogits, gains, gains_r,
        attn_gains[1], moe_gains[1],
    )
    seen = gates_seen(back_0, after(grad, rows), table_0, experts)
    seen_r = swap(seen, "tensor")
    grad_rows = after(grad_rows, keep, seen)
    dx, made, dgu = experts_backward(owns[0], rows_0, grad_rows, ff_0)
    half_1 = keep + swap(after(give, dx), "pipe")
    level_1 = background_sum(half_1, 0)
    late = mul_tn(gated_1, after(back_1, dx)).astype(BF16)
    dx = exchange_rows(dx, experts)
    (both_0,) = experts_grads(owns[0], rows_0, grad_rows, made, dgu, ff_0)
    late_r = swap(late, "tensor")
    y_1 = h_1 + (late.astype(F32) + late_r.astype(F32))
    dx = after(dx, both_0, late_r, far_z, half_1, seen_r)
    share = mul_tn(table_0, dx).astype(BF16)
    share_r = swap(share, "tensor")
    level_1 = background_sum(after(level_1, dx), 1)
    both_0r = over(after(both_0, share), 0)
    dqkv, da, grad_h, dlogits, gains = attend_backward(
        owns[0], grad, h_0, x_0, (share, share_r), gates_0, (seen, seen_r),
        routers[0], moe_gains[0], attn_gains[0], kept_0, cosine, sine, attn_weights,
    )
    gains_r = swap(gains, "tensor")
    keep, give = attend_grads(
        owns[0], x_0, h_0, grad_h, kept_0[2], dqkv, dlogits, gains, gains_r,
        attn_gains[0], moe_gains[0],
    )

    cuts = ((0, model * 2 // 3), (model * 2 // 3, model))
    far_sum = [both_0[1, a:b] + both_0r[1, a:b] for a, b in cuts]
    half_0 = after(keep, *far_sum) + swap(give, "pipe")
    da_r = swap(after(da, half_0), "tensor")
    got_y, layer_out = by_layer(y_0, after(y_1, keep))
    level_0 = plane_sum(half_0, 0, da_r, got_y)
    piece_1 = across_planes(after(level_1, level_0))
    sum_1 = gather_plane(piece_1)
    part = plane_copy(plane_sum(level_0, 2), 2)
    far_z = [across(after(v, part), 0) for v in far_sum]
    da = da.astype(F32) + after(da_r, part).astype(F32)
    x_f = x_0.astype(F32)
    grad_0 = grad_h + norm_back(x_f, row_scale_of(x_f), attn_gains[0], da)
    got_g, input_grads = by_layer(grad_0, grad_1)
    sum_0 = after(plane_copy(part, 0), far_z[0])
    core_v = core.astype(jnp.int32).reshape(1)
    over_0 = over(after(sum_0, got_g), 0)
    sizes = (width, model, experts)
    attn_g = attn_total(core_v, 0, sum_0, sum_1, (), *sizes)
    over_1 = over(after(sum_1, far_z[1], attn_g[0]), 1)
    ff_g = ff_total(
        after(core_v, attn_g[0]), 0, (both_0, both_0r, far_z[0]), ff_grads_1, ()
    )
    over_0, over_1 = after(over_0, ff_g[0]), after(over_1, ff_g[0])
    attn_g = attn_total(core_v, 1, over_0, over_1, attn_g, *sizes)
    query_g, key_g, value_g, out_g, router_g, attn_g, moe_g = attn_g
    gate_g, up_g, down_g = ff_total(
        after(core_v, moe_g), 1, (both_0, both_0r, *far_z), ff_grads_1, ff_g
    )
    return (
        layer_out[None],
        input_grads[None],
        attn_g,
        query_g[None],
        key_g[None],
        value_g[None],
        out_g[None],
        moe_g,
        router_g.T[None],
        gate_g[None, None],
        up_g[None, None],
        down_g[None, None],
    )


def solution(mesh):
    layered = P("pipe", None, "expert", None)
    by_expert = P("pipe", "expert", None, "tensor")
    columns = P("pipe", None, "tensor")
    rows = P("pipe", "tensor", None)
    down = P("pipe", "expert", "tensor", None)
    whole = P("pipe", None)
    router = P("pipe", None, None)
    tokens = P(None, "expert", None)
    return jax.shard_map(
        on_device,
        mesh=mesh,
        in_specs=(
            tokens,
            tokens,
            layered,
            whole,
            columns,
            columns,
            columns,
            rows,
            whole,
            router,
            by_expert,
            by_expert,
            down,
        ),
        out_specs=(
            layered,
            layered,
            whole,
            columns,
            columns,
            columns,
            rows,
            whole,
            router,
            by_expert,
            by_expert,
            down,
        ),
        check_vma=False,
    )
```

```python
import jax
import jax.numpy as jnp
from jax import lax
from jax.experimental import pallas as pl
from jax.experimental.pallas import tpu as pltpu
from jax.sharding import PartitionSpec as P

HEAD = 128
NORM_EPS = 1e-06
ROPE_BASE = 10000.0
BF16 = jnp.bfloat16
F32 = jnp.float32
SWAP = [(0, 1), (1, 0)]
VMEM_LIMIT = 52 * 1024 * 1024


def swap(value, axis):
    return lax.ppermute(value, axis, SWAP)


def slot_groups(experts):
    return [[e * 2 + ((e % 2) ^ s) for e in range(experts)] for s in range(2)]


def expert_exchange(value):
    return lax.all_to_all(
        value,
        ("expert", "tensor"),
        split_axis=0,
        concat_axis=0,
        axis_index_groups=slot_groups(value.shape[0]),
        tiled=True,
    )


def plane_groups(level):
    groups = []
    if level < 2:
        for z in range(2):
            for i in range(4):
                along_y = [(y * 4 + i) * 2 + z for y in range(4)]
                along_x = [(i * 4 + x) * 2 + z for x in range(4)]
                zero, one = (along_y, along_x) if level == 0 else (along_x, along_y)
                groups += [zero, [32 + e for e in one]]
    else:
        for i in range(4):
            along_x = [(i * 4 + x) * 2 + z for x in range(4) for z in range(2)]
            along_y = [(y * 4 + i) * 2 + z for y in range(4) for z in range(2)]
            groups += [along_x, [32 + e for e in along_y]]
    return groups


def mul(left, right, dims):
    return lax.dot_general(left, right, (dims, ((), ())), preferred_element_type=F32)


def mul_nn(left, right):
    return mul(left, right, ((1,), (0,)))


def mul_nt(left, right):
    return mul(left, right, ((1,), (1,)))


def mul_tn(left, right):
    return mul(left, right, ((0,), (0,)))


VMEM = pl.BlockSpec(memory_space=pltpu.VMEM)
SMEM = pl.BlockSpec(memory_space=pltpu.SMEM)
ANY = pl.BlockSpec(memory_space=pl.ANY)
HBM = pl.BlockSpec(memory_space=pltpu.HBM)


def call(body, outs, in_specs, scratch, operands, name, spaces=None, aliases=None):
    return pl.pallas_call(
        body,
        out_shape=[jax.ShapeDtypeStruct(shape, kind) for shape, kind in outs],
        in_specs=in_specs,
        out_specs=spaces or [VMEM] * len(outs),
        scratch_shapes=scratch,
        input_output_aliases=aliases or {},
        compiler_params=pltpu.CompilerParams(vmem_limit_bytes=VMEM_LIMIT),
        cost_estimate=pl.CostEstimate(flops=1024, bytes_accessed=1024, transcendentals=0),
        name=name,
    )(*operands)


def fetch(own, mine, theirs, target, sem):
    @pl.when(own == 1)
    def _():
        pltpu.make_async_copy(mine, target, sem).start()

    @pl.when(own != 1)
    def _():
        pltpu.make_async_copy(theirs, target, sem).start()


def arrive(mine, target, sem):
    pltpu.make_async_copy(mine, target, sem).wait()


def rotary_tables(count):
    half = HEAD // 2
    frequency = ROPE_BASE ** (-(jnp.arange(half, dtype=F32) * 2.0) / HEAD)
    angles = jnp.arange(count, dtype=F32)[:, None] * frequency[None, :]
    cosine = jnp.concatenate([jnp.cos(angles), jnp.cos(angles)], axis=1)
    sine = jnp.concatenate([-jnp.sin(angles), jnp.sin(angles)], axis=1)
    return cosine, sine


def turn(vector, cosine, sine):
    return vector * cosine + pltpu.roll(vector, HEAD // 2, 1) * sine


def turn_back(grad, cosine, sine):
    return grad * cosine - pltpu.roll(grad, HEAD // 2, 1) * sine


def row_scale_of(rows):
    return lax.rsqrt(jnp.mean(rows * rows, axis=-1, keepdims=True) + NORM_EPS)


def norm_back(rows, scale, gain, grad):
    scaled = grad * gain
    return scale * scaled - rows * (scale * scale * scale) * jnp.mean(
        scaled * rows, axis=-1, keepdims=True
    )


def attention_weights(q, k):
    count = q.shape[0]
    scores = mul_nt(q, k)
    row = lax.broadcasted_iota(jnp.int32, (count, count), 0)
    column = lax.broadcasted_iota(jnp.int32, (count, count), 1)
    scores = jnp.where(row >= column, scores, -1e30)
    raised = jnp.exp(scores - jnp.max(scores, axis=-1, keepdims=True))
    return raised / jnp.sum(raised, axis=-1, keepdims=True)


def head_of(index):
    return slice(index * HEAD, (index + 1) * HEAD)


def attend_body(own, x_ref, h_ref, a_ref, b_ref, gain, cos, sin, refs, outs, scratch):
    (wq, wq_r, wk, wk_r, wv, wv_r, wo, wo_r) = refs
    (qkv_s, wo_s, sems) = scratch
    (branch, q_o, kv_o, o_o, x_o, y_o) = outs
    mine = own[0]
    width = wo.shape[0]
    heads = width // HEAD
    kv_at = width + HEAD
    moves = [
        (wq, wq_r, qkv_s.at[:, :width]),
        (wk, wk_r, qkv_s.at[:, width:kv_at]),
        (wv, wv_r, qkv_s.at[:, kv_at:]),
        (wo, wo_r, wo_s),
    ]
    for i, (a, b, target) in enumerate(moves):
        fetch(mine, a, b, target, sems.at[i])
    if h_ref is None:
        x = x_ref[...].astype(F32)
    else:
        y = h_ref[...] + (a_ref[...].astype(F32) + b_ref[...].astype(F32))
        y_o[...] = y
        x_o[...] = y.astype(BF16)
        x = y.astype(BF16).astype(F32)
    normed = (x * row_scale_of(x) * gain[...]).astype(BF16)
    cosine, sine = cos[...], sin[...]
    for i in range(3):
        arrive(moves[i][0], moves[i][2], sems.at[i])
    made = mul_nn(normed, qkv_s[...])
    k = turn(made[:, width : width + HEAD], cosine, sine).astype(BF16)
    v = made[:, width + HEAD :].astype(BF16)
    kv_o[:, :HEAD] = k
    kv_o[:, HEAD:] = v
    for i in range(heads):
        q = (turn(made[:, head_of(i)], cosine, sine) * HEAD**-0.5).astype(BF16)
        q_o[:, head_of(i)] = q
        weights = attention_weights(q, k)
        o_o[:, head_of(i)] = mul_nn(weights.astype(BF16), v).astype(BF16)
    arrive(wo, wo_s, sems.at[3])
    branch[...] = mul_nn(o_o[...], wo_s[...]).astype(BF16)


def attend_forward(own, source, gain, cosine, sine, weights):
    later = isinstance(source, tuple)
    count = cosine.shape[0]
    width, model = weights[6].shape

    def body(own_ref, *refs):
        if later:
            h_ref, a_ref, b_ref, gain_ref, cos, sin = refs[:6]
            x_ref, rest = None, refs[6:]
        else:
            x_ref, gain_ref, cos, sin = refs[:4]
            h_ref, a_ref, b_ref, rest = None, None, None, refs[4:]
        ws, rest = rest[:8], rest[8:]
        outs, scratch = (rest[:6], rest[6:]) if later else (rest[:4] + (None, None), rest[4:])
        attend_body(
            own_ref, x_ref, h_ref, a_ref, b_ref, gain_ref, cos, sin, ws, outs, scratch
        )

    outs = [
        ((count, model), BF16),
        ((count, width), BF16),
        ((count, 2 * HEAD), BF16),
        ((count, width), BF16),
    ]
    if later:
        outs += [((count, model), BF16), ((count, model), F32)]
    values = source if later else (source,)
    return call(
        body,
        outs,
        [SMEM] + [VMEM] * (len(values) + 3) + [ANY] * 8,
        [
            pltpu.VMEM((model, width + 2 * HEAD), BF16),
            pltpu.VMEM((width, model), BF16),
            pltpu.SemaphoreType.DMA((4,)),
        ],
        (own, *values, gain, cosine, sine, *weights),
        "attend_forward",
    )


def hot_of(routes_ref, experts):
    count = routes_ref.shape[1]
    names = lax.broadcasted_iota(jnp.int32, (experts, count), 0)
    hot = routes_ref[0:1, :] == names
    for pick in range(1, routes_ref.shape[0]):
        hot = hot | (routes_ref[pick : pick + 1, :] == names)
    return hot


def slot_tables(lane, routes, top, experts, lanes):
    count, model = top.shape
    slots = experts * lanes

    def body(lane_ref, first_ref, second_ref, top_ref, first_o, second_o, rows_o):
        row = lax.broadcasted_iota(jnp.int32, (count, count), 0)
        column = lax.broadcasted_iota(jnp.int32, (count, count), 1)
        before = jnp.where(row < column, 1.0, 0.0).astype(BF16)
        place = lax.broadcasted_iota(jnp.int32, (lanes, count), 0).astype(F32)
        start = (lane_ref[0] * lanes).astype(F32)
        for routes_ref, out in ((first_ref, first_o), (second_ref, second_o)):
            hot = hot_of(routes_ref, experts)
            rank = mul_nn(jnp.where(hot, 1.0, 0.0).astype(BF16), before)
            rank = jnp.where(hot, rank, -1.0) - start
            for e in range(experts):
                chosen = jnp.where(rank[e : e + 1, :] == place, 1.0, 0.0)
                out[e * lanes : (e + 1) * lanes, :] = chosen.astype(BF16)
        rows_o[...] = mul_nn(second_o[...], top_ref[...].astype(BF16)).astype(BF16)

    return call(
        body,
        [((slots, count), BF16), ((slots, count), BF16), ((slots, model), BF16)],
        [SMEM] + [VMEM] * 3,
        [],
        (lane, *routes, top),
        "slot_tables",
    )


def pair_columns(value, count):
    high = value.astype(BF16).astype(F32)
    lanes = lax.broadcasted_iota(jnp.int32, (count, HEAD), 1)
    both = jnp.where(lanes == 0, high, jnp.where(lanes == 1, value - high, 0.0))
    return both.astype(BF16)


def dispatch(table, routes, x, own, received, gain, router, lanes, with_gates):
    count, model = x.shape
    experts = router.shape[0]
    slots = experts * lanes
    wide = model + HEAD if with_gates else model

    def body(table_ref, routes_ref, x_ref, a_ref, b_ref, gain_ref, router_ref, *outs):
        h_o, rows_o, gated_o, gates_o = outs
        h = x_ref[...].astype(F32) + (a_ref[...].astype(F32) + b_ref[...].astype(F32))
        h_o[...] = h
        normed = (h * row_scale_of(h) * gain_ref[...]).astype(BF16)
        rows_o[:, :model] = mul_nn(table_ref[...], normed).astype(BF16)
        hot = hot_of(routes_ref, experts)
        logits = jnp.where(hot, mul_nt(router_ref[...], normed), -1e30)
        raised = jnp.where(hot, jnp.exp(logits - jnp.max(logits, axis=0, keepdims=True)), 0.0)
        gates = raised / jnp.sum(raised, axis=0, keepdims=True)
        gates_o[...] = gates
        for e in range(experts):
            spot = slice(e * lanes, (e + 1) * lanes)
            gated = table_ref[spot, :].astype(F32) * gates[e : e + 1, :]
            gated_o[spot, :] = gated.astype(BF16)
            if with_gates:
                total = jnp.sum(gated, axis=1, keepdims=True)
                rows_o[spot, model:] = pair_columns(total, lanes)

    return call(
        body,
        [
            ((count, model), F32),
            ((slots, wide), BF16),
            ((slots, count), BF16),
            ((experts, count), F32),
        ],
        [VMEM] * 7,
        [],
        (table, routes, x, own, received, gain, router),
        "dispatch",
    )


def collect(table, back, experts):
    slots, count = table.shape
    lanes = slots // experts
    model = back.shape[1] - HEAD

    def body(table_ref, back_ref, share_o, seen_s):
        share_o[:, :model] = mul_tn(table_ref[...], back_ref[:, :model]).astype(BF16)
        value = back_ref[:, model:].astype(F32)
        value = value[:, 0:1] + value[:, 1:2]
        seen_s[...] = jnp.zeros_like(seen_s)
        for e in range(experts):
            spot = slice(e * lanes, (e + 1) * lanes)
            part = table_ref[spot, :].astype(F32) * value[spot, :]
            seen_s[e : e + 1, :] = jnp.sum(part, axis=0, keepdims=True)
        seen = seen_s[:experts, :]
        high = seen.astype(BF16).astype(F32)
        seen_s[experts : 2 * experts, :] = seen - high
        seen_s[:experts, :] = high
        share_o[:, model:] = seen_s[...].T.astype(BF16)

    return call(
        body,
        [((count, model + HEAD), BF16)],
        [VMEM] * 2,
        [pltpu.VMEM((HEAD, count), F32)],
        (table, back),
        "collect",
    )[0]


def turn_over(grad, x, own, received, gain, gated):
    slots, count = gated.shape
    model = x.shape[1]

    def body(g_ref, x_ref, a_ref, b_ref, gain_ref, gated_ref, grad_o, low_o, rows_o):
        x_v = x_ref[...].astype(F32)
        da = a_ref[...].astype(F32) + b_ref[...].astype(F32)
        total = g_ref[...] + norm_back(x_v, row_scale_of(x_v), gain_ref[...], da)
        grad_o[...] = total
        low = total.astype(BF16)
        low_o[...] = low
        rows_o[...] = mul_nn(gated_ref[...], low).astype(BF16)

    return call(
        body,
        [((count, model), F32), ((count, model), BF16), ((slots, model), BF16)],
        [VMEM] * 6,
        [],
        (grad, x, own, received, gain, gated),
        "turn_over",
    )


def gates_seen(back, low, table, experts):
    slots, count = table.shape
    lanes = slots // experts

    def body(back_ref, low_ref, table_ref, seen_o):
        seen = mul_nt(back_ref[...], low_ref[...]) * table_ref[...].astype(F32)
        for e in range(experts):
            spot = slice(e * lanes, (e + 1) * lanes)
            seen_o[e : e + 1, :] = jnp.sum(seen[spot, :], axis=0, keepdims=True)

    return call(
        body, [((experts, count), F32)], [VMEM] * 3, [], (back, low, table), "gates_seen"
    )[0]


def expert_sources(refs, half):
    if len(refs) == 12:
        return refs
    far, far_r = refs[6], refs[8]
    columns = (slice(0, half), slice(half, 2 * half))
    return (
        *refs[:6],
        *[far.at[:, spot] for spot in columns],
        refs[7],
        *[far_r.at[:, spot] for spot in columns],
        refs[9],
    )


def expert_moves(sources, wgu, wd, half):
    hidden = 2 * half
    targets = (wgu.at[:, :half], wgu.at[:, hidden : hidden + half], wd.at[:half, :])
    targets += (wgu.at[:, half:hidden], wgu.at[:, hidden + half :], wd.at[half:, :])
    return [(sources[i], sources[i + 3], t) for i, t in zip((0, 1, 2, 6, 7, 8), targets)]


def experts_forward(own, rows, weights):
    slots, model = rows.shape
    half = weights[0].shape[1]
    hidden = 2 * half
    tile = 256

    def body(own_ref, x_ref, *refs):
        sources, (y_o, x_s, wgu, wd, h_s, sems) = refs[:12], refs[12:]
        moves = expert_moves(sources, wgu, wd, half)
        arrival = pltpu.make_async_copy(x_ref, x_s, sems.at[6])
        arrival.start()
        for i in (0, 1, 3, 4, 2, 5):
            fetch(own_ref[0], moves[i][0], moves[i][1], moves[i][2], sems.at[i])
        arrival.wait()
        for i in (0, 1):
            arrive(moves[i][0], moves[i][2], sems.at[i])

        def step(c, carry):
            @pl.when(c == 1)
            def _():
                for i in (3, 4):
                    arrive(moves[i][0], moves[i][2], sems.at[i])

            at = pl.multiple_of(c * tile, tile)
            gate = mul_nn(x_s[...], wgu[:, pl.ds(at, tile)])
            up = mul_nn(x_s[...], wgu[:, pl.ds(at + hidden, tile)])
            act = gate / (1.0 + jnp.exp(-gate))
            h_s[:, pl.ds(at, tile)] = (act * up).astype(BF16)
            return carry

        lax.fori_loop(0, hidden // tile, step, 0)
        for i in (2, 5):
            arrive(moves[i][0], moves[i][2], sems.at[i])

        def finish(c, carry):
            spot = pl.ds(pl.multiple_of(c * tile, tile), tile)
            y_o[:, spot] = mul_nn(h_s[...], wd[:, spot]).astype(BF16)
            return carry

        lax.fori_loop(0, model // tile, finish, 0)

    return call(
        body,
        [((slots, model), BF16)],
        [SMEM] + [ANY] * 13,
        [
            pltpu.VMEM((slots, model), BF16),
            pltpu.VMEM((model, 2 * hidden), BF16),
            pltpu.VMEM((hidden, model), BF16),
            pltpu.VMEM((slots, hidden), BF16),
            pltpu.SemaphoreType.DMA((7,)),
        ],
        (own, rows, *weights),
        "experts_forward",
    )[0]


def experts_backward(own, rows, grads, weights):
    slots, wide = rows.shape
    model, half = weights[0].shape
    hidden = 2 * half
    gated = wide > model
    tile = 256

    def body(own_ref, x_ref, g_ref, *refs):
        sources, refs = expert_sources(refs[: len(weights)], half), refs[len(weights) :]
        dx_o, h_o, dgu_o, x_s, g_s, h_s, dgu_s, wgu, wd, sems = refs[:10]
        moves = expert_moves(sources, wgu, wd, half)
        arrivals = [
            pltpu.make_async_copy(x_ref, x_s, sems.at[6]),
            pltpu.make_async_copy(g_ref, g_s, sems.at[7]),
        ]
        leaving = [
            pltpu.make_async_copy(h_s, h_o, sems.at[8]),
            pltpu.make_async_copy(dgu_s, dgu_o, sems.at[9]),
        ]
        arrivals[0].start()
        for i in (0, 1, 2, 3, 4, 5):
            fetch(own_ref[0], moves[i][0], moves[i][1], moves[i][2], sems.at[i])
            if i == 1:
                arrivals[1].start()
        arrivals[0].wait()
        if gated:
            scale = x_s[:, model:].astype(F32)
            scale = scale[:, 0:1] + scale[:, 1:2]
            seen_s = refs[10]
            seen_s[...] = jnp.zeros_like(seen_s)
        for i in (0, 1):
            arrive(moves[i][0], moves[i][2], sems.at[i])
        arrivals[1].wait()
        arrive(moves[2][0], moves[2][2], sems.at[2])

        def step(c, carry):
            @pl.when(c == 1)
            def _():
                for i in (3, 4, 5):
                    arrive(moves[i][0], moves[i][2], sems.at[i])

            at = pl.multiple_of(c * tile, tile)
            spot, later = pl.ds(at, tile), pl.ds(at + hidden, tile)
            gate = mul_nn(x_s[:, :model], wgu[:, spot])
            up = mul_nn(x_s[:, :model], wgu[:, later])
            sig = 1.0 / (1.0 + jnp.exp(-gate))
            act = gate * sig
            made = act * up
            h_s[:, spot] = made.astype(BF16)
            grad_hidden = mul_nt(g_s[...], wd[spot, :])
            if gated:
                seen = made * grad_hidden
                seen_s[...] += seen[:, :HEAD] + seen[:, HEAD:]
                grad_hidden = grad_hidden * scale
            dgu_s[:, spot] = (grad_hidden * up * sig * (1.0 + gate * (1.0 - sig))).astype(BF16)
            dgu_s[:, later] = (grad_hidden * act).astype(BF16)
            return carry

        lax.fori_loop(0, hidden // tile, step, 0)
        for copy in leaving:
            copy.start()

        def finish(c, carry):
            spot = pl.ds(pl.multiple_of(c * tile, tile), tile)
            dx_o[:, spot] = mul_nt(dgu_s[...], wgu[spot, :]).astype(BF16)
            return carry

        lax.fori_loop(0, model // tile, finish, 0)
        if gated:
            total = jnp.sum(seen_s[...], axis=1, keepdims=True)
            dx_o[:, model:] = pair_columns(total, slots)
        for copy in leaving:
            copy.wait()

    return call(
        body,
        [((slots, wide), BF16), ((slots, hidden), BF16), ((slots, 2 * hidden), BF16)],
        [SMEM] + [ANY] * (2 + len(weights)),
        [
            pltpu.VMEM((slots, wide), BF16),
            pltpu.VMEM((slots, model), BF16),
            pltpu.VMEM((slots, hidden), BF16),
            pltpu.VMEM((slots, 2 * hidden), BF16),
            pltpu.VMEM((model, 2 * hidden), BF16),
            pltpu.VMEM((hidden, model), BF16),
            pltpu.SemaphoreType.DMA((10,)),
        ]
        + ([pltpu.VMEM((slots, HEAD), F32)] if gated else []),
        (own, rows, grads, *weights),
        "experts_backward",
        [VMEM, ANY, ANY],
    )


def experts_grads(own, rows, grads, hidden_rows, dgu, weights):
    slots, wide = rows.shape
    model, half = weights[0].shape
    hidden = 2 * half
    blocks = model // half
    gated = wide > model
    tile = 256

    def body(own_ref, x_in, g_in, h_in, dgu_in, *refs):
        sources, refs = refs[:4], refs[4:]
        both_o, refs = refs[0], refs[1:]
        x_ref, g_ref, h_ref, dgu_ref, load = refs[-5:]
        refs = refs[:-5]
        loads = [
            pltpu.make_async_copy(a, b, load.at[i])
            for i, (a, b) in enumerate(
                ((x_in, x_ref), (dgu_in, dgu_ref), (g_in, g_ref), (h_in, h_ref))
            )
        ]
        for copy in loads:
            copy.start()
        if gated:
            y_o, xt_s, dy_s, wd, sems = refs
            moves = [
                (sources[0], sources[1], wd.at[:half, :]),
                (sources[2], sources[3], wd.at[half:, :]),
            ]
            for i, (a, b, target) in enumerate(moves):
                fetch(own_ref[0], a, b, target, sems.at[i])
            loads[0].wait()
            scale = x_ref[:, model:].astype(F32)
            scale = scale[:, 0:1] + scale[:, 1:2]
        else:
            (xt_s,), dy_s = refs, g_ref
            loads[0].wait()
        for i in range(model // tile):
            xt_s[i * tile : (i + 1) * tile, :] = x_ref[:, i * tile : (i + 1) * tile].T
        for copy in loads[1:]:
            copy.wait()
        if gated:
            dy_s[...] = (g_ref[...].astype(F32) * scale).astype(BF16)
            for i, (a, b, target) in enumerate(moves):
                arrive(a, target, sems.at[i])

        def step(c, carry):
            spot = pl.ds(pl.multiple_of(c * tile, tile), tile)
            made = mul_nn(xt_s[spot, :], dgu_ref[...]).astype(BF16)
            both_o[0, spot, :half] = made[:, :half]
            both_o[1, spot, :half] = made[:, half:hidden]
            both_o[0, spot, half:hidden] = made[:, hidden : hidden + half]
            both_o[1, spot, half:hidden] = made[:, hidden + half :]
            if gated:
                y_o[:, spot] = mul_nn(h_ref[...], wd[:, spot]).astype(BF16)
            return carry

        lax.fori_loop(0, model // tile, step, 0)
        down = tile // 2
        for i in range(hidden // down):
            made = mul_tn(h_ref[:, i * down : (i + 1) * down], dy_s[...]).astype(BF16)
            low = i * down
            side, low = (0, low) if low < half else (1, low - half)
            for j in range(blocks):
                at = j * half + low
                both_o[side, at : at + down, hidden:] = made[:, j * half : (j + 1) * half]

    outs = [((2, model, 3 * half), BF16)]
    scratch = [pltpu.VMEM((model, slots), BF16)]
    if gated:
        outs = outs + [((slots, model), BF16)]
        scratch += [
            pltpu.VMEM((slots, model), BF16),
            pltpu.VMEM((hidden, model), BF16),
            pltpu.SemaphoreType.DMA((2,)),
        ]
    scratch += [
        pltpu.VMEM((slots, wide), BF16),
        pltpu.VMEM((slots, model), BF16),
        pltpu.VMEM((slots, hidden), BF16),
        pltpu.VMEM((slots, 2 * hidden), BF16),
        pltpu.SemaphoreType.DMA((4,)),
    ]
    return call(
        body,
        outs,
        [SMEM] + [ANY] * 8,
        scratch,
        (own, rows, grads, hidden_rows, dgu, *[weights[i] for i in (2, 5, -(len(weights) // 6) - 2, -1)]),
        "experts_grads",
    )


def attend_backward(
    own, grad, h, x, shares, gates, seen, router, moe_gain, attn_gain, kept, cosine, sine, weights
):
    count, model = h.shape
    width = weights[6].shape[0]
    heads = width // HEAD
    experts = router.shape[0]
    kv_at, out_at = width + HEAD, width + 2 * HEAD
    riding = len(seen) == 0

    def body(own_ref, *refs):
        (g_ref, h_ref, x_ref, a_ref, b_ref, gates_ref) = refs[:6]
        refs = refs[6:]
        if riding:
            tail = a_ref[:, model:].astype(F32) + b_ref[:, model:].astype(F32)
            tail = tail.T
            grad_gates = tail[:experts, :] + tail[experts : 2 * experts, :]
        else:
            grad_gates = refs[0][...] + refs[1][...]
            refs = refs[2:]
        (router_ref, mgain_ref, again_ref, q_ref, kv_ref, cos, sin) = refs[:7]
        (wq, wq_r, wk, wk_r, wv, wv_r, wo, wo_r) = refs[7:15]
        (dqkv_o, da_o, gh_o, dlogits_o, gains_o) = refs[15:20]
        (qkv_s, wo_s, sems) = refs[20:]
        mine = own_ref[0]
        moves = [
            (wo, wo_r, wo_s),
            (wq, wq_r, qkv_s.at[:, :width]),
            (wk, wk_r, qkv_s.at[:, width:kv_at]),
            (wv, wv_r, qkv_s.at[:, kv_at:]),
        ]
        for i, (a, b, target) in enumerate(moves):
            fetch(mine, a, b, target, sems.at[i])
        gates_v = gates_ref[...]
        dlogits = gates_v * (grad_gates - jnp.sum(gates_v * grad_gates, axis=0, keepdims=True))
        dlogits = dlogits.astype(BF16)
        dlogits_o[...] = dlogits
        dn = a_ref[:, :model].astype(F32) + b_ref[:, :model].astype(F32)
        dn = dn + mul_tn(dlogits, router_ref[...])
        hv = h_ref[...]
        scale = row_scale_of(hv)
        gh = g_ref[...].astype(F32) + norm_back(hv, scale, mgain_ref[...], dn)
        gh_o[...] = gh
        moe_part = jnp.sum(dn * hv * scale, axis=0, keepdims=True)
        dz = gh.astype(BF16)
        arrive(wo, wo_s, sems.at[0])
        do = mul_nt(dz, wo_s[...]).astype(BF16)
        cosine_v, sine_v = cos[...], sin[...]
        k, v = kv_ref[:, :HEAD], kv_ref[:, HEAD:]
        dk, dv = 0.0, 0.0
        for i in range(heads):
            q = q_ref[:, head_of(i)]
            p = attention_weights(q, k)
            do_i = do[:, head_of(i)]
            dp = mul_nt(do_i, v)
            ds = (p * (dp - jnp.sum(p * dp, axis=-1, keepdims=True))).astype(BF16)
            dv = dv + mul_tn(p.astype(BF16), do_i)
            dk = dk + mul_tn(ds, q)
            dq = turn_back(mul_nn(ds, k), cosine_v, sine_v) * HEAD**-0.5
            dqkv_o[:, head_of(i)] = dq.astype(BF16)
        dqkv_o[:, width:kv_at] = turn_back(dk, cosine_v, sine_v).astype(BF16)
        dqkv_o[:, kv_at:] = dv.astype(BF16)
        for i in range(1, 4):
            arrive(moves[i][0], moves[i][2], sems.at[i])
        da = mul_nt(dqkv_o[...], qkv_s[...])
        da_o[...] = da.astype(BF16)
        xv = x_ref[...].astype(F32)
        attn_part = jnp.sum(da * xv * row_scale_of(xv), axis=0, keepdims=True)
        lane = lax.broadcasted_iota(jnp.int32, (16, model), 0)
        total = jnp.zeros((16, model), F32)
        for i, value in enumerate((attn_part, moe_part)):
            high = value.astype(BF16).astype(F32)
            total = jnp.where(lane == 2 * i, high, total)
            total = jnp.where(lane == 2 * i + 1, value - high, total)
        gains_o[...] = total.astype(BF16)

    q, kv, _ = kept
    operands = (own, grad, h, x, *shares, gates, *seen, router, moe_gain, attn_gain)
    operands += (q, kv, cosine, sine)
    return call(
        body,
        [
            ((count, out_at), BF16),
            ((count, model), BF16),
            ((count, model), F32),
            ((experts, count), BF16),
            ((16, model), BF16),
        ],
        [SMEM] + [VMEM] * (len(operands) - 1) + [ANY] * 8,
        [
            pltpu.VMEM((model, out_at), BF16),
            pltpu.VMEM((width, model), BF16),
            pltpu.SemaphoreType.DMA((4,)),
        ],
        (*operands, *weights),
        "attend_backward",
    )


def attend_grads(own, x, h, grad_h, o, dqkv, dlogits, gains, gains_r, attn_gain, moe_gain):
    count, model = h.shape
    width, out_at = o.shape[1], dqkv.shape[1]
    experts = dlogits.shape[0]
    side_at = out_at + model // 2
    tile = 256
    parts = model // tile // 2

    def body(own_ref, x_ref, h_ref, gh_ref, o_ref, dqkv_ref, dl_ref, *rest):
        gains_ref, far_ref, again, mgain, *rest = rest
        keep_o, give_o, left_s, pack_s, sems = rest
        xv = x_ref[...].astype(F32)
        normed = (xv * row_scale_of(xv) * again[...]).astype(BF16)
        for i in range(model // tile):
            left_s[i * tile : (i + 1) * tile, :] = normed[:, i * tile : (i + 1) * tile].T
        hv = h_ref[...]
        normed_m = (hv * row_scale_of(hv) * mgain[...]).astype(BF16)
        dz = gh_ref[...].astype(BF16)
        row = lax.broadcasted_iota(jnp.int32, (experts, HEAD), 0)
        column = lax.broadcasted_iota(jnp.int32, (experts, HEAD), 1)
        spread_logits = mul_tn(dl_ref[...], jnp.where(row == column, 1.0, 0.0).astype(BF16))
        spread_logits = spread_logits.astype(BF16)
        row = lax.broadcasted_iota(jnp.int32, (16, HEAD), 0)
        column = lax.broadcasted_iota(jnp.int32, (16, HEAD), 1)
        hit = (column == experts + row // 2) & (row < 4)
        marks = jnp.where(hit, 1.0, 0.0).astype(BF16)
        far_marks = jnp.where(hit & (row < 2), 1.0, 0.0).astype(BF16)

        def step(c, carry):
            spot = pl.ds(pl.multiple_of(c * tile, tile), tile)
            target = pl.ds(pl.multiple_of(lax.rem(c, parts) * tile, tile), tile)
            made = mul_nn(left_s[spot, :], dqkv_ref[...]).astype(BF16)
            pack_s[lax.div(c, parts), target, :out_at] = made
            return carry

        lax.fori_loop(0, model // tile, step, 0)
        for i in range(width // HEAD):
            made = mul_tn(o_ref[:, head_of(i)], dz).astype(BF16)
            spot = slice(i * HEAD, (i + 1) * HEAD)
            pack_s[0, spot, out_at:side_at] = made[:, : model // 2]
            pack_s[1, spot, out_at:side_at] = made[:, model // 2 :]
        for i in range(model // tile):
            spot = slice(i * tile, (i + 1) * tile)
            total = mul_tn(normed_m[:, spot], spread_logits)
            total = total + mul_tn(gains_ref[:, spot], marks)
            total = total + mul_tn(far_ref[:, spot], far_marks)
            at = (i % parts) * tile
            pack_s[i // parts, at : at + tile, side_at:] = total.astype(BF16)
        kept = 1 - own_ref[0]
        copies = [
            pltpu.make_async_copy(pack_s.at[kept], keep_o, sems.at[0]),
            pltpu.make_async_copy(pack_s.at[1 - kept], give_o, sems.at[1]),
        ]
        for copy in copies:
            copy.start()
        for copy in copies:
            copy.wait()

    return call(
        body,
        [((model // 2, side_at + HEAD), BF16)] * 2,
        [SMEM] + [VMEM] * 10,
        [
            pltpu.VMEM((model, count), BF16),
            pltpu.VMEM((2, model // 2, side_at + HEAD), BF16),
            pltpu.SemaphoreType.DMA((2,)),
        ],
        (own, x, h, grad_h, o, dqkv, dlogits, gains, gains_r, attn_gain, moe_gain),
        "attend_grads",
        [ANY, ANY],
    )


def move_all(pairs, sems, first):
    copies = [pltpu.make_async_copy(a, b, sems.at[first + i]) for i, (a, b) in enumerate(pairs)]
    for copy in copies:
        copy.start()
    return copies


def ff_total(core, which, zero, one, done):
    _, model, wide = zero[0].shape
    half = wide // 3
    rows = model // 2
    low = which * rows
    pieces = rows // half

    given = len(zero) + len(one)

    def body(core_ref, *refs):
        ins = (refs[: len(zero)], refs[len(zero) : given])
        outs = refs[given + len(done) : given + len(done) + 3]
        held, gate_s, up_s, down_s, sems = refs[given + len(done) + 3 :]
        spot = slice(low, low + rows)
        for number in range(2):
            near, near_r = ins[number][:2]
            pairs = [(near.at[0, spot], held.at[0]), (near_r.at[0, spot], held.at[1])]
            start = 0
            for z in ins[number][2:]:
                stop = start + z.shape[0]
                a, b = max(start, low), min(stop, low + rows)
                if a < b:
                    pairs.append((z.at[a - start : b - start], held.at[2, a - low : b - low]))
                start = stop

            @pl.when(core_ref[0] == number)
            def _(pairs=pairs):
                for copy in move_all(pairs, sems, 0):
                    copy.wait()

        def total(at, columns):
            return (
                held[0, at, columns].astype(F32)
                + held[1, at, columns].astype(F32)
                + held[2, at, columns].astype(F32)
            )

        gate_s[...] = total(slice(0, rows), slice(0, half))
        up_s[...] = total(slice(0, rows), slice(half, 2 * half))
        for i in range(pieces):
            at = slice(i * half, (i + 1) * half)
            down_s[:, at] = total(at, slice(2 * half, wide))
        pairs = (
            (gate_s, outs[0].at[spot]),
            (up_s, outs[1].at[spot]),
            (down_s, outs[2].at[:, spot]),
        )
        for copy in move_all(pairs, sems, 4):
            copy.wait()

    return call(
        body,
        [((model, half), F32), ((model, half), F32), ((half, model), F32)],
        [SMEM] + [HBM] * (given + len(done)),
        [
            pltpu.VMEM((3, rows, wide), BF16),
            pltpu.VMEM((rows, half), F32),
            pltpu.VMEM((rows, half), F32),
            pltpu.VMEM((half, rows), F32),
            pltpu.SemaphoreType.DMA((7,)),
        ],
        (core, *zero, *one, *done),
        "ff_total",
        [HBM] * 3,
        {1 + given + i: i for i in range(len(done))},
    )


def attn_total(core, which, zero, one, done, width, model, experts):
    rows, wide = zero.shape
    out_at = width + 2 * HEAD
    side_at = out_at + model // 2
    mixed = which == 0

    def body(core_ref, zero_ref, one_ref, *refs):
        outs = refs[len(done) : len(done) + 7]
        held, query, key, value, out, router, gains, sems = refs[len(done) + 7 :]
        piece = rows // 16

        @pl.when(core_ref[0] == 1)
        def _():
            if mixed:
                for y in range(4):
                    for x in range(4):
                        source = one_ref.at[(y * 4 + x) * piece : (y * 4 + x + 1) * piece]
                        target = held.at[(x * 4 + y) * piece : (x * 4 + y + 1) * piece]
                        pltpu.make_async_copy(source, target, sems.at[0]).start()
            else:
                pltpu.make_async_copy(one_ref, held, sems.at[0]).start()

        @pl.when(core_ref[0] != 1)
        def _():
            pltpu.make_async_copy(zero_ref, held, sems.at[0]).start()

        pltpu.make_async_copy(zero_ref, held, sems.at[0]).wait()
        spot = slice(which * rows, (which + 1) * rows)
        query[...] = held[:, :width].astype(F32)
        copies = move_all([(query, outs[0].at[spot])], sems, 1)
        out[...] = held[:, out_at:side_at].astype(F32)
        copies += move_all([(out, outs[3].at[:, spot])], sems, 2)
        key[...] = held[:, width : width + HEAD].astype(F32)
        value[...] = held[:, width + HEAD : out_at].astype(F32)
        for j in range(0, rows, HEAD):
            side = held[j : j + HEAD, side_at:].astype(F32).T
            at = slice(j, j + HEAD)
            router[:, at] = side[:experts, :]
            gains[:, at] = side[experts : experts + 8, :]
        pairs = (
            (key, outs[1].at[spot]),
            (value, outs[2].at[spot]),
            (router, outs[4].at[:, spot]),
            (gains.at[0:1], outs[5].at[:, spot]),
            (gains.at[1:2], outs[6].at[:, spot]),
        )
        copies += move_all(pairs, sems, 3)
        for copy in copies:
            copy.wait()

    return call(
        body,
        [
            ((model, width), F32),
            ((model, HEAD), F32),
            ((model, HEAD), F32),
            ((width, model), F32),
            ((experts, model), F32),
            ((1, model), F32),
            ((1, model), F32),
        ],
        [SMEM] + [HBM] * (2 + len(done)),
        [
            pltpu.VMEM((rows, wide), BF16),
            pltpu.VMEM((rows, width), F32),
            pltpu.VMEM((rows, HEAD), F32),
            pltpu.VMEM((rows, HEAD), F32),
            pltpu.VMEM((width, model // 2), F32),
            pltpu.VMEM((experts, rows), F32),
            pltpu.VMEM((8, rows), F32),
            pltpu.SemaphoreType.DMA((8,)),
        ],
        (core, zero, one, *done),
        "attn_total",
        [HBM] * 7,
        {3 + i: i for i in range(len(done))},
    )


def exchange_rows(rows, experts):
    return expert_exchange(rows.reshape(experts, -1, rows.shape[1])).reshape(-1, rows.shape[1])


def plane_exchange(value, level):
    return lax.all_to_all(
        value,
        ("pipe", "expert"),
        split_axis=0,
        concat_axis=0,
        axis_index_groups=plane_groups(level),
        tiled=True,
    )


def plane_sum(value, level, *others):
    rows, wide = value.shape
    count = len(plane_groups(level)[0])
    arrived = plane_exchange(value.reshape(count, rows // count, wide), level)
    return jnp.sum(after(arrived, *others).astype(F32), axis=0).astype(BF16)


def plane_copy(piece, level):
    rows, wide = piece.shape
    count = len(plane_groups(level)[0])
    spread = jnp.broadcast_to(piece[None], (count, rows, wide))
    return plane_exchange(spread, level).reshape(count * rows, wide)


def gather_plane(piece):
    plane = [[(y * 4 + x) * 2 + z for y in range(4) for x in range(4)] for z in range(2)]
    groups = plane + [[32 + e for e in group] for group in plane]
    return lax.all_gather(
        piece, ("pipe", "expert"), axis=0, axis_index_groups=groups, tiled=True
    )


def background_sum(value, level):
    return lax.psum_scatter(
        value,
        ("pipe", "expert"),
        scatter_dimension=0,
        axis_index_groups=plane_groups(level),
        tiled=True,
    )


def across_planes(piece):
    return piece + lax.ppermute(piece, "expert", [(e, e ^ 1) for e in range(32)])


def after(value, *others):
    return lax.optimization_barrier((value, *others))[0]


def on_device(
    tokens,
    cotangent,
    routes,
    attn_gain,
    w_query,
    key_weight,
    value_weight,
    w_out,
    moe_gain,
    w_router,
    w_gate,
    w_up,
    w_down,
):
    core = lax.axis_index("pipe")
    part = lax.axis_index("tensor")
    first = core == 0
    experts = w_router.shape[2]
    count, model = tokens.shape[1], tokens.shape[2]
    lanes = 2 * routes.shape[3] * count // experts // 2
    lane = (part ^ (lax.axis_index("expert") % 2)).astype(jnp.int32).reshape(1)
    owns = [(core == layer).astype(jnp.int32).reshape(1) for layer in range(2)]

    mine = lax.dynamic_index_in_dim(routes[0], core, 0, keepdims=False)
    give = lax.dynamic_index_in_dim(routes[0], 1 - core, 0, keepdims=False)
    got = swap(give, "pipe")
    picks = [jnp.where(first, mine, got).T, jnp.where(first, got, mine).T]
    half = w_gate.shape[3]
    width = w_out.shape[1]
    mine_w = (w_query[0], key_weight[0], value_weight[0], w_out[0])
    attn_weights = [v for w in mine_w for v in (w, swap(w, "pipe"))]
    small = jnp.concatenate([w_router[0].T, attn_gain, moe_gain], axis=0)
    small_r = swap(small, "pipe")
    smalls = jnp.where(first, small, small_r), jnp.where(first, small_r, small)
    routers = [v[:experts] for v in smalls]
    attn_gains = [v[experts : experts + 1].astype(F32) for v in smalls]
    moe_gains = [v[experts + 1 :].astype(F32) for v in smalls]

    def over(value, layer):
        return lax.ppermute(value, "pipe", [(1 - layer, layer)])

    def across(value, layer):
        pairs = [(2 * layer, 2 * layer + 1), (2 * layer + 1, 2 * layer)]
        return lax.ppermute(value, ("pipe", "tensor"), pairs)

    def by_layer(zero, one):
        own, other = jnp.where(first, zero, one), jnp.where(first, one, zero)
        got = swap(other, "pipe")
        return got, jnp.where(first, jnp.stack([own, got]), jnp.stack([got, own]))

    cosine, sine = rotary_tables(count)
    x_0 = lax.dynamic_index_in_dim(tokens, core, 0, keepdims=False)
    top = lax.dynamic_index_in_dim(cotangent, core, 0, keepdims=False)
    near = (w_gate[0, 0], w_up[0, 0], w_down[0, 0])
    far_0 = [across(near[0], 0)]

    table_0, table_1, top_rows = slot_tables(lane, picks, top, experts, lanes)
    x_0 = after(x_0, table_0)
    branch, *kept_0 = attend_forward(owns[0], x_0, attn_gains[0], cosine, sine, attn_weights)
    branch_r = swap(after(branch, far_0[0]), "tensor")
    far_0 += [across(after(w, branch_r), 0) for w in near[1:]]
    h_0, rows, gated_0, gates_0 = dispatch(
        table_0, picks[0], x_0, branch, branch_r, moe_gains[0], routers[0], lanes, False
    )
    rows_0 = exchange_rows(rows, experts)
    near_r = [swap(after(w, branch_r), "pipe") for w in near]
    far_0r = [over(w, 1) for w in far_0]
    rows_0 = after(rows_0, *near_r, *far_0r)
    pair = jnp.concatenate(near[:2], axis=1)
    far_1 = [across(after(pair, rows_0), 1)]
    ff_0 = (*near, *near_r, *far_0, *far_0r)
    back_0 = exchange_rows(experts_forward(owns[0], rows_0, ff_0), experts)
    share = after(mul_tn(gated_0, back_0).astype(BF16), *far_1)
    share_r = swap(share, "tensor")
    top_rows = exchange_rows(after(top_rows, share), experts)
    far_1r = [over(after(w, share_r), 0) for w in far_1]

    branch, *kept_1, x_1, y_0 = attend_forward(
        owns[1], (h_0, share, share_r), attn_gains[1], cosine, sine, attn_weights
    )
    branch_r = swap(branch, "tensor")
    far_1 += [across(after(near[2], branch_r), 1)]
    far_1r += [over(far_1[1], 0)]
    h_1, rows, gated_1, gates_1 = dispatch(
        table_1, picks[1], x_1, branch, branch_r, moe_gains[1], routers[1], lanes, True
    )
    rows_1 = exchange_rows(after(rows, top_rows), experts)
    ff_1 = (*near, *near_r, *far_1, *far_1r)
    dx, made, dgu = experts_backward(owns[1], rows_1, top_rows, ff_1)
    dx = exchange_rows(dx, experts)
    both_1, out_rows = experts_grads(owns[1], rows_1, top_rows, made, dgu, ff_1)
    dx = after(dx, both_1)
    share = collect(table_1, dx, experts)
    share_r = swap(share, "tensor")
    back_1 = exchange_rows(after(out_rows, share), experts)
    both_1r = over(after(both_1, share), 1)
    dqkv, da, grad_h, dlogits, gains = attend_backward(
        owns[1], top, h_1, x_1, (share, share_r), gates_1, (),
        routers[1], moe_gains[1], attn_gains[1], kept_1, cosine, sine, attn_weights,
    )
    da_r = swap(after(da, both_1r), "tensor")
    far_sum = both_1[1] + both_1r[1]
    gains_r = swap(gains, "tensor")
    grad_1, grad, rows = turn_over(
        grad_h, x_1, da, after(da_r, back_1, far_sum, gains_r), attn_gains[1], gated_0
    )

    grad_rows = exchange_rows(rows, experts)
    far_z = across(after(far_sum, da_r), 1)
    ff_grads_1 = (both_1, both_1r, far_z)
    keep, give = attend_grads(
        owns[1], x_1, h_1, grad_h, kept_1[2], dqkv, dlogits, gains, gains_r,
        attn_gains[1], moe_gains[1],
    )
    seen = gates_seen(back_0, after(grad, rows), table_0, experts)
    seen_r = swap(seen, "tensor")
    grad_rows = after(grad_rows, keep, seen)
    dx, made, dgu = experts_backward(owns[0], rows_0, grad_rows, ff_0)
    half_1 = keep + swap(after(give, dx), "pipe")
    level_1 = background_sum(half_1, 0)
    late = mul_tn(gated_1, after(back_1, dx)).astype(BF16)
    dx = exchange_rows(dx, experts)
    (both_0,) = experts_grads(owns[0], rows_0, grad_rows, made, dgu, ff_0)
    late_r = swap(late, "tensor")
    y_1 = h_1 + (late.astype(F32) + late_r.astype(F32))
    dx = after(dx, both_0, late_r, far_z, half_1, seen_r)
    share = mul_tn(table_0, dx).astype(BF16)
    share_r = swap(share, "tensor")
    level_1 = background_sum(after(level_1, dx), 1)
    both_0r = over(after(both_0, share), 0)
    dqkv, da, grad_h, dlogits, gains = attend_backward(
        owns[0], grad, h_0, x_0, (share, share_r), gates_0, (seen, seen_r),
        routers[0], moe_gains[0], attn_gains[0], kept_0, cosine, sine, attn_weights,
    )
    gains_r = swap(gains, "tensor")
    keep, give = attend_grads(
        owns[0], x_0, h_0, grad_h, kept_0[2], dqkv, dlogits, gains, gains_r,
        attn_gains[0], moe_gains[0],
    )

    cuts = ((0, model * 5 // 6), (model * 5 // 6, model))
    far_sum = [both_0[1, a:b] + both_0r[1, a:b] for a, b in cuts]
    half_0 = after(keep, *far_sum) + swap(give, "pipe")
    da_r = swap(after(da, half_0), "tensor")
    got_y, layer_out = by_layer(y_0, after(y_1, keep))
    level_0 = plane_sum(half_0, 0, da_r, got_y)
    piece_1 = across_planes(after(level_1, level_0))
    sum_1 = gather_plane(piece_1)
    part = plane_copy(plane_sum(level_0, 2), 2)
    far_z = [across(after(v, part), 0) for v in far_sum]
    da = da.astype(F32) + after(da_r, part).astype(F32)
    x_f = x_0.astype(F32)
    grad_0 = grad_h + norm_back(x_f, row_scale_of(x_f), attn_gains[0], da)
    got_g, input_grads = by_layer(grad_0, grad_1)
    sum_0 = plane_copy(part, 0)
    core_v = core.astype(jnp.int32).reshape(1)
    over_0 = over(after(sum_0, got_g), 0)
    sizes = (width, model, experts)
    attn_g = attn_total(core_v, 0, sum_0, sum_1, (), *sizes)
    over_1 = over(after(sum_1, far_z[0], attn_g[0]), 1)
    ff_g = ff_total(
        after(core_v, attn_g[0]), 0, (both_0, both_0r, far_z[0]), ff_grads_1, ()
    )
    over_0, over_1 = after(over_0, ff_g[0]), after(over_1, ff_g[0])
    attn_g = attn_total(core_v, 1, over_0, over_1, attn_g, *sizes)
    query_g, key_g, value_g, out_g, router_g, attn_g, moe_g = attn_g
    gate_g, up_g, down_g = ff_total(
        after(core_v, moe_g), 1, (both_0, both_0r, *far_z), ff_grads_1, ff_g
    )
    return (
        layer_out[None],
        input_grads[None],
        attn_g,
        query_g[None],
        key_g[None],
        value_g[None],
        out_g[None],
        moe_g,
        router_g.T[None],
        gate_g[None, None],
        up_g[None, None],
        down_g[None, None],
    )


def solution(mesh):
    layered = P("pipe", None, "expert", None)
    by_expert = P("pipe", "expert", None, "tensor")
    columns = P("pipe", None, "tensor")
    rows = P("pipe", "tensor", None)
    down = P("pipe", "expert", "tensor", None)
    whole = P("pipe", None)
    router = P("pipe", None, None)
    tokens = P(None, "expert", None)
    return jax.shard_map(
        on_device,
        mesh=mesh,
        in_specs=(
            tokens,
            tokens,
            layered,
            whole,
            columns,
            columns,
            columns,
            rows,
            whole,
            router,
            by_expert,
            by_expert,
            down,
        ),
        out_specs=(
            layered,
            layered,
            whole,
            columns,
            columns,
            columns,
            rows,
            whole,
            router,
            by_expert,
            by_expert,
            down,
        ),
        check_vma=False,
    )
```
